128 devices in a mesh: dp: 16 (over y_lo, x, core), tensor: 8 (over z, y_hi).
Axes of the slice: x: 4, y: 4 (y_hi: 2, y_lo: 2; y = y_hi * 2 + y_lo), z: 4, core: 2. Of those that a mesh axis runs over, the one named last changes fastest.
Arguments:
- inputs: bfloat16 [12288, 2048], P('dp'), may hold values from -6 to 6
- segments: int32 [16, 768], P('dp'), may hold values from 0 to 2, never falling along the last dimension, each value on 1 to 384 neighbouring positions
- attn_gain: float32 [2048], replicated, may hold values from 0.1 to 1.9
- w_query: bfloat16 [2048, 2048], P(None, 'tensor'), may hold values from -0.125 to 0.125
- w_key: bfloat16 [2048, 2048], P(None, 'tensor'), may hold values from -0.125 to 0.125
- w_value: bfloat16 [2048, 4096], P(None, 'tensor'), may hold values from -0.125 to 0.125
- w_gate: bfloat16 [2048, 4096], P(None, 'tensor'), may hold values from -0.125 to 0.125
- w_beta: bfloat16 [2048, 16], P(None, 'tensor'), may hold values from -0.125 to 0.125
- w_alpha: bfloat16 [2048, 16], P(None, 'tensor'), may hold values from -0.125 to 0.125
- conv_query: float32 [4, 2048], P(None, 'tensor'), may hold values from -3 to 3
- conv_key: float32 [4, 2048], P(None, 'tensor'), may hold values from -3 to 3
- conv_value: float32 [4, 4096], P(None, 'tensor'), may hold values from -3 to 3
- decay_log: float32 [16], P('tensor'), may hold values from -6.5 to -2.5
- decay_bias: float32 [16], P('tensor'), may hold values from -1 to 1
- head_gain: float32 [256], replicated, may hold values from 0.1 to 1.9
- w_out: bfloat16 [4096, 2048], P('tensor'), may hold values from -0.09375 to 0.09375
- ffn_gain: float32 [2048], replicated, may hold values from 0.1 to 1.9
- w_up_gate: bfloat16 [2048, 5632], P(None, 'tensor'), may hold values from -0.125 to 0.125
- w_up: bfloat16 [2048, 5632], P(None, 'tensor'), may hold values from -0.125 to 0.125
- w_down: bfloat16 [5632, 2048], P('tensor'), may hold values from -0.078125 to 0.078125
- out_grad: bfloat16 [12288, 2048], P('dp'), may hold values from -6 to 6
Outputs:
- outputs: bfloat16 [12288, 2048], P('dp')
- input_grad: bfloat16 [12288, 2048], P('dp')
- grad_attn_gain: float32 [2048], replicated
- grad_query: float32 [2048, 2048], P('dp', 'tensor')
- grad_key: float32 [2048, 2048], P('dp', 'tensor')
- grad_value: float32 [2048, 4096], P('dp', 'tensor')
- grad_gate: float32 [2048, 4096], P('dp', 'tensor')
- grad_beta: float32 [2048, 16], P('dp', 'tensor')
- grad_alpha: float32 [2048, 16], P('dp', 'tensor')
- grad_conv_query: float32 [4, 2048], P(None, 'tensor')
- grad_conv_key: float32 [4, 2048], P(None, 'tensor')
- grad_conv_value: float32 [4, 4096], P(None, 'tensor')
- grad_decay_log: float32 [16], P('tensor')
- grad_decay_bias: float32 [16], P('tensor')
- grad_head_gain: float32 [256], replicated
- grad_out: float32 [4096, 2048], P('tensor', 'dp')
- grad_ffn_gain: float32 [2048], replicated
- grad_up_gate: float32 [2048, 5632], P('dp', 'tensor')
- grad_up: float32 [2048, 5632], P('dp', 'tensor')
- grad_down: float32 [5632, 2048], P('tensor', 'dp')
The draws below stay inside these ranges and needn't reach their ends.
Inputs may be any that keep to these rules, and one draw needn't show every extreme that they name: `segments`: within each sequence document numbers never fall, every number 0 to 2 is used, and the longest document has exactly half of 768 tokens.
All inputs are finite; a program needn't handle non-finite values.
Results may differ from the reference program's by a relative error of at most 0.015.
Values sent between devices are 32-bit elements; how exact they have to be, the bound alone decides.
A program may use at most 256 MiB of HBM per device.

```python
import math
import jax
import jax.numpy as jnp
import numpy as np
from jax import lax

D = 2048
H = 16
K = 128
V = 256
FF = 5632
CONV = 4
BLOCK = 64
LEN = 768
DOCS = 3
SEQUENCES = 16
TOKENS = 12288


def strengthened(values, rng, source, target, parts, factor):
    owner, partner = [(jnp.arange(values.shape[position]) // (values.shape[position] // parts)).reshape([-1 if axis == position else 1 for axis in range(values.ndim)]) for position in (source, target)]
    chosen = jax.random.permutation(rng, parts)[partner]
    strong = (owner == chosen) | (owner == (partner + parts // 2) % parts)
    return jnp.where(strong, factor * values, values)


def block_levels(own_key, dims, cuts, low, high):
    gain = 1.0
    for position, shards_of in cuts:
        steps = jax.random.uniform(jax.random.fold_in(jax.random.fold_in(own_key, 6), position), (shards_of,), jnp.float32, low / len(cuts), high / len(cuts))
        gain = gain * jnp.repeat(jnp.exp(steps), dims[position] // shards_of).reshape((-1,) + (1,) * (len(dims) - 1 - position))
    return gain


def profile(count, total, bound, lean):
    portions = [(1 << 20) // math.isqrt(standing ** lean) + 1 for standing in range(2, count + 1)]
    spare, counts = total - bound - (count - 1), [1] * (count - 1)
    while spare > 0:
        movable = [i for i in range(count - 1) if counts[i] < bound]
        mass, left = sum([portions[i] for i in movable]), spare
        for i in movable:
            extra = min(bound - counts[i], max(1, left * portions[i] // mass), spare)
            counts[i] = counts[i] + extra
            spare = spare - extra
    return np.array([bound] + counts)


def ragged_sizes(stream_key, number_of, total, bound, slope):
    if number_of == 2:
        one = jax.random.randint(stream_key, (), max(1, total - bound), min(bound, total - 1) + 1)
        return jnp.stack([one, total - one])
    lengths = jnp.asarray(profile(number_of, total, bound, slope), jnp.int32)
    twos = (number_of - 1) // 2
    donor, taker = lengths[1:1 + 2 * twos:2], lengths[2:2 + 2 * twos:2]
    room = jnp.minimum(donor - 1, bound - taker)
    moved = jax.random.randint(jax.random.fold_in(stream_key, 1), (twos,), 0, 1 << 20) % (room + 1)
    lengths = lengths.at[1:1 + 2 * twos:2].set(donor - moved).at[2:2 + 2 * twos:2].set(taker + moved)
    return lengths[jax.random.permutation(jax.random.fold_in(stream_key, 2), number_of)]


def normal_values(own_key, shape, deviation, most, cuts=(), kind=jnp.bfloat16):
    entries = jax.random.normal(own_key, shape, jnp.float32) * deviation
    if len(cuts) > 0:
        entries = block_levels(own_key, shape, cuts, -0.22, 0.18) * entries
    return jnp.clip(entries, min=-most, max=most).astype(kind)


def bell_draw_with(own_key, shape, scale, reach, cuts, heavy, held_as=jnp.bfloat16):
    result = scale * jax.random.normal(own_key, shape, jnp.float32)
    if cuts:
        result = result * block_levels(own_key, shape, cuts, -0.22, 0.18)
    return jnp.clip(strengthened(result, jax.random.fold_in(own_key, 3), *heavy), -reach, reach).astype(held_as)


def setup_inputs(seed: int = 0) -> dict:
    arg_keys = jax.random.split(jax.random.key(seed), 22)
    return {
        "inputs": normal_values(arg_keys[0], (TOKENS, D), 1.0, 6.0, ((0, 16),)),
        "segments": jax.vmap(lambda own: jnp.searchsorted(jnp.cumsum(ragged_sizes(own, DOCS, LEN, LEN // 2, 0)), jnp.arange(LEN), side="right"))(jax.random.split(arg_keys[1], SEQUENCES)).reshape((SEQUENCES, LEN)).astype(jnp.int32),
        "attn_gain": jnp.clip(1.0 + 0.18 * jax.random.normal(arg_keys[2], (D,), jnp.float32), 0.1, 1.9),
        "w_query": normal_values(arg_keys[3], (D, H * K), D ** -0.5, 0.125, ((1, 8),)),
        "w_key": normal_values(arg_keys[4], (D, H * K), D ** -0.5, 0.125, ((1, 8),)),
        "w_value": normal_values(arg_keys[5], (D, H * V), D ** -0.5, 0.125, ((1, 8),)),
        "w_gate": normal_values(arg_keys[6], (D, H * V), D ** -0.5, 0.125, ((1, 8),)),
        "w_beta": normal_values(arg_keys[7], (D, H), D ** -0.5, 0.125, ((1, 8),)),
        "w_alpha": normal_values(arg_keys[8], (D, H), D ** -0.5, 0.125, ((1, 8),)),
        "conv_query": normal_values(arg_keys[9], (CONV, H * K), CONV ** -0.5, 3.0, ((1, 8),), jnp.float32),
        "conv_key": normal_values(arg_keys[10], (CONV, H * K), CONV ** -0.5, 3.0, ((1, 8),), jnp.float32),
        "conv_value": normal_values(arg_keys[11], (CONV, H * V), CONV ** -0.5, 3.0, ((1, 8),), jnp.float32),
        "decay_log": jnp.clip(-6.5 + 4.0 * jax.random.uniform(arg_keys[12], (H,), jnp.float32) ** block_levels(arg_keys[12], (H,), ((0, 8),), -0.2, 0.2), -6.5, -2.5),
        "decay_bias": jnp.clip(jax.random.uniform(arg_keys[13], (H,), jnp.float32, -1.0, 1.0) * block_levels(arg_keys[13], (H,), ((0, 8),), -0.4, 0.0), -1.0, 1.0),
        "head_gain": jnp.clip(1.0 + 0.18 * jax.random.normal(arg_keys[14], (V,), jnp.float32), 0.1, 1.9),
        "w_out": normal_values(arg_keys[15], (H * V, D), (H * V) ** -0.5, 0.09375, ((0, 8),)),
        "ffn_gain": jnp.clip(1.0 + 0.18 * jax.random.normal(arg_keys[16], (D,), jnp.float32), 0.1, 1.9),
        "w_up_gate": normal_values(arg_keys[17], (D, FF), D ** -0.5, 0.125, ((1, 8),)),
        "w_up": normal_values(arg_keys[18], (D, FF), D ** -0.5, 0.125, ((1, 8),)),
        "w_down": normal_values(arg_keys[19], (FF, D), FF ** -0.5, 0.078125, ((0, 8),)),
        "out_grad": bell_draw_with(arg_keys[20], (TOKENS, D), 1.0, 6.0, ((0, 16),), (0, 1, 16, 2.0)),
    }


@jax.custom_vjp
def low(v):
    return lax.optimization_barrier(v.astype(jnp.bfloat16)).astype(jnp.float32)

@jax.custom_vjp
def low_back(v):
    return v

def low_keep(v):
    return (low(v), None)

def low_pass(kept, grad):
    return (grad,)

def back_keep(v):
    return (v, None)

def back_low(kept, grad):
    return (low(grad),)
low.defvjp(low_keep, low_pass)
low_back.defvjp(back_keep, back_low)

def mean_norm(values):
    return values * lax.rsqrt(lax.optimization_barrier(jnp.mean(values * values, axis=-1, keepdims=True)) + 1e-05)

def short_conv(signal, taps, seg_table):
    seq_count, length = seg_table.shape
    shaped = signal.reshape(seq_count, length, signal.shape[-1])
    total = shaped * taps[0]
    for offset in range(1, taps.shape[0]):
        moved = jnp.pad(shaped, ((0, 0), (offset, 0), (0, 0)))[:, :length]
        seg_moved = jnp.pad(seg_table, ((0, 0), (offset, 0)), constant_values=-1)[:, :length]
        same_doc = (seg_moved == seg_table).astype(jnp.float32)[:, :, None]
        total = total + moved * same_doc * taps[offset]
    return total.reshape(signal.shape)

def block_step(memory_state, pieces):
    query_rows, key, value_rows, beta, log_decay, seg_rows, prev_seg = pieces
    highest_precision = lax.Precision.HIGHEST
    span = seg_rows.shape[-1]
    row_index = lax.broadcasted_iota(jnp.int32, (span, span), 0)
    col_index = lax.broadcasted_iota(jnp.int32, (span, span), 1)
    cumul = jnp.cumsum(log_decay, axis=-1)
    keep = (seg_rows[:, :, None] == seg_rows[:, None, :]) & (row_index >= col_index)[None]
    spread = cumul[:, :, None] - cumul[:, None, :]
    decay = jnp.where(keep, jnp.exp(jnp.where(keep, spread, 0.0)), 0.0)
    carried_state = jnp.where(seg_rows == prev_seg[:, None], jnp.exp(cumul), 0.0)
    key_key = jnp.einsum('nik,njk->nij', key, key, precision=highest_precision)
    strict = jnp.where((row_index > col_index)[None], decay, 0.0) * key_key * beta[:, None, :]
    ident_mat = (row_index == col_index).astype(strict.dtype)[None]
    target_value = value_rows - carried_state[:, :, None] * jnp.einsum('fmc,fcq->fmq', key, memory_state, precision=highest_precision)
    delta_update = jax.scipy.linalg.solve_triangular(ident_mat + strict, target_value, lower=True, unit_diagonal=True)
    query_key = jnp.einsum('nik,njk->nij', query_rows, key, precision=highest_precision)
    within = decay * query_key * beta[:, None, :]
    result_value = carried_state[:, :, None] * jnp.einsum('fmc,fcq->fmq', query_rows, memory_state, precision=highest_precision)
    result_value = result_value + jnp.einsum('nij,njv->niv', within, delta_update, precision=highest_precision)
    final_tap_weight = decay[:, -1, :] * beta
    updated_state = carried_state[:, -1][:, None, None] * memory_state
    updated_state = updated_state + jnp.einsum('ite,itr->ier', key * final_tap_weight[:, :, None], delta_update, precision=highest_precision)
    return (updated_state, result_value)

def delta_rule(query_rows, key, value_rows, beta, log_decay, seg_table, span):
    seq_count, length, heads, key_size = query_rows.shape
    blocks = length // span

    def arrange(tensor):
        moved = jnp.transpose(tensor, (0, 2, 1, 3)).reshape(seq_count * heads, blocks, span, tensor.shape[-1])
        return jnp.transpose(moved, (1, 0, 2, 3))

    def arrange_flat(tensor):
        moved = jnp.transpose(tensor, (0, 2, 1)).reshape(seq_count * heads, blocks, span)
        return jnp.transpose(moved, (1, 0, 2))
    seg_rows = jnp.broadcast_to(seg_table[:, None, :], (seq_count, heads, length))
    seg_blocks = jnp.transpose(seg_rows.reshape(seq_count * heads, blocks, span), (1, 0, 2))
    prev_seg = jnp.concatenate([seg_blocks[:1, :, 0], seg_blocks[:-1, :, -1]], axis=0)
    memory_state = jnp.zeros((seq_count * heads, key_size, value_rows.shape[-1]), jnp.float32)
    final_state, results = lax.scan(jax.checkpoint(block_step), memory_state, (arrange(query_rows), arrange(key), arrange(value_rows), arrange_flat(beta), arrange_flat(log_decay), seg_blocks, prev_seg))
    results = jnp.transpose(results, (1, 0, 2, 3)).reshape(seq_count, heads, length, value_rows.shape[-1])
    return jnp.transpose(results, (0, 2, 1, 3))

def mixer(query_pre, key_pre, value_pre, gate_in, beta_pre, alpha_pre, conv_q, conv_k, conv_v, rate_log, rate_bias, gain_heads, seg_table):
    seq_count, length = seg_table.shape
    heads = rate_log.shape[0]
    key_size = query_pre.shape[-1] // heads
    value_size = value_pre.shape[-1] // heads
    query_rows = jax.nn.silu(short_conv(query_pre, conv_q, seg_table)).reshape(seq_count, length, heads, key_size)
    query_rows = query_rows * lax.rsqrt(lax.optimization_barrier(jnp.sum(query_rows * query_rows, axis=-1, keepdims=True)) + 1e-06) * key_size ** (-0.5)
    key = jax.nn.silu(short_conv(key_pre, conv_k, seg_table)).reshape(seq_count, length, heads, key_size)
    key = key * lax.rsqrt(lax.optimization_barrier(jnp.sum(key * key, axis=-1, keepdims=True)) + 1e-06)
    value_rows = jax.nn.silu(short_conv(value_pre, conv_v, seg_table)).reshape(seq_count, length, heads, value_size)
    beta = jax.nn.sigmoid(beta_pre).reshape(seq_count, length, heads)
    log_decay = (-jnp.exp(rate_log) * jax.nn.softplus(alpha_pre + rate_bias)).reshape(seq_count, length, heads)
    mixed = delta_rule(query_rows, key, value_rows, beta, log_decay, seg_table, BLOCK)
    gate = jax.nn.silu(gate_in).reshape(seq_count, length, heads, value_size)
    normed = mean_norm(mixed) * gain_heads * gate
    return normed.reshape(seq_count * length, heads * value_size)

def forward(param_set, tokens_val, seg_table):
    attn_gain, w_query, w_key, w_value, w_gate, w_beta, w_alpha, conv_query, conv_key, conv_value, decay_log, decay_bias, head_gain, w_out, ffn_gain, w_up_gate, w_up, w_down = param_set
    highest_precision = lax.Precision.HIGHEST

    def matmul(left, right):
        return jnp.dot(left, right, precision=highest_precision)
    hidden_in = low(mean_norm(tokens_val) * attn_gain)
    query_pre = low_back(matmul(hidden_in, w_query))
    key_pre = low_back(matmul(hidden_in, w_key))
    value_pre = low_back(matmul(hidden_in, w_value))
    gate_pre = low_back(matmul(hidden_in, w_gate))
    beta_pre = low_back(matmul(hidden_in, w_beta))
    alpha_pre = low_back(matmul(hidden_in, w_alpha))
    mixed = mixer(query_pre, key_pre, value_pre, gate_pre, beta_pre, alpha_pre, conv_query, conv_key, conv_value, decay_log, decay_bias, head_gain, seg_table)
    mixed_low = low(mixed)
    resid_mid = tokens_val + low_back(matmul(mixed_low, w_out))
    hidden_mid = low(mean_norm(resid_mid) * ffn_gain)
    ffn_gate_pre = low_back(matmul(hidden_mid, w_up_gate))
    up_pre = low_back(matmul(hidden_mid, w_up))
    inner = low(jax.nn.silu(ffn_gate_pre) * up_pre)
    return resid_mid + low_back(matmul(inner, w_down))

def reference(inputs, segments, attn_gain, w_query, w_key, w_value, w_gate, w_beta, w_alpha, conv_query, conv_key, conv_value, decay_log, decay_bias, head_gain, w_out, ffn_gain, w_up_gate, w_up, w_down, out_grad):
    params = tuple((weight.astype(jnp.float32) for weight in (attn_gain, w_query, w_key, w_value, w_gate, w_beta, w_alpha, conv_query, conv_key, conv_value, decay_log, decay_bias, head_gain, w_out, ffn_gain, w_up_gate, w_up, w_down)))
    tokens_all = inputs.astype(jnp.float32).reshape(SEQUENCES, LEN, D)
    cotan_all = out_grad.astype(jnp.float32).reshape(SEQUENCES, LEN, D)

    def one_sequence(totals, pieces):
        tokens_seq, segment_row, cotangent = pieces

        def forward_fn(param_set, tokens_val):
            return forward(param_set, tokens_val, segment_row[None, :])
        result_value, backward_fn = jax.vjp(forward_fn, params, tokens_seq)
        param_grads, token_grads = backward_fn(cotangent)
        return (jax.tree.map(jnp.add, totals, param_grads), (result_value, token_grads))
    zero_grads = tuple((jnp.zeros_like(weight) for weight in params))
    totals, (results, token_grads) = lax.scan(one_sequence, zero_grads, (tokens_all, segments, cotan_all))
    outputs = results.reshape(TOKENS, D).astype(jnp.bfloat16)
    input_grad = token_grads.reshape(TOKENS, D).astype(jnp.bfloat16)
    return (outputs, input_grad, totals[0], totals[1], totals[2], totals[3], totals[4], totals[5], totals[6], totals[7], totals[8], totals[9], totals[10], totals[11], totals[12], totals[13], totals[14], totals[15], totals[16], totals[17])
```

```python
import functools
import jax, jax.numpy as jnp
from jax import lax
from jax.experimental import pallas as pl
from jax.experimental.pallas import tpu as pltpu
from jax.sharding import PartitionSpec as P

F32 = jnp.float32
BF16 = jnp.bfloat16
L = 128
PAD = 8
NN = (((1,), (0,)), ((), ()))
NT = (((1,), (1,)), ((), ()))
TN = (((0,), (0,)), ((), ()))


def split(x):
    hi = x.astype(BF16)
    return hi, (x - hi.astype(F32)).astype(BF16)


def mm1(a, b, dims):
    return lax.dot_general(a, b, dims, preferred_element_type=F32)


def mm3(a, b, dims=NN):
    return mm1(a[0], b[0], dims) + (mm1(a[0], b[1], dims) + mm1(a[1], b[0], dims))


def sigmoid(x):
    return 1.0 / (1.0 + jnp.exp(-x))


def rows(ref, b, n=L, lead=0):
    return ref[pl.ds(pl.multiple_of(b * L, L) + lead, n)]


def decay_tile(ba, rate, bias):
    lane = lax.broadcasted_iota(jnp.int32, ba.shape, 1)
    shifted = ba + bias
    soft = jnp.maximum(shifted, 0.0) + jnp.log1p(jnp.exp(-jnp.abs(shifted)))
    return jnp.where(lane < 2, sigmoid(ba), rate * soft)


def tri_sum(tile, dims):
    r = lax.broadcasted_iota(jnp.int32, (L, L), 0)
    c = lax.broadcasted_iota(jnp.int32, (L, L), 1)
    tri = (r >= c).astype(BF16)
    p0 = tile.astype(BF16)
    rest = tile - p0.astype(F32)
    p1 = rest.astype(BF16)
    p2 = (rest - p1.astype(F32)).astype(BF16)
    return mm1(tri, p0, dims) + (mm1(tri, p1, dims) + mm1(tri, p2, dims))


def block_decay(b, seg_ref, ba_ref, rate, bias):
    tile = decay_tile(rows(ba_ref, b), rate, bias)
    cum = tri_sum(tile, NN)
    lane = lax.broadcasted_iota(jnp.int32, (L, L), 1)
    both = jnp.where(lane < 2, tile, cum)
    flat = both.T
    seg_row = seg_ref[b, 0:1, :]
    seg_col = jnp.broadcast_to(seg_row, (L, L)).T
    prev = seg_ref[b, 1:2, 0:1]
    r = lax.broadcasted_iota(jnp.int32, (L, L), 0)
    keep = (seg_col == seg_row) & (r >= lane)
    strict_keep = r > lane
    carry_keep = seg_col[:, 0:1] == prev
    out = []
    for h in range(2):
        c_col = cum[:, 2 + h:3 + h]
        c_row = flat[2 + h:3 + h, :]
        beta_row = flat[h:h + 1, :]
        decay = jnp.where(keep, jnp.exp(jnp.where(keep, c_col - c_row, 0.0)), 0.0)
        carry = jnp.where(carry_keep, jnp.exp(c_col), 0.0)
        last_keep = seg_col[:, 0:1] == seg_row[:, L - 1:L]
        last_decay = jnp.where(last_keep, jnp.exp(jnp.where(last_keep, c_col[L - 1:L, :] - c_col, 0.0)), 0.0)
        beta_col = tile[:, h:h + 1]
        out.append((decay, carry, beta_row, beta_col, last_decay))
    return out, strict_keep, (tile, seg_col)


def conv_block(b, pre_ref, taps_ref, seg_ref, cols, segpad_ref):
    base = pl.multiple_of(b * L, L)
    z = pre_ref[pl.ds(base, L + PAD), cols]
    s = segpad_ref[pl.ds(base, L + PAD), 0:1]
    total = z[PAD:] * taps_ref[0:1, cols]
    for k in range(1, 4):
        same = (s[PAD - k:PAD - k + L] == s[PAD:]).astype(F32)
        total = total + z[PAD - k:PAD - k + L] * same * taps_ref[k:k + 1, cols]
    return total


def inverse_many(mats):
    r = lax.broadcasted_iota(jnp.int32, (L, L), 0)
    c = lax.broadcasted_iota(jnp.int32, (L, L), 1)
    eye = (r == c).astype(F32)
    xs = [eye - jnp.where((r // 2 == c // 2), a, 0.0) for a in mats]
    s = 2
    while s < L:
        pick = (r // (2 * s) == c // (2 * s)) & (r // s != c // s)
        sx = [split(x) for x in xs]
        sa = [split(jnp.where(pick, a, 0.0)) for a in mats]
        t = [mm3(x, a) for x, a in zip(sx, sa)]
        xs = [x - mm3(split(y), z) for x, y, z in zip(xs, t, sx)]
        s *= 2
    return xs


def fwd_kernel(blocks, group, seg_ref, qp_ref, kp_ref, vp_ref, gp_ref, ba_ref, cq_ref, ck_ref, cv_ref, rate_ref, bias_ref, gain_ref,
               low_ref, q_ref, k_ref, x_ref, u_ref, s_ref, o_ref,
               qpad, kpad, vpad, segpad, w_s, u0_s, kw_s):
    T = blocks * L
    rate, bias = rate_ref[0:1, :], bias_ref[0:1, :]
    for pad, src in ((qpad, qp_ref), (kpad, kp_ref), (vpad, vp_ref)):
        pad[0:PAD, :] = jnp.zeros((PAD, pad.shape[1]), F32)
        pad[PAD:PAD + T, :] = src[...]
    segpad[0:PAD, :] = jnp.full((PAD, L), -1.0, F32)
    for b in range(blocks):
        segpad[PAD + b * L:PAD + (b + 1) * L, :] = jnp.broadcast_to(seg_ref[b, 0:1, :], (L, L)).T

    def phase_a(g, _):
        a_mats, keepers = [], []
        for i in range(group):
            b = g * group + i
            base = pl.multiple_of(b * L, L)
            per_head, strict_keep, _u = block_decay(b, seg_ref, ba_ref, rate, bias)
            for h in range(2):
                decay, carry, beta_row, beta_col, last_decay = per_head[h]
                kc = slice(h * 128, h * 128 + 128)
                vc = slice(h * 256, h * 256 + 256)
                y = conv_block(b, qpad, cq_ref, seg_ref, kc, segpad)
                q = y * sigmoid(y)
                q = q * (lax.rsqrt(jnp.sum(q * q, axis=-1, keepdims=True) + 1e-06) * (128 ** -0.5))
                y = conv_block(b, kpad, ck_ref, seg_ref, kc, segpad)
                k = y * sigmoid(y)
                k = k * lax.rsqrt(jnp.sum(k * k, axis=-1, keepdims=True) + 1e-06)
                q_ref[pl.ds(base, L), kc] = q
                k_ref[pl.ds(base, L), kc] = k
                y = conv_block(b, vpad, cv_ref, seg_ref, vc, segpad)
                v = y * sigmoid(y)
                ks = split(k)
                kk = mm3(ks, ks, NT)
                a_mats.append(jnp.where(strict_keep, decay, 0.0) * kk * beta_row)
                kw_s[pl.ds(base, L), kc] = k * (last_decay * beta_col)
                keepers.append((b, base, h, kc, vc, v, k * carry))
        xs = inverse_many(a_mats)
        for x, (b, base, h, kc, vc, v, gk) in zip(xs, keepers):
            x_ref[pl.ds(base, L), kc] = x
            sx = split(x)
            u0_s[pl.ds(base, L), vc] = mm3(sx, split(v))
            w_s[pl.ds(base, L), kc] = mm3(sx, split(gk))
        return 0

    lax.fori_loop(0, blocks // group, phase_a, 0)

    def phase_b(b, state):
        base = pl.multiple_of(b * L, L)
        per_head, strict_keep, _u = block_decay(b, seg_ref, ba_ref, rate, bias)
        new = []
        for h in range(2):
            decay, carry, beta_row, beta_col, last_decay = per_head[h]
            kc = slice(h * 128, h * 128 + 128)
            vc = slice(h * 256, h * 256 + 256)
            s = state[h]
            s_ref[pl.ds(base, L), vc] = s
            ss = split(s)
            u = u0_s[pl.ds(base, L), vc] - mm3(split(w_s[pl.ds(base, L), kc]), ss)
            u_ref[pl.ds(base, L), vc] = u
            new.append(carry[L - 1:L, :] * s + mm3(split(kw_s[pl.ds(base, L), kc]), split(u), TN))
        return tuple(new)

    zero = jnp.zeros((128, 256), F32)
    lax.fori_loop(0, blocks, phase_b, (zero, zero))

    def phase_c(b, _):
        base = pl.multiple_of(b * L, L)
        per_head, strict_keep, _u = block_decay(b, seg_ref, ba_ref, rate, bias)
        for h in range(2):
            decay, carry, beta_row, beta_col, last_decay = per_head[h]
            kc = slice(h * 128, h * 128 + 128)
            vc = slice(h * 256, h * 256 + 256)
            q = q_ref[pl.ds(base, L), kc]
            qk = mm3(split(q), split(k_ref[pl.ds(base, L), kc]), NT)
            p = decay * qk * beta_row
            o = mm3(split(q * carry), split(s_ref[pl.ds(base, L), vc])) + mm3(split(p), split(u_ref[pl.ds(base, L), vc]))
            o_ref[pl.ds(base, L), vc] = o
            gp = gp_ref[pl.ds(base, L), vc]
            n = o * lax.rsqrt(jnp.mean(o * o, axis=-1, keepdims=True) + 1e-05)
            low_ref[pl.ds(base, L), vc] = (n * gain_ref[0:1, :] * (gp * sigmoid(gp))).astype(BF16)
        return 0

    lax.fori_loop(0, blocks, phase_c, 0)


VM = pl.BlockSpec(memory_space=pltpu.VMEM)


def mixer_fwd(seg3, qp, kp, vp, gp, ba, cq, ck, cv, rate, bias, gain, group=2):
    T = qp.shape[0]
    blocks = T // L
    sd = jax.ShapeDtypeStruct
    return pl.pallas_call(
        functools.partial(fwd_kernel, blocks, group),
        out_shape=(sd((T, 512), BF16), sd((T, 256), F32), sd((T, 256), F32), sd((T, 256), F32), sd((T, 512), F32),
                   sd((T, 512), F32), sd((T, 512), F32)),
        in_specs=[VM] * 12, out_specs=[VM] * 7,
        scratch_shapes=[pltpu.VMEM((T + PAD, 256), F32), pltpu.VMEM((T + PAD, 256), F32), pltpu.VMEM((T + PAD, 512), F32),
                        pltpu.VMEM((T + PAD, L), F32), pltpu.VMEM((T, 256), F32), pltpu.VMEM((T, 512), F32), pltpu.VMEM((T, 256), F32)],
        compiler_params=pltpu.CompilerParams(vmem_limit_bytes=56 * 2 ** 20),
        name="mixer_forward",
    )(seg3, qp, kp, vp, gp, ba, cq, ck, cv, rate, bias, gain)


def bwd_kernel(blocks, seg_ref, gm_ref, qp_ref, kp_ref, vp_ref, gp_ref, ba_ref, cq_ref, ck_ref, cv_ref, rate_ref, bias_ref, gain_ref,
               q_ref, k_ref, x_ref, u_ref, s_ref, o_ref,
               dqp_ref, dkp_ref, dvp_ref, dgp_ref, dba_ref, dtap_ref, dsmall_ref, dgain_ref,
               qpad, kpad, vpad, segpad, do_s, y0_s, z_s, r_s, y_s, ds_s, dq_s, dk_s, dv_s, acc_s):
    T = blocks * L
    rate, bias = rate_ref[0:1, :], bias_ref[0:1, :]
    for pad, src in ((qpad, qp_ref), (kpad, kp_ref), (vpad, vp_ref)):
        pad[0:PAD, :] = jnp.zeros((PAD, pad.shape[1]), F32)
        pad[PAD:PAD + T, :] = src[...]
    segpad[0:PAD, :] = jnp.full((PAD, L), -1.0, F32)
    segpad[PAD + T:, :] = jnp.full((PAD, L), -1.0, F32)
    for b in range(blocks):
        segpad[PAD + b * L:PAD + (b + 1) * L, :] = jnp.broadcast_to(seg_ref[b, 0:1, :], (L, L)).T
    dgain_ref[...] = jnp.zeros_like(dgain_ref)
    dsmall_ref[...] = jnp.zeros_like(dsmall_ref)
    dtap_ref[...] = jnp.zeros_like(dtap_ref)

    def phase_1(b, _):
        base = pl.multiple_of(b * L, L)
        per_head, strict_keep, _u = block_decay(b, seg_ref, ba_ref, rate, bias)
        for h in range(2):
            decay, carry, beta_row, beta_col, last_decay = per_head[h]
            kc = slice(h * 128, h * 128 + 128)
            vc = slice(h * 256, h * 256 + 256)
            o = o_ref[pl.ds(base, L), vc]
            gp = gp_ref[pl.ds(base, L), vc]
            gm = gm_ref[pl.ds(base, L), vc]
            gain = gain_ref[0:1, :]
            sg = sigmoid(gp)
            r = lax.rsqrt(jnp.mean(o * o, axis=-1, keepdims=True) + 1e-05)
            n = o * r
            act = gp * sg
            gn = gm * n
            dgain_ref[0:1, :] = dgain_ref[0:1, :] + jnp.sum(gn * act, axis=0, keepdims=True)
            dgp_ref[pl.ds(base, L), vc] = (gn * gain * (sg * (1.0 + gp * (1.0 - sg)))).astype(BF16)
            dn = gm * gain * act
            do = r * (dn - n * jnp.mean(dn * n, axis=-1, keepdims=True))
            do_s[pl.ds(base, L), vc] = do
            q, k = q_ref[pl.ds(base, L), kc], k_ref[pl.ds(base, L), kc]
            p = decay * mm3(split(q), split(k), NT) * beta_row
            sdo = split(do)
            sx = split(x_ref[pl.ds(base, L), kc])
            y0 = mm3(sx, split(mm3(split(p), sdo, TN)), TN)
            z = mm3(sx, split(k * (last_decay * beta_col)), TN)
            y0_s[pl.ds(base, L), vc] = y0
            z_s[pl.ds(base, L), kc] = z
            r_s[pl.ds(base, L), vc] = mm3(split(q * carry), sdo, TN)
        return 0

    lax.fori_loop(0, blocks, phase_1, 0)

    def phase_2(i, grads):
        b = blocks - 1 - i
        base = pl.multiple_of(b * L, L)
        per_head, strict_keep, _u = block_decay(b, seg_ref, ba_ref, rate, bias)
        new = []
        for h in range(2):
            decay, carry, beta_row, beta_col, last_decay = per_head[h]
            kc = slice(h * 128, h * 128 + 128)
            vc = slice(h * 256, h * 256 + 256)
            ds = grads[h]
            ds_s[pl.ds(base, L), vc] = ds
            y = y0_s[pl.ds(base, L), vc] + mm3(split(z_s[pl.ds(base, L), kc]), split(ds))
            y_s[pl.ds(base, L), vc] = y
            new.append(carry[L - 1:L, :] * ds + r_s[pl.ds(base, L), vc]
                       - mm3(split(k_ref[pl.ds(base, L), kc] * carry), split(y), TN))
        return tuple(new)

    zero = jnp.zeros((128, 256), F32)
    lax.fori_loop(0, blocks, phase_2, (zero, zero))

    def phase_3(b, _):
        base = pl.multiple_of(b * L, L)
        per_head, strict_keep, (tile, seg_col) = block_decay(b, seg_ref, ba_ref, rate, bias)
        lane = lax.broadcasted_iota(jnp.int32, (L, L), 1)
        rowi = lax.broadcasted_iota(jnp.int32, (L, L), 0)
        row_tile = jnp.zeros((L, L), F32)
        col_tile = jnp.zeros((L, L), F32)
        for h in range(2):
            decay, carry, beta_row, beta_col, last_decay = per_head[h]
            kc = slice(h * 128, h * 128 + 128)
            vc = slice(h * 256, h * 256 + 256)
            q, k = q_ref[pl.ds(base, L), kc], k_ref[pl.ds(base, L), kc]
            sq, sk = split(q), split(k)
            kk = mm3(sk, sk, NT)
            qk = mm3(sq, sk, NT)
            s, u = s_ref[pl.ds(base, L), vc], u_ref[pl.ds(base, L), vc]
            do, y, ds = do_s[pl.ds(base, L), vc], y_s[pl.ds(base, L), vc], ds_s[pl.ds(base, L), vc]
            ss, su, sdo, sy, sds = split(s), split(u), split(do), split(y), split(ds)
            do_st = mm3(sdo, ss, NT)
            y_st = mm3(sy, ss, NT)
            u_dst = mm3(su, sds, NT)
            dp = mm3(sdo, su, NT)
            da = -mm3(sy, su, NT)
            dcarry = jnp.sum(q * do_st - k * y_st, axis=-1, keepdims=True)
            dcarry_last = jnp.sum(jnp.sum(ds * s, axis=0, keepdims=True), axis=1, keepdims=True)
            dw = jnp.sum(u_dst * k, axis=-1, keepdims=True)
            dpd = dp * decay
            dad = jnp.where(strict_keep, da * decay, 0.0)
            dqk = dpd * beta_row
            dkk = dad * beta_row
            prod = dpd * qk + dad * kk
            dbeta_row = jnp.sum(prod, axis=0, keepdims=True)
            dec_grad = prod * beta_row
            dc_col = jnp.sum(dec_grad, axis=1, keepdims=True) + dcarry * carry
            dc_row = -jnp.sum(dec_grad, axis=0, keepdims=True)
            dlast = dw * beta_col * last_decay
            row1 = rowi[:, 0:1]
            dc_col = dc_col - dlast
            dc_col = dc_col + jnp.where(row1 == L - 1, jnp.sum(dlast, axis=0, keepdims=True) + dcarry_last * carry, 0.0)
            dbeta_col = dw * last_decay
            row_tile = row_tile + jnp.where(rowi == h, dbeta_row, 0.0) + jnp.where(rowi == 2 + h, dc_row, 0.0)
            col_tile = col_tile + jnp.where(lane == h, dbeta_col, 0.0) + jnp.where(lane == 2 + h, dc_col, 0.0)
            sdqk, sdkk = split(dqk), split(dkk + dkk.T)
            dq_s[pl.ds(base, L), kc] = carry * do_st + mm3(sdqk, sk)
            dk_s[pl.ds(base, L), kc] = (mm3(sdqk, sq, TN) + mm3(sdkk, sk) - carry * y_st
                                        + (last_decay * beta_col) * u_dst)
        grad = col_tile + row_tile.T
        dld = tri_sum(grad, TN)
        ba = rows(ba_ref, b)
        sig_alpha = sigmoid(ba + bias)
        dalpha = dld * rate * sig_alpha
        dpre = jnp.where(lane < 2, grad * tile * (1.0 - tile), jnp.where(lane < 4, dalpha, 0.0))
        dba_ref[pl.ds(base, L), :] = dpre.astype(BF16)
        dsmall_ref[0:1, :] = dsmall_ref[0:1, :] + jnp.sum(dpre, axis=0, keepdims=True)
        dsmall_ref[1:2, :] = dsmall_ref[1:2, :] + jnp.sum(dld * tile, axis=0, keepdims=True)
        return 0

    lax.fori_loop(0, blocks, phase_3, 0)

    def conv_back(pre, taps_ref, src, out_ref, cols, tap_cols, scale):
        acc_s[T:, cols] = jnp.zeros((PAD, 128), F32)

        def one(b, tap_grads):
            base = pl.multiple_of(b * L, L)
            y = conv_block(b, pre, taps_ref, None, cols, segpad)
            sg = sigmoid(y)
            act = y * sg
            d = src[pl.ds(base, L), cols]
            if scale is not None:
                r = lax.rsqrt(jnp.sum(act * act, axis=-1, keepdims=True) + 1e-06)
                d = (scale * r) * (d - act * (r * r * jnp.sum(d * act, axis=-1, keepdims=True)))
            dy = d * (sg * (1.0 + y * (1.0 - sg)))
            acc_s[pl.ds(base, L), cols] = dy
            z = pre[pl.ds(base, L + PAD), cols]
            s = segpad[pl.ds(base, L + PAD), 0:1]
            new = [tap_grads[0] + jnp.sum(dy * z[PAD:], axis=0, keepdims=True)]
            for t in range(1, 4):
                same = (s[PAD - t:PAD - t + L] == s[PAD:]).astype(F32)
                new.append(tap_grads[t] + jnp.sum(dy * (z[PAD - t:PAD - t + L] * same), axis=0, keepdims=True))
            return tuple(new)

        zero = jnp.zeros((1, 128), F32)
        res = lax.fori_loop(0, blocks, one, (zero,) * 4)
        for t in range(4):
            dtap_ref[t:t + 1, tap_cols] = res[t]

        def two(b, _):
            base = pl.multiple_of(b * L, L)
            dy = acc_s[pl.ds(base, L + PAD), cols]
            s = segpad[pl.ds(base + PAD, L + PAD), 0:1]
            total = dy[:L] * taps_ref[0:1, cols]
            for t in range(1, 4):
                same = (s[t:t + L] == s[:L]).astype(F32)
                total = total + dy[t:t + L] * same * taps_ref[t:t + 1, cols]
            out_ref[pl.ds(base, L), cols] = total.astype(BF16)
            return 0

        lax.fori_loop(0, blocks, two, 0)

    for h in range(2):
        c = slice(h * 128, h * 128 + 128)
        conv_back(qpad, cq_ref, dq_s, dqp_ref, c, slice(h * 128, h * 128 + 128), 128 ** -0.5)
        conv_back(kpad, ck_ref, dk_s, dkp_ref, c, slice(256 + h * 128, 256 + h * 128 + 128), 1.0)
    for j in range(4):
        c = slice(j * 128, j * 128 + 128)
        conv_back(vpad, cv_ref, y_s, dvp_ref, c, slice(512 + j * 128, 512 + j * 128 + 128), None)


def mixer_bwd(seg3, gm, qp, kp, vp, gp, ba, cq, ck, cv, rate, bias, gain, q, k, x, u, s, o):
    T = qp.shape[0]
    blocks = T // L
    sd = jax.ShapeDtypeStruct
    vm = lambda n, w: pltpu.VMEM((n, w), F32)
    return pl.pallas_call(
        functools.partial(bwd_kernel, blocks),
        out_shape=(sd((T, 256), BF16), sd((T, 256), BF16), sd((T, 512), BF16), sd((T, 512), BF16), sd((T, 128), BF16),
                   sd((8, 1024), F32), sd((8, 128), F32), sd((8, 256), F32)),
        in_specs=[VM] * 19, out_specs=[VM] * 8,
        scratch_shapes=[vm(T + PAD, 256), vm(T + PAD, 256), vm(T + PAD, 512), vm(T + 2 * PAD, L),
                        vm(T, 512), vm(T, 512), vm(T, 256), vm(T, 512), vm(T, 512), vm(T, 512), vm(T, 256), vm(T, 256), vm(8, 128), vm(T + PAD, 512)],
        compiler_params=pltpu.CompilerParams(vmem_limit_bytes=56 * 2 ** 20),
        name="mixer_backward",
    )(seg3, gm, qp, kp, vp, gp, ba, cq, ck, cv, rate, bias, gain, q, k, x, u, s, o)


MESH = pl.DeviceIdType.MESH
N_TENSOR = 8


def tensor_peers():
    d, t = lax.axis_index("dp"), lax.axis_index("tensor")
    return d, t, [lax.rem(t + j, N_TENSOR) for j in range(1, N_TENSOR)]


def greet(d, peers):
    barrier = pltpu.get_barrier_semaphore()
    for p in peers:
        pl.semaphore_signal(barrier, inc=1, device_id=(d, p), device_id_type=MESH)
    pl.semaphore_wait(barrier, len(peers))


def scatter_copies(d, peers, send, recv, ssem, rsem, own):
    return [
        pltpu.make_async_remote_copy(
            src_ref=send.at[pl.ds(pl.multiple_of(p * own, own), own)], dst_ref=recv.at[j],
            send_sem=ssem.at[j], recv_sem=rsem.at[j], device_id=(d, p), device_id_type=MESH)
        for j, p in enumerate(peers)]


def gather_copies(d, peers, shard, recv, ssem, rsem):
    return [
        pltpu.make_async_remote_copy(
            src_ref=shard, dst_ref=recv.at[j],
            send_sem=ssem.at[j], recv_sem=rsem.at[j], device_id=(d, p), device_id_type=MESH)
        for j, p in enumerate(peers)]


def summed(send, recv, t, own, r0, n):
    total = send[pl.ds(pl.multiple_of(t * own + r0, 8), n), :]
    for j in range(N_TENSOR - 1):
        total = total + recv[j, pl.ds(r0, n), :]
    return total


def gathered_out(t, shard, recv, out_ref, copies, own):
    out_ref[pl.ds(pl.multiple_of(t * own, own), own), :] = shard[...].astype(out_ref.dtype)
    for j in range(N_TENSOR - 1):
        copies[j].wait_recv()
        source = lax.rem(t + N_TENSOR - 1 - j, N_TENSOR)
        out_ref[pl.ds(pl.multiple_of(source * own, own), own), :] = recv[j].astype(out_ref.dtype)


def attn_kernel(low_ref, w_ref, x_ref, gain_ref, hid_ref, resid_ref,
                send, recv, shard, grecv, xown, csem, s1, r1, s2, r2):
    d, t, peers = tensor_peers()
    own = resid_ref.shape[0]
    mine = pltpu.make_async_copy(x_ref.at[pl.ds(pl.multiple_of(t * own, own), own)], xown, csem)
    mine.start()

    def partial(n, _):
        cols = pl.ds(pl.multiple_of(n * 256, 256), 256)
        send[:, cols] = mm1(low_ref[...], w_ref[:, cols], NN)
        return 0

    lax.fori_loop(0, send.shape[1] // 256, partial, 0)
    greet(d, peers)
    copies = scatter_copies(d, peers, send, recv, s1, r1, own)
    for c in copies:
        c.start()
    mine.wait()
    for c in copies:
        c.wait_recv()

    def finish(i, _):
        r0 = pl.multiple_of(i * 16, 16)
        resid = xown[pl.ds(r0, 16), :].astype(F32) + summed(send, recv, t, own, r0, 16)
        resid_ref[pl.ds(r0, 16), :] = resid
        n = resid * lax.rsqrt(jnp.mean(resid * resid, axis=-1, keepdims=True) + 1e-05)
        shard[pl.ds(r0, 16), :] = (n * gain_ref[0:1, :]).astype(BF16).astype(F32)
        return 0

    lax.fori_loop(0, own // 16, finish, 0)
    back = gather_copies(d, peers, shard, grecv, s2, r2)
    for c in back:
        c.start()
    gathered_out(t, shard, grecv, hid_ref, back, own)
    for c in copies + back:
        c.wait_send()


def dma_sems(*counts):
    return [pltpu.SemaphoreType.DMA((n,)) for n in counts]


ANY = pl.BlockSpec(memory_space=pl.ANY)


def attn_exchange(low, w_out, inputs, gain):
    T, D = inputs.shape
    own = T // N_TENSOR
    sd = jax.ShapeDtypeStruct
    return pl.pallas_call(
        attn_kernel,
        out_shape=(sd((T, D), BF16), sd((own, D), F32)),
        in_specs=[VM, VM, ANY, VM], out_specs=[VM, VM],
        scratch_shapes=[pltpu.VMEM((T, D), F32), pltpu.VMEM((7, own, D), F32), pltpu.VMEM((own, D), F32),
                        pltpu.VMEM((7, own, D), F32), pltpu.VMEM((own, D), BF16), pltpu.SemaphoreType.DMA(())] + dma_sems(7, 7, 7, 7),
        compiler_params=pltpu.CompilerParams(collective_id=1, has_side_effects=True, vmem_limit_bytes=56 * 2 ** 20),
        name="attn_exchange",
    )(low, w_out, inputs, gain)


def mid_kernel(gg_ref, gu_ref, wg_ref, wu_ref, ffn_ref, resid_in, og_ref, gain_ref,
               ga_ref, gres_ref, dgain_ref, out_ref,
               send, recv, shard, grecv, ogown, oshard, orecv, csem, s1, r1, s2, r2, s3, r3, s4, r4):
    d, t, peers = tensor_peers()
    own = gres_ref.shape[0]
    rows_t = pl.ds(pl.multiple_of(t * own, own), own)
    mine = pltpu.make_async_copy(og_ref.at[rows_t], ogown, csem.at[0])
    mine.start()
    ffn_own = pltpu.make_async_copy(ffn_ref.at[rows_t], oshard, csem.at[1])
    ffn_own.start()

    def partial(n, _):
        cols = pl.ds(pl.multiple_of(n * 256, 256), 256)
        send[:, cols] = mm1(gg_ref[...], wg_ref[cols, :], NT) + mm1(gu_ref[...], wu_ref[cols, :], NT)
        return 0

    lax.fori_loop(0, send.shape[1] // 256, partial, 0)
    greet(d, peers)
    copies = scatter_copies(d, peers, send, recv, s1, r1, own)
    copies2 = scatter_copies(d, peers, ffn_ref, orecv, s3, r3, own)
    for c in copies:
        c.start()
    for c in copies2:
        c.start()
    mine.wait()
    for c in copies:
        c.wait_recv()
    dgain_ref[...] = jnp.zeros_like(dgain_ref)

    def finish(i, _):
        r0 = pl.multiple_of(i * 16, 16)
        resid = resid_in[pl.ds(r0, 16), :]
        back = summed(send, recv, t, own, r0, 16)
        scale = lax.rsqrt(jnp.mean(resid * resid, axis=-1, keepdims=True) + 1e-05)
        n = resid * scale
        bn = back * n
        dgain_ref[...] = dgain_ref[...] + bn[0:8] + bn[8:16]
        b = back * gain_ref[0:1, :]
        g = ogown[pl.ds(r0, 16), :].astype(F32) + scale * (b - n * jnp.mean(b * n, axis=-1, keepdims=True))
        gres_ref[pl.ds(r0, 16), :] = g
        shard[pl.ds(r0, 16), :] = g.astype(BF16).astype(F32)
        return 0

    lax.fori_loop(0, own // 16, finish, 0)
    back = gather_copies(d, peers, shard, grecv, s2, r2)
    for c in back:
        c.start()
    for c in copies2:
        c.wait_recv()
    ffn_own.wait()

    def finish2(i, _):
        r0 = pl.multiple_of(i * 16, 16)
        total = oshard[pl.ds(r0, 16), :]
        for j in range(N_TENSOR - 1):
            total = total + orecv[j, pl.ds(r0, 16), :]
        oshard[pl.ds(r0, 16), :] = (resid_in[pl.ds(r0, 16), :] + total).astype(BF16).astype(F32)
        return 0

    lax.fori_loop(0, own // 16, finish2, 0)
    back2 = [
        pltpu.make_async_remote_copy(
            src_ref=oshard, dst_ref=out_ref.at[rows_t],
            send_sem=s4.at[j], recv_sem=r4.at[j], device_id=(d, p), device_id_type=MESH)
        for j, p in enumerate(peers)]
    for c in back2:
        c.start()
    own_out = pltpu.make_async_copy(oshard, out_ref.at[rows_t], csem.at[2])
    own_out.start()
    gathered_out(t, shard, grecv, ga_ref, back, own)
    for c in back2:
        c.wait_recv()
    own_out.wait()
    for c in copies + back + copies2 + back2:
        c.wait_send()


def mid_exchange(gg, gu, wg, wu, ffn, resid, og, gain):
    T, D = og.shape
    own = T // N_TENSOR
    sd = jax.ShapeDtypeStruct
    return pl.pallas_call(
        mid_kernel,
        out_shape=(sd((T, D), BF16), sd((own, D), F32), sd((8, D), F32), sd((T, D), F32)),
        in_specs=[VM, VM, VM, VM, ANY, VM, ANY, VM], out_specs=[VM, VM, VM, ANY],
        scratch_shapes=[pltpu.VMEM((T, D), F32), pltpu.VMEM((7, own, D), F32), pltpu.VMEM((own, D), F32),
                        pltpu.VMEM((7, own, D), F32), pltpu.VMEM((own, D), BF16), pltpu.VMEM((own, D), F32), pltpu.VMEM((7, own, D), F32),
                        pltpu.SemaphoreType.DMA((3,))] + dma_sems(7, 7, 7, 7, 7, 7, 7, 7),
        compiler_params=pltpu.CompilerParams(collective_id=2, has_side_effects=True, vmem_limit_bytes=58 * 2 ** 20),
        name="mid_exchange",
    )(gg, gu, wg, wu, ffn, resid, og, gain)


def in_kernel(part_ref, gres_ref, x_ref, gain_ref, ig_ref, dgain_ref,
              recv, shard, grecv, xown, pown, csem, s1, r1, s2, r2):
    d, t, peers = tensor_peers()
    own = gres_ref.shape[0]
    rows_t = pl.ds(pl.multiple_of(t * own, own), own)
    mine = pltpu.make_async_copy(x_ref.at[rows_t], xown, csem.at[0])
    mine.start()
    mine2 = pltpu.make_async_copy(part_ref.at[rows_t], pown, csem.at[1])
    mine2.start()
    greet(d, peers)
    copies = scatter_copies(d, peers, part_ref, recv, s1, r1, own)
    for c in copies:
        c.start()
    mine.wait()
    mine2.wait()
    for c in copies:
        c.wait_recv()
    dgain_ref[...] = jnp.zeros_like(dgain_ref)

    def finish(i, _):
        r0 = pl.multiple_of(i * 16, 16)
        x = xown[pl.ds(r0, 16), :].astype(F32)
        back = pown[pl.ds(r0, 16), :]
        for j in range(N_TENSOR - 1):
            back = back + recv[j, pl.ds(r0, 16), :]
        scale = lax.rsqrt(jnp.mean(x * x, axis=-1, keepdims=True) + 1e-05)
        n = x * scale
        bn = back * n
        dgain_ref[...] = dgain_ref[...] + bn[0:8] + bn[8:16]
        b = back * gain_ref[0:1, :]
        g = gres_ref[pl.ds(r0, 16), :] + scale * (b - n * jnp.mean(b * n, axis=-1, keepdims=True))
        shard[pl.ds(r0, 16), :] = g.astype(BF16).astype(F32)
        return 0

    lax.fori_loop(0, own // 16, finish, 0)
    back = gather_copies(d, peers, shard, grecv, s2, r2)
    for c in back:
        c.start()
    gathered_out(t, shard, grecv, ig_ref, back, own)
    for c in copies + back:
        c.wait_send()


def in_exchange(part, gres, inputs, gain):
    T, D = inputs.shape
    own = T // N_TENSOR
    sd = jax.ShapeDtypeStruct
    return pl.pallas_call(
        in_kernel,
        out_shape=(sd((T, D), BF16), sd((8, D), F32)),
        in_specs=[ANY, VM, ANY, VM], out_specs=[VM, VM],
        scratch_shapes=[pltpu.VMEM((7, own, D), F32), pltpu.VMEM((own, D), F32),
                        pltpu.VMEM((7, own, D), F32), pltpu.VMEM((own, D), BF16), pltpu.VMEM((own, D), F32), pltpu.SemaphoreType.DMA((2,))] + dma_sems(7, 7, 7, 7),
        compiler_params=pltpu.CompilerParams(collective_id=3, has_side_effects=True, vmem_limit_bytes=56 * 2 ** 20),
        name="in_exchange",
    )(part, gres, inputs, gain)


def matmul(left, right):
    return jnp.dot(left, right, preferred_element_type=F32)


def rows8(v):
    return jnp.broadcast_to(v[None, :], (8, v.shape[0]))


def per_device(inputs, segments, attn_gain, w_query, w_key, w_value, w_gate, w_beta, w_alpha, conv_query, conv_key, conv_value,
               decay_log, decay_bias, head_gain, w_out, ffn_gain, w_up_gate, w_up, w_down, out_grad):
    T, D = inputs.shape
    blocks = T // L
    tokens_in = inputs.astype(F32)
    scale_in = lax.rsqrt(jnp.mean(tokens_in * tokens_in, axis=-1, keepdims=True) + 1e-05)
    hidden_in = (tokens_in * scale_in * attn_gain).astype(BF16)
    w_ba = jnp.concatenate([w_beta, w_alpha, jnp.zeros((D, 124), BF16)], axis=1)
    qp, kp, vp, gp = (matmul(hidden_in, w) for w in (w_query, w_key, w_value, w_gate))
    ba = matmul(hidden_in, w_ba)
    rate = jnp.zeros((8, 128), F32).at[:, 2:4].set(-jnp.exp(decay_log))
    bias = jnp.zeros((8, 128), F32).at[:, 2:4].set(decay_bias)
    seg = segments.astype(F32).reshape(blocks, 1, L)
    prev = jnp.concatenate([seg[:1, :, :1], seg[:-1, :, L - 1:]], axis=0)
    seg3 = jnp.concatenate([seg, jnp.broadcast_to(prev, seg.shape), jnp.zeros((blocks, 6, L), F32)], axis=1)
    gain8 = rows8(head_gain)
    low, q, k, x, u, s, o = mixer_fwd(seg3, qp, kp, vp, gp, ba, conv_query, conv_key, conv_value, rate, bias, gain8)
    hidden_mid, resid = attn_exchange(low, w_out, inputs, rows8(ffn_gain))
    gate_pre = matmul(hidden_mid, w_up_gate)
    up_pre = matmul(hidden_mid, w_up)
    sig = jax.nn.sigmoid(gate_pre)
    act = gate_pre * sig
    inner = (act * up_pre).astype(BF16)
    ffn = matmul(inner, w_down)
    grad_inner = matmul(out_grad, w_down.T)
    grad_down = matmul(inner.T, out_grad)
    gg = (grad_inner * up_pre * sig * (1.0 + gate_pre * (1.0 - sig))).astype(BF16)
    gu = (grad_inner * act).astype(BF16)
    grad_up_gate = matmul(hidden_mid.T, gg)
    grad_up = matmul(hidden_mid.T, gu)
    grad_attn, grad_resid, ffn_gain_part, out32 = mid_exchange(gg, gu, w_up_gate, w_up, ffn, resid, out_grad, rows8(ffn_gain))
    outputs = out32.astype(BF16)
    grad_out = matmul(low.T, grad_attn)
    grad_mixed = matmul(grad_attn, w_out.T)
    gq, gk, gv, gt, gba, taps, small, hgain = mixer_bwd(
        seg3, grad_mixed, qp, kp, vp, gp, ba, conv_query, conv_key, conv_value, rate, bias, gain8, q, k, x, u, s, o)
    grad_query = matmul(hidden_in.T, gq)
    grad_key = matmul(hidden_in.T, gk)
    grad_value = matmul(hidden_in.T, gv)
    grad_gate = matmul(hidden_in.T, gt)
    grad_ba = matmul(hidden_in.T, gba)
    part = matmul(gq, w_query.T) + matmul(gk, w_key.T) + matmul(gv, w_value.T) + matmul(gt, w_gate.T) + matmul(gba, w_ba.T)
    input_grad, attn_gain_part = in_exchange(part, grad_resid, inputs, rows8(attn_gain))
    both = lax.psum((jnp.sum(attn_gain_part, axis=0), jnp.sum(ffn_gain_part, axis=0), hgain[0]), ("dp", "tensor"))
    sums = lax.psum((taps[:4], small[:2, 2:4]), "dp")

    def scatter(g, dim=0):
        return lax.psum_scatter(g, "dp", scatter_dimension=dim, tiled=True)

    return (outputs, input_grad, both[0], scatter(grad_query), scatter(grad_key), scatter(grad_value), scatter(grad_gate),
            scatter(grad_ba[:, 0:2]), scatter(grad_ba[:, 2:4]), sums[0][:, 0:256], sums[0][:, 256:512], sums[0][:, 512:1024],
            sums[1][1], sums[1][0], both[2], scatter(grad_out, 1), both[1], scatter(grad_up_gate), scatter(grad_up), scatter(grad_down, 1))


def solution(mesh):
    col, row, rep = P(None, "tensor"), P("tensor", None), P()
    tok, both, head = P("dp", None), P("dp", "tensor"), P("tensor")
    return jax.shard_map(
        per_device,
        mesh=mesh,
        in_specs=(tok, tok, rep, col, col, col, col, col, col, col, col, col, head, head, rep, row, rep, col, col, row, tok),
        out_specs=(tok, tok, rep, both, both, both, both, both, both, col, col, col, head, head, rep, P("tensor", "dp"), rep, both, both, P("tensor", "dp")),
        check_vma=False,
    )
```

```python
import functools
import jax, jax.numpy as jnp
from jax import lax
from jax.experimental import pallas as pl
from jax.experimental.pallas import tpu as pltpu
from jax.sharding import PartitionSpec as P

F32 = jnp.float32
BF16 = jnp.bfloat16
L = 128
PAD = 8
NN = (((1,), (0,)), ((), ()))
NT = (((1,), (1,)), ((), ()))
TN = (((0,), (0,)), ((), ()))


def split(x):
    hi = x.astype(BF16)
    return hi, (x - hi.astype(F32)).astype(BF16)


def mm1(a, b, dims):
    return lax.dot_general(a, b, dims, preferred_element_type=F32)


def mm3(a, b, dims=NN):
    return mm1(a[0], b[0], dims) + (mm1(a[0], b[1], dims) + mm1(a[1], b[0], dims))


def sigmoid(x):
    return 1.0 / (1.0 + jnp.exp(-x))


def rows(ref, b, n=L, lead=0):
    return ref[pl.ds(pl.multiple_of(b * L, L) + lead, n)]


def decay_tile(ba, rate, bias):
    lane = lax.broadcasted_iota(jnp.int32, ba.shape, 1)
    shifted = ba + bias
    soft = jnp.maximum(shifted, 0.0) + jnp.log1p(jnp.exp(-jnp.abs(shifted)))
    return jnp.where(lane < 2, sigmoid(ba), rate * soft)


def tri_sum(tile, dims):
    r = lax.broadcasted_iota(jnp.int32, (L, L), 0)
    c = lax.broadcasted_iota(jnp.int32, (L, L), 1)
    tri = (r >= c).astype(BF16)
    p0 = tile.astype(BF16)
    rest = tile - p0.astype(F32)
    p1 = rest.astype(BF16)
    p2 = (rest - p1.astype(F32)).astype(BF16)
    return mm1(tri, p0, dims) + (mm1(tri, p1, dims) + mm1(tri, p2, dims))


def block_decay(b, seg_ref, ba_ref, rate, bias):
    tile = decay_tile(rows(ba_ref, b), rate, bias)
    cum = tri_sum(tile, NN)
    lane = lax.broadcasted_iota(jnp.int32, (L, L), 1)
    both = jnp.where(lane < 2, tile, cum)
    flat = both.T
    seg_row = seg_ref[b, 0:1, :]
    seg_col = jnp.broadcast_to(seg_row, (L, L)).T
    prev = seg_ref[b, 1:2, 0:1]
    r = lax.broadcasted_iota(jnp.int32, (L, L), 0)
    keep = (seg_col == seg_row) & (r >= lane)
    strict_keep = r > lane
    carry_keep = seg_col[:, 0:1] == prev
    out = []
    for h in range(2):
        c_col = cum[:, 2 + h:3 + h]
        c_row = flat[2 + h:3 + h, :]
        beta_row = flat[h:h + 1, :]
        decay = jnp.where(keep, jnp.exp(jnp.where(keep, c_col - c_row, 0.0)), 0.0)
        carry = jnp.where(carry_keep, jnp.exp(c_col), 0.0)
        last_keep = seg_col[:, 0:1] == seg_row[:, L - 1:L]
        last_decay = jnp.where(last_keep, jnp.exp(jnp.where(last_keep, c_col[L - 1:L, :] - c_col, 0.0)), 0.0)
        beta_col = tile[:, h:h + 1]
        out.append((decay, carry, beta_row, beta_col, last_decay))
    return out, strict_keep, (tile, seg_col)


def conv_block(b, pre_ref, taps_ref, seg_ref, cols, segpad_ref):
    base = pl.multiple_of(b * L, L)
    z = pre_ref[pl.ds(base, L + PAD), cols]
    s = segpad_ref[pl.ds(base, L + PAD), 0:1]
    total = z[PAD:] * taps_ref[0:1, cols]
    for k in range(1, 4):
        same = (s[PAD - k:PAD - k + L] == s[PAD:]).astype(F32)
        total = total + z[PAD - k:PAD - k + L] * same * taps_ref[k:k + 1, cols]
    return total


def inverse_many(mats):
    r = lax.broadcasted_iota(jnp.int32, (L, L), 0)
    c = lax.broadcasted_iota(jnp.int32, (L, L), 1)
    eye = (r == c).astype(F32)
    xs = [eye - jnp.where((r // 2 == c // 2), a, 0.0) for a in mats]
    s = 2
    while s < L:
        pick = (r // (2 * s) == c // (2 * s)) & (r // s != c // s)
        sx = [split(x) for x in xs]
        sa = [split(jnp.where(pick, a, 0.0)) for a in mats]
        t = [mm3(x, a) for x, a in zip(sx, sa)]
        xs = [x - mm3(split(y), z) for x, y, z in zip(xs, t, sx)]
        s *= 2
    return xs


def fwd_kernel(blocks, group, seg_ref, qp_ref, kp_ref, vp_ref, gp_ref, ba_ref, cq_ref, ck_ref, cv_ref, rate_ref, bias_ref, gain_ref,
               low_ref, q_ref, k_ref, x_ref, u_ref, s_ref, o_ref,
               qpad, kpad, vpad, segpad, w_s, u0_s, kw_s):
    T = blocks * L
    rate, bias = rate_ref[0:1, :], bias_ref[0:1, :]
    for pad, src in ((qpad, qp_ref), (kpad, kp_ref), (vpad, vp_ref)):
        pad[0:PAD, :] = jnp.zeros((PAD, pad.shape[1]), F32)
        pad[PAD:PAD + T, :] = src[...]
    segpad[0:PAD, :] = jnp.full((PAD, L), -1.0, F32)
    for b in range(blocks):
        segpad[PAD + b * L:PAD + (b + 1) * L, :] = jnp.broadcast_to(seg_ref[b, 0:1, :], (L, L)).T

    def phase_a(g, _):
        a_mats, keepers = [], []
        for i in range(group):
            b = g * group + i
            base = pl.multiple_of(b * L, L)
            per_head, strict_keep, _u = block_decay(b, seg_ref, ba_ref, rate, bias)
            for h in range(2):
                decay, carry, beta_row, beta_col, last_decay = per_head[h]
                kc = slice(h * 128, h * 128 + 128)
                vc = slice(h * 256, h * 256 + 256)
                y = conv_block(b, qpad, cq_ref, seg_ref, kc, segpad)
                q = y * sigmoid(y)
                q = q * (lax.rsqrt(jnp.sum(q * q, axis=-1, keepdims=True) + 1e-06) * (128 ** -0.5))
                y = conv_block(b, kpad, ck_ref, seg_ref, kc, segpad)
                k = y * sigmoid(y)
                k = k * lax.rsqrt(jnp.sum(k * k, axis=-1, keepdims=True) + 1e-06)
                q_ref[pl.ds(base, L), kc] = q
                k_ref[pl.ds(base, L), kc] = k
                y = conv_block(b, vpad, cv_ref, seg_ref, vc, segpad)
                v = y * sigmoid(y)
                ks = split(k)
                kk = mm3(ks, ks, NT)
                a_mats.append(jnp.where(strict_keep, decay, 0.0) * kk * beta_row)
                kw_s[pl.ds(base, L), kc] = k * (last_decay * beta_col)
                keepers.append((b, base, h, kc, vc, v, k * carry))
        xs = inverse_many(a_mats)
        for x, (b, base, h, kc, vc, v, gk) in zip(xs, keepers):
            x_ref[pl.ds(base, L), kc] = x
            sx = split(x)
            u0_s[pl.ds(base, L), vc] = mm3(sx, split(v))
            w_s[pl.ds(base, L), kc] = mm3(sx, split(gk))
        return 0

    lax.fori_loop(0, blocks // group, phase_a, 0)

    def phase_b(b, state):
        base = pl.multiple_of(b * L, L)
        per_head, strict_keep, _u = block_decay(b, seg_ref, ba_ref, rate, bias)
        new = []
        for h in range(2):
            decay, carry, beta_row, beta_col, last_decay = per_head[h]
            kc = slice(h * 128, h * 128 + 128)
            vc = slice(h * 256, h * 256 + 256)
            s = state[h]
            s_ref[pl.ds(base, L), vc] = s
            ss = split(s)
            u = u0_s[pl.ds(base, L), vc] - mm3(split(w_s[pl.ds(base, L), kc]), ss)
            u_ref[pl.ds(base, L), vc] = u
            new.append(carry[L - 1:L, :] * s + mm3(split(kw_s[pl.ds(base, L), kc]), split(u), TN))
        return tuple(new)

    zero = jnp.zeros((128, 256), F32)
    lax.fori_loop(0, blocks, phase_b, (zero, zero))

    def phase_c(b, _):
        base = pl.multiple_of(b * L, L)
        per_head, strict_keep, _u = block_decay(b, seg_ref, ba_ref, rate, bias)
        for h in range(2):
            decay, carry, beta_row, beta_col, last_decay = per_head[h]
            kc = slice(h * 128, h * 128 + 128)
            vc = slice(h * 256, h * 256 + 256)
            q = q_ref[pl.ds(base, L), kc]
            qk = mm3(split(q), split(k_ref[pl.ds(base, L), kc]), NT)
            p = decay * qk * beta_row
            o = mm3(split(q * carry), split(s_ref[pl.ds(base, L), vc])) + mm3(split(p), split(u_ref[pl.ds(base, L), vc]))
            o_ref[pl.ds(base, L), vc] = o
            gp = gp_ref[pl.ds(base, L), vc]
            n = o * lax.rsqrt(jnp.mean(o * o, axis=-1, keepdims=True) + 1e-05)
            low_ref[pl.ds(base, L), vc] = (n * gain_ref[0:1, :] * (gp * sigmoid(gp))).astype(BF16)
        return 0

    lax.fori_loop(0, blocks, phase_c, 0)


VM = pl.BlockSpec(memory_space=pltpu.VMEM)


def mixer_fwd(seg3, qp, kp, vp, gp, ba, cq, ck, cv, rate, bias, gain, group=2):
    T = qp.shape[0]
    blocks = T // L
    sd = jax.ShapeDtypeStruct
    return pl.pallas_call(
        functools.partial(fwd_kernel, blocks, group),
        out_shape=(sd((T, 512), BF16), sd((T, 256), F32), sd((T, 256), F32), sd((T, 256), F32), sd((T, 512), F32),
                   sd((T, 512), F32), sd((T, 512), F32)),
        in_specs=[VM] * 12, out_specs=[VM] * 7,
        scratch_shapes=[pltpu.VMEM((T + PAD, 256), F32), pltpu.VMEM((T + PAD, 256), F32), pltpu.VMEM((T + PAD, 512), F32),
                        pltpu.VMEM((T + PAD, L), F32), pltpu.VMEM((T, 256), F32), pltpu.VMEM((T, 512), F32), pltpu.VMEM((T, 256), F32)],
        compiler_params=pltpu.CompilerParams(vmem_limit_bytes=56 * 2 ** 20),
        name="mixer_forward",
    )(seg3, qp, kp, vp, gp, ba, cq, ck, cv, rate, bias, gain)


def bwd_kernel(blocks, seg_ref, gm_ref, qp_ref, kp_ref, vp_ref, gp_ref, ba_ref, cq_ref, ck_ref, cv_ref, rate_ref, bias_ref, gain_ref,
               q_ref, k_ref, x_ref, u_ref, s_ref, o_ref,
               dqp_ref, dkp_ref, dvp_ref, dgp_ref, dba_ref, dtap_ref, dsmall_ref, dgain_ref,
               qpad, kpad, vpad, segpad, do_s, y0_s, z_s, r_s, y_s, ds_s, dq_s, dk_s, dv_s, acc_s):
    T = blocks * L
    rate, bias = rate_ref[0:1, :], bias_ref[0:1, :]
    for pad, src in ((qpad, qp_ref), (kpad, kp_ref), (vpad, vp_ref)):
        pad[0:PAD, :] = jnp.zeros((PAD, pad.shape[1]), F32)
        pad[PAD:PAD + T, :] = src[...]
    segpad[0:PAD, :] = jnp.full((PAD, L), -1.0, F32)
    segpad[PAD + T:, :] = jnp.full((PAD, L), -1.0, F32)
    for b in range(blocks):
        segpad[PAD + b * L:PAD + (b + 1) * L, :] = jnp.broadcast_to(seg_ref[b, 0:1, :], (L, L)).T
    dgain_ref[...] = jnp.zeros_like(dgain_ref)
    dsmall_ref[...] = jnp.zeros_like(dsmall_ref)
    dtap_ref[...] = jnp.zeros_like(dtap_ref)

    def phase_1(b, _):
        base = pl.multiple_of(b * L, L)
        per_head, strict_keep, _u = block_decay(b, seg_ref, ba_ref, rate, bias)
        for h in range(2):
            decay, carry, beta_row, beta_col, last_decay = per_head[h]
            kc = slice(h * 128, h * 128 + 128)
            vc = slice(h * 256, h * 256 + 256)
            o = o_ref[pl.ds(base, L), vc]
            gp = gp_ref[pl.ds(base, L), vc]
            gm = gm_ref[pl.ds(base, L), vc]
            gain = gain_ref[0:1, :]
            sg = sigmoid(gp)
            r = lax.rsqrt(jnp.mean(o * o, axis=-1, keepdims=True) + 1e-05)
            n = o * r
            act = gp * sg
            gn = gm * n
            dgain_ref[0:1, :] = dgain_ref[0:1, :] + jnp.sum(gn * act, axis=0, keepdims=True)
            dgp_ref[pl.ds(base, L), vc] = (gn * gain * (sg * (1.0 + gp * (1.0 - sg)))).astype(BF16)
            dn = gm * gain * act
            do = r * (dn - n * jnp.mean(dn * n, axis=-1, keepdims=True))
            do_s[pl.ds(base, L), vc] = do
            q, k = q_ref[pl.ds(base, L), kc], k_ref[pl.ds(base, L), kc]
            p = decay * mm3(split(q), split(k), NT) * beta_row
            sdo = split(do)
            sx = split(x_ref[pl.ds(base, L), kc])
            y0 = mm3(sx, split(mm3(split(p), sdo, TN)), TN)
            z = mm3(sx, split(k * (last_decay * beta_col)), TN)
            y0_s[pl.ds(base, L), vc] = y0
            z_s[pl.ds(base, L), kc] = z
            r_s[pl.ds(base, L), vc] = mm3(split(q * carry), sdo, TN)
        return 0

    lax.fori_loop(0, blocks, phase_1, 0)

    def phase_2(i, grads):
        b = blocks - 1 - i
        base = pl.multiple_of(b * L, L)
        per_head, strict_keep, _u = block_decay(b, seg_ref, ba_ref, rate, bias)
        new = []
        for h in range(2):
            decay, carry, beta_row, beta_col, last_decay = per_head[h]
            kc = slice(h * 128, h * 128 + 128)
            vc = slice(h * 256, h * 256 + 256)
            ds = grads[h]
            ds_s[pl.ds(base, L), vc] = ds
            y = y0_s[pl.ds(base, L), vc] + mm3(split(z_s[pl.ds(base, L), kc]), split(ds))
            y_s[pl.ds(base, L), vc] = y
            new.append(carry[L - 1:L, :] * ds + r_s[pl.ds(base, L), vc]
                       - mm3(split(k_ref[pl.ds(base, L), kc] * carry), split(y), TN))
        return tuple(new)

    zero = jnp.zeros((128, 256), F32)
    lax.fori_loop(0, blocks, phase_2, (zero, zero))

    def phase_3(b, _):
        base = pl.multiple_of(b * L, L)
        per_head, strict_keep, (tile, seg_col) = block_decay(b, seg_ref, ba_ref, rate, bias)
        lane = lax.broadcasted_iota(jnp.int32, (L, L), 1)
        rowi = lax.broadcasted_iota(jnp.int32, (L, L), 0)
        row_tile = jnp.zeros((L, L), F32)
        col_tile = jnp.zeros((L, L), F32)
        for h in range(2):
            decay, carry, beta_row, beta_col, last_decay = per_head[h]
            kc = slice(h * 128, h * 128 + 128)
            vc = slice(h * 256, h * 256 + 256)
            q, k = q_ref[pl.ds(base, L), kc], k_ref[pl.ds(base, L), kc]
            sq, sk = split(q), split(k)
            kk = mm3(sk, sk, NT)
            qk = mm3(sq, sk, NT)
            s, u = s_ref[pl.ds(base, L), vc], u_ref[pl.ds(base, L), vc]
            do, y, ds = do_s[pl.ds(base, L), vc], y_s[pl.ds(base, L), vc], ds_s[pl.ds(base, L), vc]
            ss, su, sdo, sy, sds = split(s), split(u), split(do), split(y), split(ds)
            do_st = mm3(sdo, ss, NT)
            y_st = mm3(sy, ss, NT)
            u_dst = mm3(su, sds, NT)
            dp = mm3(sdo, su, NT)
            da = -mm3(sy, su, NT)
            dcarry = jnp.sum(q * do_st - k * y_st, axis=-1, keepdims=True)
            dcarry_last = jnp.sum(jnp.sum(ds * s, axis=0, keepdims=True), axis=1, keepdims=True)
            dw = jnp.sum(u_dst * k, axis=-1, keepdims=True)
            dpd = dp * decay
            dad = jnp.where(strict_keep, da * decay, 0.0)
            dqk = dpd * beta_row
            dkk = dad * beta_row
            prod = dpd * qk + dad * kk
            dbeta_row = jnp.sum(prod, axis=0, keepdims=True)
            dec_grad = prod * beta_row
            dc_col = jnp.sum(dec_grad, axis=1, keepdims=True) + dcarry * carry
            dc_row = -jnp.sum(dec_grad, axis=0, keepdims=True)
            dlast = dw * beta_col * last_decay
            row1 = rowi[:, 0:1]
            dc_col = dc_col - dlast
            dc_col = dc_col + jnp.where(row1 == L - 1, jnp.sum(dlast, axis=0, keepdims=True) + dcarry_last * carry, 0.0)
            dbeta_col = dw * last_decay
            row_tile = row_tile + jnp.where(rowi == h, dbeta_row, 0.0) + jnp.where(rowi == 2 + h, dc_row, 0.0)
            col_tile = col_tile + jnp.where(lane == h, dbeta_col, 0.0) + jnp.where(lane == 2 + h, dc_col, 0.0)
            sdqk, sdkk = split(dqk), split(dkk + dkk.T)
            dq_s[pl.ds(base, L), kc] = carry * do_st + mm3(sdqk, sk)
            dk_s[pl.ds(base, L), kc] = (mm3(sdqk, sq, TN) + mm3(sdkk, sk) - carry * y_st
                                        + (last_decay * beta_col) * u_dst)
        grad = col_tile + row_tile.T
        dld = tri_sum(grad, TN)
        ba = rows(ba_ref, b)
        sig_alpha = sigmoid(ba + bias)
        dalpha = dld * rate * sig_alpha
        dpre = jnp.where(lane < 2, grad * tile * (1.0 - tile), jnp.where(lane < 4, dalpha, 0.0))
        dba_ref[pl.ds(base, L), :] = dpre.astype(BF16)
        dsmall_ref[0:1, :] = dsmall_ref[0:1, :] + jnp.sum(dpre, axis=0, keepdims=True)
        dsmall_ref[1:2, :] = dsmall_ref[1:2, :] + jnp.sum(dld * tile, axis=0, keepdims=True)
        return 0

    lax.fori_loop(0, blocks, phase_3, 0)

    def conv_back(pre, taps_ref, src, out_ref, cols, tap_cols, scale):
        acc_s[T:, cols] = jnp.zeros((PAD, 128), F32)

        def one(b, tap_grads):
            base = pl.multiple_of(b * L, L)
            y = conv_block(b, pre, taps_ref, None, cols, segpad)
            sg = sigmoid(y)
            act = y * sg
            d = src[pl.ds(base, L), cols]
            if scale is not None:
                r = lax.rsqrt(jnp.sum(act * act, axis=-1, keepdims=True) + 1e-06)
                d = (scale * r) * (d - act * (r * r * jnp.sum(d * act, axis=-1, keepdims=True)))
            dy = d * (sg * (1.0 + y * (1.0 - sg)))
            acc_s[pl.ds(base, L), cols] = dy
            z = pre[pl.ds(base, L + PAD), cols]
            s = segpad[pl.ds(base, L + PAD), 0:1]
            new = [tap_grads[0] + jnp.sum(dy * z[PAD:], axis=0, keepdims=True)]
            for t in range(1, 4):
                same = (s[PAD - t:PAD - t + L] == s[PAD:]).astype(F32)
                new.append(tap_grads[t] + jnp.sum(dy * (z[PAD - t:PAD - t + L] * same), axis=0, keepdims=True))
            return tuple(new)

        zero = jnp.zeros((1, 128), F32)
        res = lax.fori_loop(0, blocks, one, (zero,) * 4)
        for t in range(4):
            dtap_ref[t:t + 1, tap_cols] = res[t]

        def two(b, _):
            base = pl.multiple_of(b * L, L)
            dy = acc_s[pl.ds(base, L + PAD), cols]
            s = segpad[pl.ds(base + PAD, L + PAD), 0:1]
            total = dy[:L] * taps_ref[0:1, cols]
            for t in range(1, 4):
                same = (s[t:t + L] == s[:L]).astype(F32)
                total = total + dy[t:t + L] * same * taps_ref[t:t + 1, cols]
            out_ref[pl.ds(base, L), cols] = total.astype(BF16)
            return 0

        lax.fori_loop(0, blocks, two, 0)

    for h in range(2):
        c = slice(h * 128, h * 128 + 128)
        conv_back(qpad, cq_ref, dq_s, dqp_ref, c, slice(h * 128, h * 128 + 128), 128 ** -0.5)
        conv_back(kpad, ck_ref, dk_s, dkp_ref, c, slice(256 + h * 128, 256 + h * 128 + 128), 1.0)
    for j in range(4):
        c = slice(j * 128, j * 128 + 128)
        conv_back(vpad, cv_ref, y_s, dvp_ref, c, slice(512 + j * 128, 512 + j * 128 + 128), None)


def mixer_bwd(seg3, gm, qp, kp, vp, gp, ba, cq, ck, cv, rate, bias, gain, q, k, x, u, s, o):
    T = qp.shape[0]
    blocks = T // L
    sd = jax.ShapeDtypeStruct
    vm = lambda n, w: pltpu.VMEM((n, w), F32)
    return pl.pallas_call(
        functools.partial(bwd_kernel, blocks),
        out_shape=(sd((T, 256), BF16), sd((T, 256), BF16), sd((T, 512), BF16), sd((T, 512), BF16), sd((T, 128), BF16),
                   sd((8, 1024), F32), sd((8, 128), F32), sd((8, 256), F32)),
        in_specs=[VM] * 19, out_specs=[VM] * 8,
        scratch_shapes=[vm(T + PAD, 256), vm(T + PAD, 256), vm(T + PAD, 512), vm(T + 2 * PAD, L),
                        vm(T, 512), vm(T, 512), vm(T, 256), vm(T, 512), vm(T, 512), vm(T, 512), vm(T, 256), vm(T, 256), vm(8, 128), vm(T + PAD, 512)],
        compiler_params=pltpu.CompilerParams(vmem_limit_bytes=56 * 2 ** 20),
        name="mixer_backward",
    )(seg3, gm, qp, kp, vp, gp, ba, cq, ck, cv, rate, bias, gain, q, k, x, u, s, o)


MESH = pl.DeviceIdType.MESH
NT_ = 8
HALF = 1024


class Ring:
    def __init__(self):
        self.d = lax.axis_index("dp")
        self.t = lax.axis_index("tensor")
        self.y = lax.rem(self.t, 2)
        self.z = self.t // 2
        self.right = (self.d, self.at(1) * 2 + self.y)
        self.left = (self.d, self.at(3) * 2 + self.y)
        self.flip = (self.d, self.z * 2 + 1 - self.y)

    def at(self, k):
        return lax.rem(self.z + k, 4)

    def rows(self, k, other, own):
        side = 1 - self.y if other else self.y
        return pl.ds(pl.multiple_of((self.at(k) * 2 + side) * own, own), own)

    def quarter(self, k, own):
        return pl.ds(pl.multiple_of(self.at(k) * 2 * own, 2 * own), 2 * own)


class Sends:
    def __init__(self, ssem, rsem):
        self.ssem, self.rsem, self.made = ssem, rsem, []

    def make(self, i, src, dst, device):
        return pltpu.make_async_remote_copy(src_ref=src, dst_ref=dst, send_sem=self.ssem.at[i], recv_sem=self.rsem.at[i],
                                            device_id=device, device_id_type=MESH)

    def go(self, i, src, dst, device):
        c = self.make(i, src, dst, device)
        c.start()
        self.made.append(c)

    def got(self, i, dst, device):
        self.make(i, dst, dst, device).wait_recv()

    def drain(self):
        for c in self.made:
            c.wait_send()


def greet(devices):
    barrier = pltpu.get_barrier_semaphore()
    for dev in devices:
        pl.semaphore_signal(barrier, inc=1, device_id=dev, device_id_type=MESH)
    pl.semaphore_wait(barrier, len(devices))


ZA, ZB, YA, YB = (pl.ds(i * 512, 512) for i in range(4))
ZZ, YY = pl.ds(0, HALF), pl.ds(HALF, HALF)
LO, HI = pl.ds(0, 512), pl.ds(512, 512)


def scatter_scratch(own):
    return [pltpu.VMEM((4, own, 1024), F32), pltpu.VMEM((6, 2 * own, 512), F32), pltpu.VMEM((6, own, 512), F32),
            pltpu.VMEM((own, 1024), F32), pltpu.VMEM((own, 1024), F32),
            pltpu.SemaphoreType.DMA((17,)), pltpu.SemaphoreType.DMA((17,))]


def add_rows(dst, src_of, n):
    def one(i, _):
        r = pl.multiple_of(i * 16, 16)
        dst[pl.ds(r, 16), :] = dst[pl.ds(r, 16), :] + src_of(r)
        return 0
    lax.fori_loop(0, n // 16, one, 0)


def sub(ref, rows, cols):
    return lambda r: ref[pl.ds(pl.multiple_of(rows.start + r, 16), 16), cols]


class Scatter:
    def __init__(self, ring, part, scratch, own):
        self.ring, self.part, self.own = ring, part, own
        self.yb, self.zb, self.yr, self.zsend, self.zf, ssem, rsem = scratch
        self.s = Sends(ssem, rsem)

    def start(self):
        g, s, p, own = self.ring, self.s, self.part, self.own
        s.go(0, p.at[g.quarter(2, own), ZB], self.zb.at[0], g.right)
        s.go(1, p.at[g.quarter(2, own), ZA], self.zb.at[1], g.left)
        s.go(6, p.at[g.rows(2, True, own), YY], self.yb.at[2], g.flip)
        s.go(2, p.at[g.quarter(1, own), ZA], self.zb.at[2], g.right)
        s.go(3, p.at[g.quarter(3, own), ZB], self.zb.at[3], g.left)
        s.go(7, p.at[g.rows(1, True, own), YY], self.yb.at[1], g.flip)
        s.go(8, p.at[g.rows(3, True, own), YY], self.yb.at[3], g.flip)
        s.go(9, p.at[g.rows(0, True, own), YY], self.yb.at[0], g.flip)

    def middle(self):
        g, s, p, own = self.ring, self.s, self.part, self.own
        yb, zb, yr = self.yb, self.zb, self.yr
        s.got(6, yb.at[2], g.flip)
        add_rows(yb.at[2], sub(p, g.rows(2, False, own), YY), own)
        s.go(10, yb.at[2, :, HI], yr.at[0], g.right)
        s.go(11, yb.at[2, :, LO], yr.at[1], g.left)
        s.got(0, zb.at[0], g.left)
        add_rows(zb.at[0], sub(p, g.quarter(1, own), ZB), 2 * own)
        s.go(4, zb.at[0], zb.at[4], g.right)
        s.got(1, zb.at[1], g.right)
        add_rows(zb.at[1], sub(p, g.quarter(3, own), ZA), 2 * own)
        s.go(5, zb.at[1], zb.at[5], g.left)
        s.got(7, yb.at[1], g.flip)
        add_rows(yb.at[1], sub(p, g.rows(1, False, own), YY), own)
        s.go(12, yb.at[1, :, LO], yr.at[2], g.right)
        s.got(10, yr.at[0], g.left)
        add_rows(yr.at[0], lambda r: yb[1, pl.ds(r, 16), HI], own)
        s.go(14, yr.at[0], yr.at[4], g.right)
        s.got(8, yb.at[3], g.flip)
        add_rows(yb.at[3], sub(p, g.rows(3, False, own), YY), own)
        s.go(13, yb.at[3, :, HI], yr.at[3], g.left)
        s.got(11, yr.at[1], g.right)
        add_rows(yr.at[1], lambda r: yb[3, pl.ds(r, 16), LO], own)
        s.go(15, yr.at[1], yr.at[5], g.left)
        s.got(2, zb.at[2], g.left)
        s.got(3, zb.at[3], g.right)
        s.got(4, zb.at[4], g.left)
        s.got(5, zb.at[5], g.right)
        base = g.rows(0, True, own).start
        lead = (1 - g.y) * own

        def one(i, _):
            r = pl.multiple_of(i * 16, 16)
            at = pl.ds(pl.multiple_of(lead + r, 16), 16)
            mine = pl.ds(pl.multiple_of(base + r, 16), 16)
            self.zsend[pl.ds(r, 16), LO] = p[mine, ZA] + (zb[2, at, :] + zb[5, at, :])
            self.zsend[pl.ds(r, 16), HI] = p[mine, ZB] + (zb[3, at, :] + zb[4, at, :])
            return 0

        lax.fori_loop(0, own // 16, one, 0)
        s.go(16, self.zsend, self.zf, g.flip)

    def finish(self):
        g, s = self.ring, self.s
        s.got(9, self.yb.at[0], g.flip)
        s.got(12, self.yr.at[2], g.left)
        s.got(13, self.yr.at[3], g.right)
        s.got(14, self.yr.at[4], g.left)
        s.got(15, self.yr.at[5], g.right)
        s.got(16, self.zf, g.flip)

    def value(self, r):
        g, p, own = self.ring, self.part, self.own
        zb, yr = self.zb, self.yr
        at = pl.ds(pl.multiple_of(g.y * own + r, 16), 16)
        here = pl.ds(r, 16)
        mine = pl.ds(pl.multiple_of(g.rows(0, False, own).start + r, 16), 16)
        za = p[mine, ZA] + (zb[2, at, :] + zb[5, at, :]) + self.zf[here, LO]
        zz = p[mine, ZB] + (zb[3, at, :] + zb[4, at, :]) + self.zf[here, HI]
        ya = p[mine, YA] + self.yb[0, here, LO] + (yr[2, here, :] + yr[5, here, :])
        yz = p[mine, YB] + self.yb[0, here, HI] + (yr[3, here, :] + yr[4, here, :])
        return jnp.concatenate([za, zz, ya, yz], axis=1)


def gather_sems():
    return [pltpu.SemaphoreType.DMA((17,)), pltpu.SemaphoreType.DMA((17,))]


class Gather:
    def __init__(self, ring, whole, sems, own):
        self.ring, self.whole, self.own = ring, whole, own
        self.s = Sends(*sems)

    def _go(self, i, rows, cols, device):
        ref = self.whole.at[rows, cols]
        self.s.go(i, ref, ref, device)

    def _got(self, i, rows, cols, device):
        self.s.got(i, self.whole.at[rows, cols], device)

    def start(self):
        g, own = self.ring, self.own
        mine = g.rows(0, False, own)
        self._go(0, mine, YY, g.right)
        self._go(1, mine, YY, g.left)
        self._go(2, mine, ZZ, g.flip)
        self._go(3, mine, ZZ, g.right)
        self._go(4, mine, ZZ, g.left)
        self._go(5, mine, YY, g.flip)

    def middle(self):
        g, own = self.ring, self.own
        lf, rt = g.rows(3, False, own), g.rows(1, False, own)
        lo, ro = g.rows(3, True, own), g.rows(1, True, own)
        far, faro, other = g.rows(2, False, own), g.rows(2, True, own), g.rows(0, True, own)
        self._got(0, lf, YY, g.left)
        self._go(6, lf, YB, g.right)
        self._go(7, lf, YY, g.flip)
        self._got(1, rt, YY, g.right)
        self._go(8, rt, YA, g.left)
        self._go(9, rt, YY, g.flip)
        self._got(2, other, ZZ, g.flip)
        self._go(10, other, ZZ, g.right)
        self._go(11, other, ZZ, g.left)
        self._got(6, far, YB, g.left)
        self._got(8, far, YA, g.right)
        self._go(12, far, YY, g.flip)
        self._got(3, lf, ZZ, g.left)
        self._go(13, lf, ZB, g.right)
        self._got(4, rt, ZZ, g.right)
        self._go(14, rt, ZA, g.left)
        self._got(10, lo, ZZ, g.left)
        self._go(15, lo, ZB, g.right)
        self._got(11, ro, ZZ, g.right)
        self._go(16, ro, ZA, g.left)

    def finish(self):
        g, own = self.ring, self.own
        far, faro, other = g.rows(2, False, own), g.rows(2, True, own), g.rows(0, True, own)
        self._got(5, other, YY, g.flip)
        self._got(7, g.rows(3, True, own), YY, g.flip)
        self._got(9, g.rows(1, True, own), YY, g.flip)
        self._got(12, faro, YY, g.flip)
        self._got(13, far, ZB, g.left)
        self._got(14, far, ZA, g.right)
        self._got(15, faro, ZB, g.left)
        self._got(16, faro, ZA, g.right)


class DpScatter:
    ORDER = (2, 1, 3, 0)

    def __init__(self, ring, scratch, compute):
        d, t = ring.d, ring.t
        self.c, self.x, self.y = lax.rem(d, 2), lax.rem(d // 2, 4), d // 8
        self.pair = (d + 1 - 2 * self.c, t)
        self.right = ((self.y * 4 + self.step(1)) * 2 + self.c, t)
        self.left = ((self.y * 4 + self.step(3)) * 2 + self.c, t)
        self.far = (((1 - self.y) * 4 + self.x) * 2 + self.c, t)
        self.csend, self.crecv, self.xr, self.yr, ssem, rsem = scratch
        self.s = Sends(ssem, rsem)
        self.compute = compute

    def step(self, k):
        return lax.rem(self.x + k, 4)

    def devices(self):
        return [self.pair, self.right, self.left, self.far]

    def cols(self, k, side, core):
        return pl.ds(pl.multiple_of(((side * 4 + self.step(k)) * 2 + core) * 128, 128), 128)

    def cores(self):
        sent = []
        for n, k in enumerate(self.ORDER):
            slot = 2 * (n % 2)
            if n >= 2:
                for c in sent[2 * n - 4:2 * n - 2]:
                    c.wait_send()

            def put(rows, both):
                self.csend[slot, rows, :] = both[:, :128]
                self.csend[slot + 1, rows, :] = both[:, 128:]

            self.compute(self.cols(k, 0, 1 - self.c), self.cols(k, 1, 1 - self.c), put)
            for side in range(2):
                c = self.s.make(2 * k + side, self.csend.at[slot + side], self.crecv.at[2 * k + side], self.pair)
                c.start()
                sent.append(c)
        self.s.made += sent[4:]

    def along(self):
        s, acc, xr = self.s, self.crecv, self.xr
        for k in self.ORDER:
            for side in range(2):
                s.got(2 * k + side, acc.at[2 * k + side], self.pair)

            def put(rows, both):
                acc[2 * k, rows, :] = acc[2 * k, rows, :] + both[:, :128]
                acc[2 * k + 1, rows, :] = acc[2 * k + 1, rows, :] + both[:, 128:]

            self.compute(self.cols(k, 0, self.c), self.cols(k, 1, self.c), put)
            if k == 2:
                s.go(8, acc.at[5], xr.at[0], self.right)
                s.go(9, acc.at[4], xr.at[1], self.left)
            if k == 1:
                s.go(10, acc.at[2], xr.at[2], self.right)
            if k == 3:
                s.go(11, acc.at[7], xr.at[3], self.left)

    def second(self):
        s, acc, xr = self.s, self.crecv, self.xr
        n = acc.shape[1]
        s.got(8, xr.at[0], self.left)
        add_rows(xr.at[0], lambda r: acc[3, pl.ds(r, 16), :], n)
        s.go(12, xr.at[0], xr.at[4], self.right)
        s.got(9, xr.at[1], self.right)
        add_rows(xr.at[1], lambda r: acc[6, pl.ds(r, 16), :], n)
        s.go(13, xr.at[1], xr.at[5], self.left)

    def third(self):
        s, acc, xr = self.s, self.crecv, self.xr
        n = acc.shape[1]
        s.got(10, xr.at[2], self.left)
        s.got(13, xr.at[5], self.right)
        add_rows(acc.at[0], lambda r: xr[2, pl.ds(r, 16), :] + xr[5, pl.ds(r, 16), :], n)
        s.got(11, xr.at[3], self.right)
        s.got(12, xr.at[4], self.left)
        add_rows(acc.at[1], lambda r: xr[3, pl.ds(r, 16), :] + xr[4, pl.ds(r, 16), :], n)
        s.go(14, acc.at[1 - self.y], self.yr, self.far)

    def finish(self, out_ref):
        self.s.got(14, self.yr, self.far)
        n = self.yr.shape[0]

        def one(i, _):
            r = pl.ds(pl.multiple_of(i * 16, 16), 16)
            out_ref[r, :] = self.crecv[self.y, r, :] + self.yr[r, :]
            return 0

        lax.fori_loop(0, n // 16, one, 0)
        self.s.drain()


def dp_scratch(n):
    return [pltpu.VMEM((4, n, 128), F32), pltpu.VMEM((8, n, 128), F32), pltpu.VMEM((6, n, 128), F32), pltpu.VMEM((n, 128), F32),
            pltpu.SemaphoreType.DMA((15,)), pltpu.SemaphoreType.DMA((15,))]


def params(cid, mib):
    return pltpu.CompilerParams(collective_id=cid, has_side_effects=True, vmem_limit_bytes=mib * 2 ** 20)


def attn_kernel(low_ref, w_ref, x_ref, gain_ref, hid_ref, resid_ref, part, whole, xown, csem, *rest):
    scr, gsem = rest[:7], rest[7:]
    ring = Ring()
    own = resid_ref.shape[0]
    mine = ring.rows(0, False, own)
    fetch = pltpu.make_async_copy(x_ref.at[mine], xown, csem)
    fetch.start()

    def partial(n, _):
        cols = pl.ds(pl.multiple_of(n * 256, 256), 256)
        part[:, cols] = mm1(low_ref[...], w_ref[:, cols], NN)
        return 0

    lax.fori_loop(0, part.shape[1] // 256, partial, 0)
    greet([ring.right, ring.left, ring.flip])
    sc = Scatter(ring, part, scr, own)
    sc.start()
    fetch.wait()
    sc.middle()
    sc.finish()

    def finish(i, _):
        r = pl.multiple_of(i * 16, 16)
        resid = xown[pl.ds(r, 16), :].astype(F32) + sc.value(r)
        resid_ref[pl.ds(r, 16), :] = resid
        n = resid * lax.rsqrt(jnp.mean(resid * resid, axis=-1, keepdims=True) + 1e-05)
        whole[pl.ds(pl.multiple_of(mine.start + r, 16), 16), :] = (n * gain_ref[0:1, :]).astype(BF16).astype(F32)
        return 0

    lax.fori_loop(0, own // 16, finish, 0)
    ga = Gather(ring, whole, gsem, own)
    ga.start()
    ga.middle()
    ga.finish()

    def cast(i, _):
        r = pl.ds(pl.multiple_of(i * 32, 32), 32)
        hid_ref[r, :] = whole[r, :].astype(BF16)
        return 0

    lax.fori_loop(0, whole.shape[0] // 32, cast, 0)
    sc.s.drain()
    ga.s.drain()


VM = pl.BlockSpec(memory_space=pltpu.VMEM)
ANY = pl.BlockSpec(memory_space=pl.ANY)


def attn_exchange(low, w_out, inputs, gain):
    T, D = inputs.shape
    own = T // NT_
    sd = jax.ShapeDtypeStruct
    return pl.pallas_call(
        attn_kernel,
        out_shape=(sd((T, D), BF16), sd((own, D), F32)),
        in_specs=[VM, VM, ANY, VM], out_specs=[VM, VM],
        scratch_shapes=[pltpu.VMEM((T, D), F32), pltpu.VMEM((T, D), F32), pltpu.VMEM((own, D), BF16),
                        pltpu.SemaphoreType.DMA(())] + scatter_scratch(own) + gather_sems(),
        compiler_params=params(1, 56),
        name="attn_exchange",
    )(low, w_out, inputs, gain)


def mid_kernel(gg_ref, gu_ref, inner_ref, wg_ref, wu_ref, hid_ref, og_ref, resid_in, gain_ref,
               whole, gres_ref, dgain_ref, grads_ref,
               part, shard, left, csem, *rest):
    scr, gsem, dscr = rest[:7], rest[7:9], rest[9:]
    ring = Ring()
    own = gres_ref.shape[0]
    n = gg_ref.shape[1]
    mine = ring.rows(0, False, own)

    def partial(i, _):
        cols = pl.ds(pl.multiple_of(i * 256, 256), 256)
        part[:, cols] = mm1(gg_ref[...], wg_ref[:, cols], NN) + mm1(gu_ref[...], wu_ref[:, cols], NN)
        return 0

    lax.fori_loop(0, part.shape[1] // 256, partial, 0)

    def compute(a, b, put):
        hid = jnp.concatenate([hid_ref[:, a], hid_ref[:, b]], axis=1)
        put(slice(0, n), mm1(left[0:n, :], hid, NN))
        put(slice(n, 2 * n), mm1(left[n:2 * n, :], hid, NN))
        put(slice(2 * n, 3 * n), mm1(left[2 * n:, :], jnp.concatenate([og_ref[:, a], og_ref[:, b]], axis=1), NN))

    dp = DpScatter(ring, dscr, compute)
    greet([ring.right, ring.left, ring.flip] + dp.devices())
    sc = Scatter(ring, part, scr, own)
    sc.start()
    left[0:n, :] = gg_ref[...].T
    left[n:2 * n, :] = gu_ref[...].T
    left[2 * n:, :] = inner_ref[...].T
    dp.cores()
    sc.middle()
    dp.along()
    sc.finish()
    dgain_ref[...] = jnp.zeros_like(dgain_ref)

    def finish(i, _):
        r = pl.multiple_of(i * 16, 16)
        resid = resid_in[pl.ds(r, 16), :]
        back = sc.value(r)
        scale = lax.rsqrt(jnp.mean(resid * resid, axis=-1, keepdims=True) + 1e-05)
        nn = resid * scale
        bn = back * nn
        dgain_ref[...] = dgain_ref[...] + bn[0:8] + bn[8:16]
        b = back * gain_ref[0:1, :]
        g = og_ref[pl.ds(pl.multiple_of(mine.start + r, 16), 16), :].astype(F32) + scale * (b - nn * jnp.mean(b * nn, axis=-1, keepdims=True))
        gres_ref[pl.ds(r, 16), :] = g
        shard[pl.ds(r, 16), :] = g.astype(BF16).astype(F32)
        return 0

    lax.fori_loop(0, own // 16, finish, 0)
    place = pltpu.make_async_copy(shard, whole.at[mine], csem)
    place.start()
    place.wait()
    ga = Gather(ring, whole, gsem, own)
    ga.start()
    dp.second()
    ga.middle()
    dp.third()
    ga.finish()
    dp.finish(grads_ref)
    sc.s.drain()
    ga.s.drain()


def mid_exchange(gg, gu, inner, wg, wu, hid, og, resid, gain):
    T, D = og.shape
    own = T // NT_
    n = 3 * gg.shape[1]
    sd = jax.ShapeDtypeStruct
    return pl.pallas_call(
        mid_kernel,
        out_shape=(sd((T, D), F32), sd((own, D), F32), sd((8, D), F32), sd((n, 128), F32)),
        in_specs=[VM] * 9, out_specs=[ANY, VM, VM, VM],
        scratch_shapes=[pltpu.VMEM((T, D), F32), pltpu.VMEM((own, D), F32), pltpu.VMEM((n, T), BF16),
                        pltpu.SemaphoreType.DMA(())] + scatter_scratch(own) + gather_sems() + dp_scratch(n),
        compiler_params=params(2, 60),
        name="mid_exchange",
    )(gg, gu, inner, wg, wu, hid, og, resid, gain)


SMALL = 40
TAPS = 40


def in_kernel(gq, gk, gv, gt, gba, low_ref, wq, wk, wv, wt, wba, hid_ref, ga_ref, gres_ref, x_ref, gain_ref, gains_ref, taps_ref,
              whole, grads_ref, gains_out, taps_out,
              part, shard, left, xown, g_own, g_recv, s_own, s_recv, csem, ssem, srsem, *rest):
    scr, gsem, dscr = rest[:7], rest[7:9], rest[9:]
    ring = Ring()
    own = gres_ref.shape[0]
    mine = ring.rows(0, False, own)
    fetch = pltpu.make_async_copy(x_ref.at[mine], xown, csem)
    fetch.start()

    def partial(i, _):
        rows_w = pl.ds(pl.multiple_of(i * 256, 256), 256)
        total = mm1(gq[...], wq[rows_w, :], NT) + mm1(gk[...], wk[rows_w, :], NT)
        total = total + mm1(gv[...], wv[rows_w, :], NT) + mm1(gt[...], wt[rows_w, :], NT)
        part[:, rows_w] = total + mm1(gba[...], wba[rows_w, :], NT)
        return 0

    lax.fori_loop(0, part.shape[1] // 256, partial, 0)

    def compute(a, b, put):
        hid = jnp.concatenate([hid_ref[:, a], hid_ref[:, b]], axis=1)
        put(slice(0, 768), mm1(left[0:768, :], hid, NN))
        put(slice(768, 1552), mm1(left[768:1552, :], hid, NN))
        put(slice(1552, 2064), mm1(left[1552:, :], jnp.concatenate([ga_ref[:, a], ga_ref[:, b]], axis=1), NN))

    dp = DpScatter(ring, dscr, compute)
    t_peers = [(ring.d, lax.rem(ring.t + j, NT_)) for j in range(1, NT_)]
    d_peers = [(lax.rem(ring.d + j, 16), ring.t) for j in range(1, 16)]
    greet(t_peers + d_peers)
    sc = Scatter(ring, part, scr, own)
    sc.start()
    left[0:256, :] = gq[...].T
    left[256:512, :] = gk[...].T
    left[512:1024, :] = gv[...].T
    left[1024:1536, :] = gt[...].T
    left[1536:1552, :] = gba[...].T[0:16]
    left[1552:, :] = low_ref[...].T
    dp.cores()
    sc.middle()
    dp.along()
    fetch.wait()
    sc.finish()
    g_own[...] = gains_ref[...]

    def finish(i, total):
        r = pl.multiple_of(i * 16, 16)
        x = xown[pl.ds(r, 16), :].astype(F32)
        back = sc.value(r)
        scale = lax.rsqrt(jnp.mean(x * x, axis=-1, keepdims=True) + 1e-05)
        nn = x * scale
        total = total + jnp.sum(back * nn, axis=0, keepdims=True)
        b = back * gain_ref[0:1, :]
        g = gres_ref[pl.ds(r, 16), :] + scale * (b - nn * jnp.mean(b * nn, axis=-1, keepdims=True))
        shard[pl.ds(r, 16), :] = g.astype(BF16).astype(F32)
        return total

    total = lax.fori_loop(0, own // 16, finish, jnp.zeros((1, x_ref.shape[1]), F32))
    for j in range(16):
        g_own[j:j + 1, :] = total[:, j * 128:(j + 1) * 128]
    place = pltpu.make_async_copy(shard, whole.at[mine], csem)
    place.start()
    place.wait()
    small = Sends(ssem, srsem)
    for j, dev in enumerate(t_peers):
        small.go(j, g_own, g_recv.at[j], dev)
    ga = Gather(ring, whole, gsem, own)
    ga.start()
    dp.second()
    for j, dev in enumerate(t_peers):
        small.got(j, g_recv.at[j], dev)
    gains = g_own[...]
    for j in range(NT_ - 1):
        gains = gains + g_recv[j]
    s_own[0:SMALL, :] = gains
    s_own[SMALL:, :] = taps_ref[...]
    for j, dev in enumerate(d_peers):
        small.go(7 + j, s_own, s_recv.at[j], dev)
    ga.middle()
    dp.third()
    for j, dev in enumerate(d_peers):
        small.got(7 + j, s_recv.at[j], dev)
    both = s_own[...]
    for j in range(15):
        both = both + s_recv[j]
    gains_out[...] = both[:SMALL]
    taps_out[...] = both[SMALL:]
    ga.finish()
    dp.finish(grads_ref)
    small.drain()
    sc.s.drain()
    ga.s.drain()


def in_exchange(grads, low, weights, hid, ga, gres, inputs, gain, gains, taps):
    T, D = inputs.shape
    own = T // NT_
    n = 2064
    sd = jax.ShapeDtypeStruct
    vm = lambda *s: pltpu.VMEM(s, F32)
    return pl.pallas_call(
        in_kernel,
        out_shape=(sd((T, D), F32), sd((n, 128), F32), sd((SMALL, 128), F32), sd((TAPS, 128), F32)),
        in_specs=[VM] * 14 + [ANY] + [VM] * 3, out_specs=[ANY, VM, VM, VM],
        scratch_shapes=[vm(T, D), vm(own, D), pltpu.VMEM((n, T), BF16), pltpu.VMEM((own, D), BF16),
                        vm(SMALL, 128), vm(7, SMALL, 128), vm(SMALL + TAPS, 128), vm(15, SMALL + TAPS, 128),
                        pltpu.SemaphoreType.DMA(()), pltpu.SemaphoreType.DMA((22,)), pltpu.SemaphoreType.DMA((22,))]
        + scatter_scratch(own) + gather_sems() + dp_scratch(n),
        compiler_params=params(3, 60),
        name="in_exchange",
    )(*grads, low, *weights, hid, ga, gres, inputs, gain, gains, taps)


def out_kernel(part, resid_in, whole, shard, csem, *rest):
    scr, gsem = rest[:7], rest[7:]
    ring = Ring()
    own = resid_in.shape[0]
    mine = ring.rows(0, False, own)
    greet([ring.right, ring.left, ring.flip])
    sc = Scatter(ring, part, scr, own)
    sc.start()
    sc.middle()
    sc.finish()

    def finish(i, _):
        r = pl.multiple_of(i * 16, 16)
        shard[pl.ds(r, 16), :] = (resid_in[pl.ds(r, 16), :] + sc.value(r)).astype(BF16).astype(F32)
        return 0

    lax.fori_loop(0, own // 16, finish, 0)
    place = pltpu.make_async_copy(shard, whole.at[mine], csem)
    place.start()
    place.wait()
    ga = Gather(ring, whole, gsem, own)
    ga.start()
    ga.middle()
    ga.finish()
    sc.s.drain()
    ga.s.drain()


def out_exchange(part, resid):
    T, D = part.shape
    own = T // NT_
    return pl.pallas_call(
        out_kernel,
        out_shape=jax.ShapeDtypeStruct((T, D), F32),
        in_specs=[VM, VM], out_specs=ANY,
        scratch_shapes=[pltpu.VMEM((own, D), F32), pltpu.SemaphoreType.DMA(())] + scatter_scratch(own) + gather_sems(),
        compiler_params=params(4, 56),
        name="out_exchange",
    )(part, resid)


def matmul(left, right):
    return jnp.dot(left, right, preferred_element_type=F32)


def rows8(v):
    return jnp.broadcast_to(v[None, :], (8, v.shape[0]))


def per_device(inputs, segments, attn_gain, w_query, w_key, w_value, w_gate, w_beta, w_alpha, conv_query, conv_key, conv_value,
               decay_log, decay_bias, head_gain, w_out, ffn_gain, w_up_gate, w_up, w_down, out_grad):
    T, D = inputs.shape
    blocks = T // L
    tokens_in = inputs.astype(F32)
    scale_in = lax.rsqrt(jnp.mean(tokens_in * tokens_in, axis=-1, keepdims=True) + 1e-05)
    hidden_in = (tokens_in * scale_in * attn_gain).astype(BF16)
    w_ba = jnp.concatenate([w_beta, w_alpha, jnp.zeros((D, 124), BF16)], axis=1)
    qp, kp, vp, gp = (matmul(hidden_in, w) for w in (w_query, w_key, w_value, w_gate))
    ba = matmul(hidden_in, w_ba)
    rate = jnp.zeros((8, 128), F32).at[:, 2:4].set(-jnp.exp(decay_log))
    bias = jnp.zeros((8, 128), F32).at[:, 2:4].set(decay_bias)
    seg = segments.astype(F32).reshape(blocks, 1, L)
    prev = jnp.concatenate([seg[:1, :, :1], seg[:-1, :, L - 1:]], axis=0)
    seg3 = jnp.concatenate([seg, jnp.broadcast_to(prev, seg.shape), jnp.zeros((blocks, 6, L), F32)], axis=1)
    gain8 = rows8(head_gain)
    low, q, k, x, u, s, o = mixer_fwd(seg3, qp, kp, vp, gp, ba, conv_query, conv_key, conv_value, rate, bias, gain8)
    hidden_mid, resid = attn_exchange(low, w_out, inputs, rows8(ffn_gain))
    gate_pre = matmul(hidden_mid, w_up_gate)
    up_pre = matmul(hidden_mid, w_up)
    sig = jax.nn.sigmoid(gate_pre)
    act = gate_pre * sig
    inner = (act * up_pre).astype(BF16)
    ffn = matmul(inner, w_down)
    grad_inner = matmul(out_grad, w_down.T)
    gg = (grad_inner * up_pre * sig * (1.0 + gate_pre * (1.0 - sig))).astype(BF16)
    gu = (grad_inner * act).astype(BF16)
    grad_attn, grad_resid, ffn_gain_part, grads_mid = mid_exchange(
        gg, gu, inner, w_up_gate.T, w_up.T, hidden_mid, out_grad, resid, rows8(ffn_gain))
    grad_attn = grad_attn.astype(BF16)
    outputs = out_exchange(ffn, resid).astype(BF16)
    grad_mixed = matmul(grad_attn, w_out.T)
    gq, gk, gv, gt, gba, taps, small, hgain = mixer_bwd(
        seg3, grad_mixed, qp, kp, vp, gp, ba, conv_query, conv_key, conv_value, rate, bias, gain8, q, k, x, u, s, o)
    gains_in = jnp.concatenate([jnp.zeros((16, 128), F32), jnp.sum(ffn_gain_part, axis=0).reshape(16, 128), hgain[0].reshape(2, 128),
                                jnp.zeros((SMALL - 34, 128), F32)], axis=0)
    taps_in = jnp.concatenate([taps[:4].reshape(32, 128), small], axis=0)
    ig, grads_in, gains, taps_sum = in_exchange(
        (gq, gk, gv, gt, gba), low, (w_query, w_key, w_value, w_gate, w_ba), hidden_in, grad_attn, grad_resid, inputs,
        rows8(attn_gain), gains_in, taps_in)
    input_grad = ig.astype(BF16)
    n = w_up.shape[1]
    ct = taps_sum[:32].reshape(4, 1024)
    return (outputs, input_grad, gains[:16].reshape(D), grads_in[0:256].T, grads_in[256:512].T, grads_in[512:1024].T, grads_in[1024:1536].T,
            grads_in[1536:1538].T, grads_in[1538:1540].T, ct[:, 0:256], ct[:, 256:512], ct[:, 512:],
            taps_sum[33, 2:4], taps_sum[32, 2:4], gains[32:34].reshape(256), grads_in[1552:], gains[16:32].reshape(D),
            grads_mid[0:n].T, grads_mid[n:2 * n].T, grads_mid[2 * n:])


def solution(mesh):
    col, row, rep = P(None, "tensor"), P("tensor", None), P()
    tok, both, head = P("dp", None), P("dp", "tensor"), P("tensor")
    return jax.shard_map(
        per_device,
        mesh=mesh,
        in_specs=(tok, tok, rep, col, col, col, col, col, col, col, col, col, head, head, rep, row, rep, col, col, row, tok),
        out_specs=(tok, tok, rep, both, both, both, both, both, both, col, col, col, head, head, rep, P("tensor", "dp"), rep, both, both, P("tensor", "dp")),
        check_vma=False,
    )
```

```python
import functools
import jax, jax.numpy as jnp
from jax import lax
from jax.experimental import pallas as pl
from jax.experimental.pallas import tpu as pltpu
from jax.sharding import PartitionSpec as P

F32 = jnp.float32
BF16 = jnp.bfloat16
L = 128
PAD = 8
NN = (((1,), (0,)), ((), ()))
NT = (((1,), (1,)), ((), ()))
TN = (((0,), (0,)), ((), ()))


def split(x):
    hi = x.astype(BF16)
    return hi, (x - hi.astype(F32)).astype(BF16)


def mm1(a, b, dims):
    return lax.dot_general(a, b, dims, preferred_element_type=F32)


def mm3(a, b, dims=NN):
    return mm1(a[0], b[0], dims) + (mm1(a[0], b[1], dims) + mm1(a[1], b[0], dims))


def sigmoid(x):
    return 1.0 / (1.0 + jnp.exp(-x))


def rows(ref, b, n=L, lead=0):
    return ref[pl.ds(pl.multiple_of(b * L, L) + lead, n)]


def decay_tile(ba, rate, bias):
    lane = lax.broadcasted_iota(jnp.int32, ba.shape, 1)
    shifted = ba + bias
    soft = jnp.maximum(shifted, 0.0) + jnp.log1p(jnp.exp(-jnp.abs(shifted)))
    return jnp.where(lane < 2, sigmoid(ba), rate * soft)


def tri_sum(tile, dims):
    r = lax.broadcasted_iota(jnp.int32, (L, L), 0)
    c = lax.broadcasted_iota(jnp.int32, (L, L), 1)
    tri = (r >= c).astype(BF16)
    p0 = tile.astype(BF16)
    rest = tile - p0.astype(F32)
    p1 = rest.astype(BF16)
    p2 = (rest - p1.astype(F32)).astype(BF16)
    return mm1(tri, p0, dims) + (mm1(tri, p1, dims) + mm1(tri, p2, dims))


def block_decay(b, seg_ref, ba_ref, rate, bias):
    tile = decay_tile(rows(ba_ref, b), rate, bias)
    cum = tri_sum(tile, NN)
    lane = lax.broadcasted_iota(jnp.int32, (L, L), 1)
    both = jnp.where(lane < 2, tile, cum)
    flat = both.T
    seg_row = seg_ref[b, 0:1, :]
    seg_col = jnp.broadcast_to(seg_row, (L, L)).T
    prev = seg_ref[b, 1:2, 0:1]
    r = lax.broadcasted_iota(jnp.int32, (L, L), 0)
    keep = (seg_col == seg_row) & (r >= lane)
    strict_keep = r > lane
    carry_keep = seg_col[:, 0:1] == prev
    out = []
    for h in range(2):
        c_col = cum[:, 2 + h:3 + h]
        c_row = flat[2 + h:3 + h, :]
        beta_row = flat[h:h + 1, :]
        decay = jnp.where(keep, jnp.exp(jnp.where(keep, c_col - c_row, 0.0)), 0.0)
        carry = jnp.where(carry_keep, jnp.exp(c_col), 0.0)
        last_keep = seg_col[:, 0:1] == seg_row[:, L - 1:L]
        last_decay = jnp.where(last_keep, jnp.exp(jnp.where(last_keep, c_col[L - 1:L, :] - c_col, 0.0)), 0.0)
        beta_col = tile[:, h:h + 1]
        out.append((decay, carry, beta_row, beta_col, last_decay))
    return out, strict_keep, (tile, seg_col)


def conv_block(b, pre_ref, taps_ref, seg_ref, cols, segpad_ref):
    base = pl.multiple_of(b * L, L)
    z = pre_ref[pl.ds(base, L + PAD), cols]
    s = segpad_ref[pl.ds(base, L + PAD), 0:1]
    total = z[PAD:] * taps_ref[0:1, cols]
    for k in range(1, 4):
        same = (s[PAD - k:PAD - k + L] == s[PAD:]).astype(F32)
        total = total + z[PAD - k:PAD - k + L] * same * taps_ref[k:k + 1, cols]
    return total


def inverse_many(mats):
    r = lax.broadcasted_iota(jnp.int32, (L, L), 0)
    c = lax.broadcasted_iota(jnp.int32, (L, L), 1)
    eye = (r == c).astype(F32)
    xs = [eye - jnp.where((r // 2 == c // 2), a, 0.0) for a in mats]
    s = 2
    while s < L:
        pick = (r // (2 * s) == c // (2 * s)) & (r // s != c // s)
        sx = [split(x) for x in xs]
        sa = [split(jnp.where(pick, a, 0.0)) for a in mats]
        t = [mm3(x, a) for x, a in zip(sx, sa)]
        xs = [x - mm3(split(y), z) for x, y, z in zip(xs, t, sx)]
        s *= 2
    return xs


def fwd_kernel(blocks, group, seg_ref, qp_ref, kp_ref, vp_ref, gp_ref, ba_ref, cq_ref, ck_ref, cv_ref, rate_ref, bias_ref, gain_ref,
               low_ref, q_ref, k_ref, x_ref, u_ref, s_ref, o_ref,
               qpad, kpad, vpad, segpad, w_s, u0_s, kw_s):
    T = blocks * L
    rate, bias = rate_ref[0:1, :], bias_ref[0:1, :]
    for pad, src in ((qpad, qp_ref), (kpad, kp_ref), (vpad, vp_ref)):
        pad[0:PAD, :] = jnp.zeros((PAD, pad.shape[1]), F32)
        pad[PAD:PAD + T, :] = src[...]
    segpad[0:PAD, :] = jnp.full((PAD, L), -1.0, F32)
    for b in range(blocks):
        segpad[PAD + b * L:PAD + (b + 1) * L, :] = jnp.broadcast_to(seg_ref[b, 0:1, :], (L, L)).T

    def phase_a(g, _):
        a_mats, keepers = [], []
        for i in range(group):
            b = g * group + i
            base = pl.multiple_of(b * L, L)
            per_head, strict_keep, _u = block_decay(b, seg_ref, ba_ref, rate, bias)
            for h in range(2):
                decay, carry, beta_row, beta_col, last_decay = per_head[h]
                kc = slice(h * 128, h * 128 + 128)
                vc = slice(h * 256, h * 256 + 256)
                y = conv_block(b, qpad, cq_ref, seg_ref, kc, segpad)
                q = y * sigmoid(y)
                q = q * (lax.rsqrt(jnp.sum(q * q, axis=-1, keepdims=True) + 1e-06) * (128 ** -0.5))
                y = conv_block(b, kpad, ck_ref, seg_ref, kc, segpad)
                k = y * sigmoid(y)
                k = k * lax.rsqrt(jnp.sum(k * k, axis=-1, keepdims=True) + 1e-06)
                q_ref[pl.ds(base, L), kc] = q
                k_ref[pl.ds(base, L), kc] = k
                y = conv_block(b, vpad, cv_ref, seg_ref, vc, segpad)
                v = y * sigmoid(y)
                ks = split(k)
                kk = mm3(ks, ks, NT)
                a_mats.append(jnp.where(strict_keep, decay, 0.0) * kk * beta_row)
                kw_s[pl.ds(base, L), kc] = k * (last_decay * beta_col)
                keepers.append((b, base, h, kc, vc, v, k * carry))
        xs = inverse_many(a_mats)
        for x, (b, base, h, kc, vc, v, gk) in zip(xs, keepers):
            x_ref[pl.ds(base, L), kc] = x
            sx = split(x)
            u0_s[pl.ds(base, L), vc] = mm3(sx, split(v))
            w_s[pl.ds(base, L), kc] = mm3(sx, split(gk))
        return 0

    lax.fori_loop(0, blocks // group, phase_a, 0)

    def phase_b(b, state):
        base = pl.multiple_of(b * L, L)
        per_head, strict_keep, _u = block_decay(b, seg_ref, ba_ref, rate, bias)
        new = []
        for h in range(2):
            decay, carry, beta_row, beta_col, last_decay = per_head[h]
            kc = slice(h * 128, h * 128 + 128)
            vc = slice(h * 256, h * 256 + 256)
            s = state[h]
            s_ref[pl.ds(base, L), vc] = s
            ss = split(s)
            u = u0_s[pl.ds(base, L), vc] - mm3(split(w_s[pl.ds(base, L), kc]), ss)
            u_ref[pl.ds(base, L), vc] = u
            new.append(carry[L - 1:L, :] * s + mm3(split(kw_s[pl.ds(base, L), kc]), split(u), TN))
        return tuple(new)

    zero = jnp.zeros((128, 256), F32)
    lax.fori_loop(0, blocks, phase_b, (zero, zero))

    def phase_c(b, _):
        base = pl.multiple_of(b * L, L)
        per_head, strict_keep, _u = block_decay(b, seg_ref, ba_ref, rate, bias)
        for h in range(2):
            decay, carry, beta_row, beta_col, last_decay = per_head[h]
            kc = slice(h * 128, h * 128 + 128)
            vc = slice(h * 256, h * 256 + 256)
            q = q_ref[pl.ds(base, L), kc]
            qk = mm3(split(q), split(k_ref[pl.ds(base, L), kc]), NT)
            p = decay * qk * beta_row
            o = mm3(split(q * carry), split(s_ref[pl.ds(base, L), vc])) + mm3(split(p), split(u_ref[pl.ds(base, L), vc]))
            o_ref[pl.ds(base, L), vc] = o
            gp = gp_ref[pl.ds(base, L), vc]
            n = o * lax.rsqrt(jnp.mean(o * o, axis=-1, keepdims=True) + 1e-05)
            low_ref[pl.ds(base, L), vc] = (n * gain_ref[0:1, :] * (gp * sigmoid(gp))).astype(BF16)
        return 0

    lax.fori_loop(0, blocks, phase_c, 0)


VM = pl.BlockSpec(memory_space=pltpu.VMEM)


def mixer_fwd(seg3, qp, kp, vp, gp, ba, cq, ck, cv, rate, bias, gain, group=2):
    T = qp.shape[0]
    blocks = T // L
    sd = jax.ShapeDtypeStruct
    return pl.pallas_call(
        functools.partial(fwd_kernel, blocks, group),
        out_shape=(sd((T, 512), BF16), sd((T, 256), F32), sd((T, 256), F32), sd((T, 256), F32), sd((T, 512), F32),
                   sd((T, 512), F32), sd((T, 512), F32)),
        in_specs=[VM] * 12, out_specs=[VM] * 7,
        scratch_shapes=[pltpu.VMEM((T + PAD, 256), F32), pltpu.VMEM((T + PAD, 256), F32), pltpu.VMEM((T + PAD, 512), F32),
                        pltpu.VMEM((T + PAD, L), F32), pltpu.VMEM((T, 256), F32), pltpu.VMEM((T, 512), F32), pltpu.VMEM((T, 256), F32)],
        compiler_params=pltpu.CompilerParams(vmem_limit_bytes=56 * 2 ** 20),
        name="mixer_forward",
    )(seg3, qp, kp, vp, gp, ba, cq, ck, cv, rate, bias, gain)


MESH = pl.DeviceIdType.MESH
NT_ = 8
ZH, YH = 512, 512


def run(steps, count=None):
    if count is None:
        for _ in steps:
            pass
    else:
        for _ in range(count):
            next(steps)


class Ring:
    def __init__(self):
        self.d = lax.axis_index("dp")
        self.t = lax.axis_index("tensor")
        self.y = lax.rem(self.t, 2)
        self.z = self.t // 2
        self.right = (self.d, self.at(1) * 2 + self.y)
        self.left = (self.d, self.at(3) * 2 + self.y)
        self.flip = (self.d, self.z * 2 + 1 - self.y)

    def at(self, k):
        return lax.rem(self.z + k, 4)

    def rows(self, k, other, own):
        side = 1 - self.y if other else self.y
        return pl.ds(pl.multiple_of((self.at(k) * 2 + side) * own, own), own)

    def quarter(self, k, own):
        return pl.ds(pl.multiple_of(self.at(k) * 2 * own, 2 * own), 2 * own)


class Sends:
    def __init__(self, ssem, rsem):
        self.ssem, self.rsem, self.made = ssem, rsem, []

    def make(self, i, src, dst, device):
        return pltpu.make_async_remote_copy(src_ref=src, dst_ref=dst, send_sem=self.ssem.at[i], recv_sem=self.rsem.at[i],
                                            device_id=device, device_id_type=MESH)

    def go(self, i, src, dst, device):
        c = self.make(i, src, dst, device)
        c.start()
        self.made.append(c)

    def got(self, i, dst, device):
        self.make(i, dst, dst, device).wait_recv()

    def drain(self):
        for c in self.made:
            c.wait_send()


def greet(devices):
    barrier = pltpu.get_barrier_semaphore()
    for dev in devices:
        pl.semaphore_signal(barrier, inc=1, device_id=dev, device_id_type=MESH)
    pl.semaphore_wait(barrier, len(devices))


ZA, ZB, ZZ = pl.ds(0, ZH), pl.ds(ZH, ZH), pl.ds(0, 2 * ZH)
YA, YB, YY = pl.ds(2 * ZH, YH), pl.ds(2 * ZH + YH, YH), pl.ds(2 * ZH, 2 * YH)
GZH, GYH = 640, 384
GZA, GZB, GZZ = pl.ds(0, GZH), pl.ds(GZH, GZH), pl.ds(0, 2 * GZH)
GYA, GYB, GYY = pl.ds(2 * GZH, GYH), pl.ds(2 * GZH + GYH, GYH), pl.ds(2 * GZH, 2 * GYH)
ZLO, ZHI, YLO, YHI = pl.ds(0, ZH), pl.ds(ZH, ZH), pl.ds(0, YH), pl.ds(YH, YH)


def scatter_scratch(own):
    return [pltpu.VMEM((4, own, 2 * YH), F32), pltpu.VMEM((6, 2 * own, ZH), F32), pltpu.VMEM((6, own, YH), F32),
            pltpu.VMEM((own, 2 * ZH), F32), pltpu.VMEM((own, 2 * ZH), F32),
            pltpu.SemaphoreType.DMA((17,)), pltpu.SemaphoreType.DMA((17,))]


def add_rows(dst, src_of, n):
    def one(i, _):
        r = pl.multiple_of(i * 16, 16)
        dst[pl.ds(r, 16), :] = dst[pl.ds(r, 16), :] + src_of(r)
        return 0
    lax.fori_loop(0, n // 16, one, 0)


def sub(ref, rows, cols):
    return lambda r: ref[pl.ds(pl.multiple_of(rows.start + r, 16), 16), cols]


class Scatter:
    def __init__(self, ring, part, scratch, own):
        self.ring, self.part, self.own = ring, part, own
        self.yb, self.zb, self.yr, self.zsend, self.zf, ssem, rsem = scratch
        self.s = Sends(ssem, rsem)

    ORDER = (2, 1, 3, 0)

    def start(self, k):
        g, s, p, own = self.ring, self.s, self.part, self.own
        if k == 2:
            s.go(0, p.at[g.quarter(2, own), ZB], self.zb.at[0], g.right)
            s.go(1, p.at[g.quarter(2, own), ZA], self.zb.at[1], g.left)
        if k == 1:
            s.go(2, p.at[g.quarter(1, own), ZA], self.zb.at[2], g.right)
        if k == 3:
            s.go(3, p.at[g.quarter(3, own), ZB], self.zb.at[3], g.left)
        s.go({2: 6, 1: 7, 3: 8, 0: 9}[k], p.at[g.rows(k, True, own), YY], self.yb.at[k], g.flip)

    def middle(self):
        g, s, p, own = self.ring, self.s, self.part, self.own
        yb, zb, yr = self.yb, self.zb, self.yr
        s.got(6, yb.at[2], g.flip)
        add_rows(yb.at[2], sub(p, g.rows(2, False, own), YY), own)
        s.go(10, yb.at[2, :, YHI], yr.at[0], g.right)
        s.go(11, yb.at[2, :, YLO], yr.at[1], g.left)
        yield
        s.got(0, zb.at[0], g.left)
        add_rows(zb.at[0], sub(p, g.quarter(1, own), ZB), 2 * own)
        s.go(4, zb.at[0], zb.at[4], g.right)
        s.got(1, zb.at[1], g.right)
        add_rows(zb.at[1], sub(p, g.quarter(3, own), ZA), 2 * own)
        s.go(5, zb.at[1], zb.at[5], g.left)
        yield
        s.got(7, yb.at[1], g.flip)
        add_rows(yb.at[1], sub(p, g.rows(1, False, own), YY), own)
        s.go(12, yb.at[1, :, YLO], yr.at[2], g.right)
        s.got(10, yr.at[0], g.left)
        add_rows(yr.at[0], lambda r: yb[1, pl.ds(r, 16), YHI], own)
        s.go(14, yr.at[0], yr.at[4], g.right)
        yield
        s.got(8, yb.at[3], g.flip)
        add_rows(yb.at[3], sub(p, g.rows(3, False, own), YY), own)
        s.go(13, yb.at[3, :, YHI], yr.at[3], g.left)
        s.got(11, yr.at[1], g.right)
        add_rows(yr.at[1], lambda r: yb[3, pl.ds(r, 16), YLO], own)
        s.go(15, yr.at[1], yr.at[5], g.left)
        yield
        s.got(2, zb.at[2], g.left)
        s.got(3, zb.at[3], g.right)
        s.got(4, zb.at[4], g.left)
        s.got(5, zb.at[5], g.right)
        base = g.rows(0, True, own).start
        lead = (1 - g.y) * own

        def one(i, _):
            r = pl.multiple_of(i * 16, 16)
            at = pl.ds(pl.multiple_of(lead + r, 16), 16)
            mine = pl.ds(pl.multiple_of(base + r, 16), 16)
            self.zsend[pl.ds(r, 16), ZLO] = p[mine, ZA] + (zb[2, at, :] + zb[5, at, :])
            self.zsend[pl.ds(r, 16), ZHI] = p[mine, ZB] + (zb[3, at, :] + zb[4, at, :])
            return 0

        lax.fori_loop(0, own // 16, one, 0)
        s.go(16, self.zsend, self.zf, g.flip)
        yield

    def finish(self):
        g, s = self.ring, self.s
        s.got(9, self.yb.at[0], g.flip)
        s.got(12, self.yr.at[2], g.left)
        s.got(13, self.yr.at[3], g.right)
        s.got(14, self.yr.at[4], g.left)
        s.got(15, self.yr.at[5], g.right)
        s.got(16, self.zf, g.flip)

    def value(self, r):
        g, p, own = self.ring, self.part, self.own
        zb, yr = self.zb, self.yr
        at = pl.ds(pl.multiple_of(g.y * own + r, 16), 16)
        here = pl.ds(r, 16)
        mine = pl.ds(pl.multiple_of(g.rows(0, False, own).start + r, 16), 16)
        za = p[mine, ZA] + (zb[2, at, :] + zb[5, at, :]) + self.zf[here, ZLO]
        zz = p[mine, ZB] + (zb[3, at, :] + zb[4, at, :]) + self.zf[here, ZHI]
        ya = p[mine, YA] + self.yb[0, here, YLO] + (yr[2, here, :] + yr[5, here, :])
        yz = p[mine, YB] + self.yb[0, here, YHI] + (yr[3, here, :] + yr[4, here, :])
        return jnp.concatenate([za, zz, ya, yz], axis=1)


def gather_sems():
    return [pltpu.SemaphoreType.DMA((17,)), pltpu.SemaphoreType.DMA((17,))]


class Gather:
    def __init__(self, ring, whole, sems, own):
        self.ring, self.whole, self.own = ring, whole, own
        self.s = Sends(*sems)

    def _go(self, i, rows, cols, device):
        ref = self.whole.at[rows, cols]
        self.s.go(i, ref, ref, device)

    def _got(self, i, rows, cols, device):
        self.s.got(i, self.whole.at[rows, cols], device)

    def start(self):
        g, own = self.ring, self.own
        mine = g.rows(0, False, own)
        self._go(0, mine, GYY, g.right)
        self._go(1, mine, GYY, g.left)
        self._go(2, mine, GZZ, g.flip)
        self._go(3, mine, GZZ, g.right)
        self._go(4, mine, GZZ, g.left)
        self._go(5, mine, GYY, g.flip)

    def middle(self):
        g, own = self.ring, self.own
        lf, rt = g.rows(3, False, own), g.rows(1, False, own)
        lo, ro = g.rows(3, True, own), g.rows(1, True, own)
        far, faro, other = g.rows(2, False, own), g.rows(2, True, own), g.rows(0, True, own)
        self._got(0, lf, GYY, g.left)
        self._go(6, lf, GYB, g.right)
        self._go(7, lf, GYY, g.flip)
        self._got(1, rt, GYY, g.right)
        self._go(8, rt, GYA, g.left)
        self._go(9, rt, GYY, g.flip)
        self._got(2, other, GZZ, g.flip)
        self._go(10, other, GZZ, g.right)
        self._go(11, other, GZZ, g.left)
        yield
        self._got(6, far, GYB, g.left)
        self._got(8, far, GYA, g.right)
        self._go(12, far, GYY, g.flip)
        yield
        self._got(3, lf, GZZ, g.left)
        self._go(13, lf, GZB, g.right)
        self._got(4, rt, GZZ, g.right)
        self._go(14, rt, GZA, g.left)
        yield
        self._got(10, lo, GZZ, g.left)
        self._go(15, lo, GZB, g.right)
        self._got(11, ro, GZZ, g.right)
        self._go(16, ro, GZA, g.left)
        yield

    def finish(self):
        g, own = self.ring, self.own
        far, faro, other = g.rows(2, False, own), g.rows(2, True, own), g.rows(0, True, own)
        self._got(5, other, GYY, g.flip)
        self._got(7, g.rows(3, True, own), GYY, g.flip)
        self._got(9, g.rows(1, True, own), GYY, g.flip)
        self._got(12, faro, GYY, g.flip)
        self._got(13, far, GZB, g.left)
        self._got(14, far, GZA, g.right)
        self._got(15, faro, GZB, g.left)
        self._got(16, faro, GZA, g.right)


class DpScatter:
    ORDER = (2, 1, 3, 0)

    def __init__(self, ring, scratch, compute):
        d, t = ring.d, ring.t
        self.c, self.x, self.y = lax.rem(d, 2), lax.rem(d // 2, 4), d // 8
        self.pair = (d + 1 - 2 * self.c, t)
        self.right = ((self.y * 4 + self.step(1)) * 2 + self.c, t)
        self.left = ((self.y * 4 + self.step(3)) * 2 + self.c, t)
        self.far = (((1 - self.y) * 4 + self.x) * 2 + self.c, t)
        self.csend, self.crecv, self.xr, self.yr, ssem, rsem = scratch
        self.s = Sends(ssem, rsem)
        self.compute = compute

    def step(self, k):
        return lax.rem(self.x + k, 4)

    def devices(self):
        return [self.pair, self.right, self.left, self.far]

    def cols(self, k, side, core):
        return pl.ds(pl.multiple_of(((side * 4 + self.step(k)) * 2 + core) * 128, 128), 128)

    def cores(self):
        slots, sent = self.csend.shape[0], []
        for n, k in enumerate(self.ORDER):
            slot = 2 * n % slots
            for c in sent[:2] if 2 * n >= slots else []:
                c.wait_send()
            sent = sent[2:] if 2 * n >= slots else sent

            def put(rows, both):
                self.csend[slot, rows, :] = both[:, :128]
                self.csend[slot + 1, rows, :] = both[:, 128:]

            self.compute(self.cols(k, 0, 1 - self.c), self.cols(k, 1, 1 - self.c), put)
            for side in range(2):
                c = self.s.make(2 * k + side, self.csend.at[slot + side], self.crecv.at[2 * k + side], self.pair)
                c.start()
                sent.append(c)
            yield
        self.s.made += sent

    def along(self):
        s, acc, xr = self.s, self.crecv, self.xr
        for k in self.ORDER:
            for side in range(2):
                s.got(2 * k + side, acc.at[2 * k + side], self.pair)

            def put(rows, both):
                acc[2 * k, rows, :] = acc[2 * k, rows, :] + both[:, :128]
                acc[2 * k + 1, rows, :] = acc[2 * k + 1, rows, :] + both[:, 128:]

            self.compute(self.cols(k, 0, self.c), self.cols(k, 1, self.c), put)
            if k == 2:
                s.go(8, acc.at[5], xr.at[0], self.right)
                s.go(9, acc.at[4], xr.at[1], self.left)
            if k == 1:
                s.go(10, acc.at[2], xr.at[2], self.right)
            if k == 3:
                s.go(11, acc.at[7], xr.at[3], self.left)
            yield

    def second(self):
        s, acc, xr = self.s, self.crecv, self.xr
        n = acc.shape[1]
        s.got(8, xr.at[0], self.left)
        add_rows(xr.at[0], lambda r: acc[3, pl.ds(r, 16), :], n)
        s.go(12, xr.at[0], xr.at[4], self.right)
        s.got(9, xr.at[1], self.right)
        add_rows(xr.at[1], lambda r: acc[6, pl.ds(r, 16), :], n)
        s.go(13, xr.at[1], xr.at[5], self.left)

    def third(self):
        s, acc, xr = self.s, self.crecv, self.xr
        n = acc.shape[1]
        s.got(10, xr.at[2], self.left)
        s.got(13, xr.at[5], self.right)
        add_rows(acc.at[0], lambda r: xr[2, pl.ds(r, 16), :] + xr[5, pl.ds(r, 16), :], n)
        s.got(11, xr.at[3], self.right)
        s.got(12, xr.at[4], self.left)
        add_rows(acc.at[1], lambda r: xr[3, pl.ds(r, 16), :] + xr[4, pl.ds(r, 16), :], n)
        s.go(14, acc.at[1 - self.y], self.yr, self.far)

    def finish(self, out_ref):
        self.s.got(14, self.yr, self.far)
        n = self.yr.shape[0]

        def one(i, _):
            r = pl.ds(pl.multiple_of(i * 16, 16), 16)
            out_ref[r, :] = self.crecv[self.y, r, :] + self.yr[r, :]
            return 0

        lax.fori_loop(0, n // 16, one, 0)
        self.s.drain()


def together(sc, dp):
    steps, cores, along = sc.middle(), dp.cores(), dp.along()
    run(cores, 2)
    run(steps, 2)
    run(along, 1)
    run(cores)
    run(steps, 1)
    run(along, 2)
    run(steps, 1)
    run(along)
    run(steps)


def dp_scratch(n, slots=8):
    return [pltpu.VMEM((slots, n, 128), F32), pltpu.VMEM((8, n, 128), F32), pltpu.VMEM((6, n, 128), F32), pltpu.VMEM((n, 128), F32),
            pltpu.SemaphoreType.DMA((15,)), pltpu.SemaphoreType.DMA((15,))]


def params(cid, mib):
    return pltpu.CompilerParams(collective_id=cid, has_side_effects=True, vmem_limit_bytes=mib * 2 ** 20)


VM = pl.BlockSpec(memory_space=pltpu.VMEM)
ANY = pl.BlockSpec(memory_space=pl.ANY)


def bwd_kernel(blocks, seg_ref, ga_ref, wout_ref, low_ref, ffn_ref, resid_ref, qp_ref, kp_ref, vp_ref, gp_ref, ba_ref, cq_ref, ck_ref, cv_ref, rate_ref, bias_ref, gain_ref,
               q_ref, k_ref, x_ref, u_ref, s_ref, o_ref,
               dqp_ref, dkp_ref, dvp_ref, dgp_ref, dba_ref, dtap_ref, dsmall_ref, dgain_ref, oshard_ref, grads_ref,
               qpad, kpad, vpad, segpad, gm_ref, do_s, y_s, z_s, ds_s, dq_s, dk_s, left, *rest):
    T = blocks * L
    scr, dscr = rest[:7], rest[7:]
    own = resid_ref.shape[0]
    ring = Ring()

    def compute(a, b, put):
        put(slice(0, 512), mm1(left[...], jnp.concatenate([ga_ref[:, a], ga_ref[:, b]], axis=1), NN))

    dp = DpScatter(ring, dscr, compute)
    greet([ring.right, ring.left, ring.flip] + dp.devices())
    sc = Scatter(ring, ffn_ref, scr, own)
    for k in sc.ORDER:
        sc.start(k)
    left[...] = low_ref[...].T
    steps, cores, along = sc.middle(), dp.cores(), dp.along()
    run(cores)

    def mixed_back(i, _):
        r = pl.ds(pl.multiple_of(i * 256, 256), 256)
        gm_ref[r, :] = mm1(ga_ref[r, :], wout_ref[...], NT)
        return 0

    lax.fori_loop(0, T // 256, mixed_back, 0)
    run(along)
    run(steps, 1)
    rate, bias = rate_ref[0:1, :], bias_ref[0:1, :]
    for pad, src in ((qpad, qp_ref), (kpad, kp_ref), (vpad, vp_ref)):
        pad[0:PAD, :] = jnp.zeros((PAD, pad.shape[1]), F32)
        pad[PAD:PAD + T, :] = src[...]
    segpad[0:PAD, :] = jnp.full((PAD, L), -1.0, F32)
    segpad[PAD + T:, :] = jnp.full((PAD, L), -1.0, F32)
    for b in range(blocks):
        segpad[PAD + b * L:PAD + (b + 1) * L, :] = jnp.broadcast_to(seg_ref[b, 0:1, :], (L, L)).T
    dgain_ref[...] = jnp.zeros_like(dgain_ref)
    dsmall_ref[...] = jnp.zeros_like(dsmall_ref)
    dtap_ref[...] = jnp.zeros_like(dtap_ref)

    def phase_1(b, _):
        base = pl.multiple_of(b * L, L)
        per_head, strict_keep, _u = block_decay(b, seg_ref, ba_ref, rate, bias)
        for h in range(2):
            decay, carry, beta_row, beta_col, last_decay = per_head[h]
            kc = slice(h * 128, h * 128 + 128)
            vc = slice(h * 256, h * 256 + 256)
            o = o_ref[pl.ds(base, L), vc]
            gp = gp_ref[pl.ds(base, L), vc]
            gm = gm_ref[pl.ds(base, L), vc]
            gain = gain_ref[0:1, :]
            sg = sigmoid(gp)
            r = lax.rsqrt(jnp.mean(o * o, axis=-1, keepdims=True) + 1e-05)
            n = o * r
            act = gp * sg
            gn = gm * n
            dgain_ref[0:1, :] = dgain_ref[0:1, :] + jnp.sum(gn * act, axis=0, keepdims=True)
            dgp_ref[pl.ds(base, L), vc] = (gn * gain * (sg * (1.0 + gp * (1.0 - sg)))).astype(BF16)
            dn = gm * gain * act
            do = r * (dn - n * jnp.mean(dn * n, axis=-1, keepdims=True))
            do_s[pl.ds(base, L), vc] = do
            q, k = q_ref[pl.ds(base, L), kc], k_ref[pl.ds(base, L), kc]
            p = decay * mm3(split(q), split(k), NT) * beta_row
            sdo = split(do)
            sx = split(x_ref[pl.ds(base, L), kc])
            y0 = mm3(sx, split(mm3(split(p), sdo, TN)), TN)
            z = mm3(sx, split(k * (last_decay * beta_col)), TN)
            y_s[pl.ds(base, L), vc] = y0
            z_s[pl.ds(base, L), kc] = z
            ds_s[pl.ds(base, L), vc] = mm3(split(q * carry), sdo, TN)
        return 0

    lax.fori_loop(0, blocks // 2, phase_1, 0)
    run(steps, 1)
    lax.fori_loop(blocks // 2, blocks, phase_1, 0)
    run(steps, 1)
    dp.second()

    def phase_2(i, grads):
        b = blocks - 1 - i
        base = pl.multiple_of(b * L, L)
        per_head, strict_keep, _u = block_decay(b, seg_ref, ba_ref, rate, bias)
        new = []
        for h in range(2):
            decay, carry, beta_row, beta_col, last_decay = per_head[h]
            kc = slice(h * 128, h * 128 + 128)
            vc = slice(h * 256, h * 256 + 256)
            ds = grads[h]
            kept = ds_s[pl.ds(base, L), vc]
            ds_s[pl.ds(base, L), vc] = ds
            y = y_s[pl.ds(base, L), vc] + mm3(split(z_s[pl.ds(base, L), kc]), split(ds))
            y_s[pl.ds(base, L), vc] = y
            new.append(carry[L - 1:L, :] * ds + kept
                       - mm3(split(k_ref[pl.ds(base, L), kc] * carry), split(y), TN))
        return tuple(new)

    zero = jnp.zeros((128, 256), F32)
    lax.fori_loop(0, blocks, phase_2, (zero, zero))
    run(steps)
    dp.third()

    def phase_3(b, _):
        base = pl.multiple_of(b * L, L)
        per_head, strict_keep, (tile, seg_col) = block_decay(b, seg_ref, ba_ref, rate, bias)
        lane = lax.broadcasted_iota(jnp.int32, (L, L), 1)
        rowi = lax.broadcasted_iota(jnp.int32, (L, L), 0)
        row_tile = jnp.zeros((L, L), F32)
        col_tile = jnp.zeros((L, L), F32)
        for h in range(2):
            decay, carry, beta_row, beta_col, last_decay = per_head[h]
            kc = slice(h * 128, h * 128 + 128)
            vc = slice(h * 256, h * 256 + 256)
            q, k = q_ref[pl.ds(base, L), kc], k_ref[pl.ds(base, L), kc]
            sq, sk = split(q), split(k)
            kk = mm3(sk, sk, NT)
            qk = mm3(sq, sk, NT)
            s, u = s_ref[pl.ds(base, L), vc], u_ref[pl.ds(base, L), vc]
            do, y, ds = do_s[pl.ds(base, L), vc], y_s[pl.ds(base, L), vc], ds_s[pl.ds(base, L), vc]
            ss, su, sdo, sy, sds = split(s), split(u), split(do), split(y), split(ds)
            do_st = mm3(sdo, ss, NT)
            y_st = mm3(sy, ss, NT)
            u_dst = mm3(su, sds, NT)
            dp = mm3(sdo, su, NT)
            da = -mm3(sy, su, NT)
            dcarry = jnp.sum(q * do_st - k * y_st, axis=-1, keepdims=True)
            dcarry_last = jnp.sum(jnp.sum(ds * s, axis=0, keepdims=True), axis=1, keepdims=True)
            dw = jnp.sum(u_dst * k, axis=-1, keepdims=True)
            dpd = dp * decay
            dad = jnp.where(strict_keep, da * decay, 0.0)
            dqk = dpd * beta_row
            dkk = dad * beta_row
            prod = dpd * qk + dad * kk
            dbeta_row = jnp.sum(prod, axis=0, keepdims=True)
            dec_grad = prod * beta_row
            dc_col = jnp.sum(dec_grad, axis=1, keepdims=True) + dcarry * carry
            dc_row = -jnp.sum(dec_grad, axis=0, keepdims=True)
            dlast = dw * beta_col * last_decay
            row1 = rowi[:, 0:1]
            dc_col = dc_col - dlast
            dc_col = dc_col + jnp.where(row1 == L - 1, jnp.sum(dlast, axis=0, keepdims=True) + dcarry_last * carry, 0.0)
            dbeta_col = dw * last_decay
            row_tile = row_tile + jnp.where(rowi == h, dbeta_row, 0.0) + jnp.where(rowi == 2 + h, dc_row, 0.0)
            col_tile = col_tile + jnp.where(lane == h, dbeta_col, 0.0) + jnp.where(lane == 2 + h, dc_col, 0.0)
            sdqk, sdkk = split(dqk), split(dkk + dkk.T)
            dq_s[pl.ds(base, L), kc] = carry * do_st + mm3(sdqk, sk)
            dk_s[pl.ds(base, L), kc] = (mm3(sdqk, sq, TN) + mm3(sdkk, sk) - carry * y_st
                                        + (last_decay * beta_col) * u_dst)
        grad = col_tile + row_tile.T
        dld = tri_sum(grad, TN)
        ba = rows(ba_ref, b)
        sig_alpha = sigmoid(ba + bias)
        dalpha = dld * rate * sig_alpha
        dpre = jnp.where(lane < 2, grad * tile * (1.0 - tile), jnp.where(lane < 4, dalpha, 0.0))
        dba_ref[pl.ds(base, L), :] = dpre.astype(BF16)
        dsmall_ref[0:1, :] = dsmall_ref[0:1, :] + jnp.sum(dpre, axis=0, keepdims=True)
        dsmall_ref[1:2, :] = dsmall_ref[1:2, :] + jnp.sum(dld * tile, axis=0, keepdims=True)
        return 0

    lax.fori_loop(0, blocks, phase_3, 0)
    sc.finish()

    def finish(i, _):
        r = pl.ds(pl.multiple_of(i * 16, 16), 16)
        oshard_ref[r, :] = (resid_ref[r, :] + sc.value(pl.multiple_of(i * 16, 16))).astype(BF16).astype(F32)
        return 0

    lax.fori_loop(0, own // 16, finish, 0)
    dp.finish(grads_ref)
    sc.s.drain()

    def conv_back(pre, taps_ref, src, out_ref, cols, tap_cols, scale):
        do_s[T:, cols] = jnp.zeros((PAD, 128), F32)

        def one(b, tap_grads):
            base = pl.multiple_of(b * L, L)
            y = conv_block(b, pre, taps_ref, None, cols, segpad)
            sg = sigmoid(y)
            act = y * sg
            d = src[pl.ds(base, L), cols]
            if scale is not None:
                r = lax.rsqrt(jnp.sum(act * act, axis=-1, keepdims=True) + 1e-06)
                d = (scale * r) * (d - act * (r * r * jnp.sum(d * act, axis=-1, keepdims=True)))
            dy = d * (sg * (1.0 + y * (1.0 - sg)))
            do_s[pl.ds(base, L), cols] = dy
            z = pre[pl.ds(base, L + PAD), cols]
            s = segpad[pl.ds(base, L + PAD), 0:1]
            new = [tap_grads[0] + jnp.sum(dy * z[PAD:], axis=0, keepdims=True)]
            for t in range(1, 4):
                same = (s[PAD - t:PAD - t + L] == s[PAD:]).astype(F32)
                new.append(tap_grads[t] + jnp.sum(dy * (z[PAD - t:PAD - t + L] * same), axis=0, keepdims=True))
            return tuple(new)

        zero = jnp.zeros((1, 128), F32)
        res = lax.fori_loop(0, blocks, one, (zero,) * 4)
        for t in range(4):
            dtap_ref[t:t + 1, tap_cols] = res[t]

        def two(b, _):
            base = pl.multiple_of(b * L, L)
            dy = do_s[pl.ds(base, L + PAD), cols]
            s = segpad[pl.ds(base + PAD, L + PAD), 0:1]
            total = dy[:L] * taps_ref[0:1, cols]
            for t in range(1, 4):
                same = (s[t:t + L] == s[:L]).astype(F32)
                total = total + dy[t:t + L] * same * taps_ref[t:t + 1, cols]
            out_ref[pl.ds(base, L), cols] = total.astype(BF16)
            return 0

        lax.fori_loop(0, blocks, two, 0)

    for h in range(2):
        c = slice(h * 128, h * 128 + 128)
        conv_back(qpad, cq_ref, dq_s, dqp_ref, c, slice(h * 128, h * 128 + 128), 128 ** -0.5)
        conv_back(kpad, ck_ref, dk_s, dkp_ref, c, slice(256 + h * 128, 256 + h * 128 + 128), 1.0)
    for j in range(4):
        c = slice(j * 128, j * 128 + 128)
        conv_back(vpad, cv_ref, y_s, dvp_ref, c, slice(512 + j * 128, 512 + j * 128 + 128), None)


def mixer_bwd(seg3, ga, wout, low, ffn, resid, qp, kp, vp, gp, ba, cq, ck, cv, rate, bias, gain, q, k, x, u, s, o):
    T = qp.shape[0]
    blocks = T // L
    own, D = resid.shape
    n = low.shape[1]
    sd = jax.ShapeDtypeStruct
    vm = lambda r, w: pltpu.VMEM((r, w), F32)
    return pl.pallas_call(
        functools.partial(bwd_kernel, blocks),
        out_shape=(sd((T, 256), BF16), sd((T, 256), BF16), sd((T, 512), BF16), sd((T, 512), BF16), sd((T, 128), BF16),
                   sd((8, 1024), F32), sd((8, 128), F32), sd((8, 256), F32), sd((own, D), F32), sd((n, 128), F32)),
        in_specs=[VM] * 23, out_specs=[VM] * 10,
        scratch_shapes=[vm(T + PAD, 256), vm(T + PAD, 256), vm(T + PAD, 512), vm(T + 2 * PAD, L), vm(T, 512),
                        vm(T + PAD, 512), vm(T, 512), vm(T, 256), vm(T, 512), vm(T, 256), vm(T, 256), pltpu.VMEM((n, T), BF16)]
        + scatter_scratch(own) + dp_scratch(n),
        compiler_params=params(4, 60),
        name="mixer_backward",
    )(seg3, ga, wout, low, ffn, resid, qp, kp, vp, gp, ba, cq, ck, cv, rate, bias, gain, q, k, x, u, s, o)


def attn_kernel(low_ref, w_ref, x_ref, gain_ref, hid_ref, resid_ref, part, whole, xown, csem, *rest):
    scr, gsem = rest[:7], rest[7:]
    ring = Ring()
    own = resid_ref.shape[0]
    mine = ring.rows(0, False, own)
    fetch = pltpu.make_async_copy(x_ref.at[mine], xown, csem)
    fetch.start()

    greet([ring.right, ring.left, ring.flip])
    sc = Scatter(ring, part, scr, own)
    for k in sc.ORDER:
        quarter = ring.quarter(k, own)

        def partial(n, _):
            cols = pl.ds(pl.multiple_of(n * 512, 512), 512)
            part[quarter, cols] = mm1(low_ref[quarter, :], w_ref[:, cols], NN)
            return 0

        lax.fori_loop(0, part.shape[1] // 512, partial, 0)
        sc.start(k)
    fetch.wait()
    run(sc.middle())
    sc.finish()

    def finish(i, _):
        r = pl.multiple_of(i * 16, 16)
        resid = xown[pl.ds(r, 16), :].astype(F32) + sc.value(r)
        resid_ref[pl.ds(r, 16), :] = resid
        n = resid * lax.rsqrt(jnp.mean(resid * resid, axis=-1, keepdims=True) + 1e-05)
        whole[pl.ds(pl.multiple_of(mine.start + r, 16), 16), :] = (n * gain_ref[0:1, :]).astype(BF16).astype(F32)
        return 0

    lax.fori_loop(0, own // 16, finish, 0)
    ga = Gather(ring, whole, gsem, own)
    ga.start()
    run(ga.middle())
    ga.finish()

    def cast(i, _):
        r = pl.ds(pl.multiple_of(i * 32, 32), 32)
        hid_ref[r, :] = whole[r, :].astype(BF16)
        return 0

    lax.fori_loop(0, whole.shape[0] // 32, cast, 0)
    sc.s.drain()
    ga.s.drain()


def attn_exchange(low, w_out, inputs, gain):
    T, D = inputs.shape
    own = T // NT_
    sd = jax.ShapeDtypeStruct
    return pl.pallas_call(
        attn_kernel,
        out_shape=(sd((T, D), BF16), sd((own, D), F32)),
        in_specs=[VM, VM, ANY, VM], out_specs=[VM, VM],
        scratch_shapes=[pltpu.VMEM((T, D), F32), pltpu.VMEM((T, D), F32), pltpu.VMEM((own, D), BF16),
                        pltpu.SemaphoreType.DMA(())] + scatter_scratch(own) + gather_sems(),
        compiler_params=params(1, 56),
        name="attn_exchange",
    )(low, w_out, inputs, gain)


def mid_kernel(wg_ref, wu_ref, wd_any, hid_ref, og_any, resid_any, gain_ref,
               ga_ref, inner_ref, ffn_any, gres_ref, dgain_ref, grads_ref,
               part, whole, left, gg_ref, gu_ref, wd_ref, og_ref, resid_in, csem, *rest):
    scr, gsem, dscr = rest[:7], rest[7:9], rest[9:]
    fetches = [pltpu.make_async_copy(src, dst, csem.at[i]) for i, (src, dst) in enumerate(
        ((wd_any, wd_ref), (og_any, og_ref), (resid_any, resid_in)))]
    for f in fetches:
        f.start()
    ring = Ring()
    own = gres_ref.shape[0]
    n = gg_ref.shape[1]
    mine = ring.rows(0, False, own)

    def compute(a, b, put):
        hid = jnp.concatenate([hid_ref[:, a], hid_ref[:, b]], axis=1)
        put(slice(0, n), mm1(left[0:n, :], hid, NN))
        put(slice(n, 2 * n), mm1(left[n:2 * n, :], hid, NN))

    dp = DpScatter(ring, dscr, compute)
    greet([ring.right, ring.left, ring.flip] + dp.devices())
    sc = Scatter(ring, part, scr, own)
    for k in sc.ORDER:
        quarter = ring.quarter(k, own)
        hid = hid_ref[quarter, :]
        gate = mm1(hid, wg_ref[...], NT)
        up = mm1(hid, wu_ref[...], NT)
        sig = sigmoid(gate)
        act = gate * sig
        inner_ref[quarter, :] = (act * up).astype(BF16)
        if k == 2:
            fetches[0].wait()
            fetches[1].wait()
        back = mm1(og_ref[quarter, :], wd_ref[...], NT)
        gg_ref[quarter, :] = (back * up * sig * (1.0 + gate * (1.0 - sig))).astype(BF16)
        gu_ref[quarter, :] = (back * act).astype(BF16)

        def partial(i, _):
            cols = pl.ds(pl.multiple_of(i * 512, 512), 512)
            part[quarter, cols] = mm1(gg_ref[quarter, :], wg_ref[:, cols], NN) + mm1(gu_ref[quarter, :], wu_ref[:, cols], NN)
            return 0

        lax.fori_loop(0, part.shape[1] // 512, partial, 0)
        sc.start(k)
    left[0:n, :] = gg_ref[...].T
    left[n:2 * n, :] = gu_ref[...].T
    together(sc, dp)
    fetches[2].wait()
    sc.finish()
    dgain_ref[...] = jnp.zeros_like(dgain_ref)

    def finish(i, _):
        r = pl.multiple_of(i * 16, 16)
        resid = resid_in[pl.ds(r, 16), :]
        back = sc.value(r)
        scale = lax.rsqrt(jnp.mean(resid * resid, axis=-1, keepdims=True) + 1e-05)
        nn = resid * scale
        bn = back * nn
        dgain_ref[...] = dgain_ref[...] + bn[0:8] + bn[8:16]
        b = back * gain_ref[0:1, :]
        g = og_ref[pl.ds(pl.multiple_of(mine.start + r, 16), 16), :].astype(F32) + scale * (b - nn * jnp.mean(b * nn, axis=-1, keepdims=True))
        gres_ref[pl.ds(r, 16), :] = g
        whole[pl.ds(pl.multiple_of(mine.start + r, 16), 16), :] = g.astype(BF16).astype(F32)
        return 0

    lax.fori_loop(0, own // 16, finish, 0)
    ga = Gather(ring, whole, gsem, own)
    ga.start()
    sc.s.drain()
    steps = ga.middle()
    run(steps, 1)
    dp.second()
    run(steps, 1)

    def down(i, _):
        cols = pl.ds(pl.multiple_of(i * 256, 256), 256)
        part[:, cols] = mm1(inner_ref[...], wd_ref[:, cols], NN)
        return 0

    lax.fori_loop(0, part.shape[1] // 256, down, 0)
    leave = pltpu.make_async_copy(part, ffn_any, csem.at[3])
    leave.start()
    run(steps)
    dp.third()
    ga.finish()

    def cast(i, _):
        r = pl.ds(pl.multiple_of(i * 32, 32), 32)
        ga_ref[r, :] = whole[r, :].astype(BF16)
        return 0

    lax.fori_loop(0, whole.shape[0] // 32, cast, 0)
    dp.finish(grads_ref)
    leave.wait()
    ga.s.drain()


def mid_exchange(wg, wu, wd, hid, og, resid, gain):
    T, D = og.shape
    own = T // NT_
    m = wg.shape[0]
    sd = jax.ShapeDtypeStruct
    return pl.pallas_call(
        mid_kernel,
        out_shape=(sd((T, D), BF16), sd((T, m), BF16), sd((T, D), F32), sd((own, D), F32), sd((8, D), F32), sd((2 * m, 128), F32)),
        in_specs=[VM, VM, ANY, VM, ANY, ANY, VM], out_specs=[VM, VM, ANY, VM, VM, VM],
        scratch_shapes=[pltpu.VMEM((T, D), F32), pltpu.VMEM((T, D), F32), pltpu.VMEM((2 * m, T), BF16),
                        pltpu.VMEM((T, m), BF16), pltpu.VMEM((T, m), BF16), pltpu.VMEM((m, D), BF16), pltpu.VMEM((T, D), BF16),
                        pltpu.VMEM((own, D), F32), pltpu.SemaphoreType.DMA((4,))]
        + scatter_scratch(own) + gather_sems() + dp_scratch(2 * m, 4),
        compiler_params=params(2, 62),
        name="mid_exchange",
    )(wg, wu, wd, hid, og, resid, gain)


SMALL = 40
TAPS = 40


def in_kernel(gq, gk, gv, gt, gba, inner_ref, wq, wk, wv, wt, wba, hid_ref, og_ref, gres_ref, x_ref, gain_ref, gains_ref, taps_ref, oshard_ref,
              whole, out_whole, grads_ref, gains_out, taps_out,
              part, shard, left, xown, g_own, g_recv, s_own, s_recv, csem, ssem, srsem, *rest):
    scr, gsem, osem, dscr = rest[:7], rest[7:9], rest[9:11], rest[11:]
    ring = Ring()
    own = gres_ref.shape[0]
    mine = ring.rows(0, False, own)
    fetch = pltpu.make_async_copy(x_ref.at[mine], xown, csem.at[0])
    fetch.start()
    place_out = pltpu.make_async_copy(oshard_ref, out_whole.at[mine], csem.at[1])
    place_out.start()
    t_peers = [(ring.d, lax.rem(ring.t + j, NT_)) for j in range(1, NT_)]
    d_peers = [(lax.rem(ring.d + j, 16), ring.t) for j in range(1, 16)]
    greet(t_peers + d_peers)
    place_out.wait()
    go = Gather(ring, out_whole, osem, own)
    go.start()

    sc = Scatter(ring, part, scr, own)
    for k in sc.ORDER:
        quarter = ring.quarter(k, own)

        def partial(i, _):
            rows_w = pl.ds(pl.multiple_of(i * 512, 512), 512)
            total = mm1(gq[quarter, :], wq[rows_w, :], NT) + mm1(gk[quarter, :], wk[rows_w, :], NT)
            total = total + mm1(gv[quarter, :], wv[rows_w, :], NT) + mm1(gt[quarter, :], wt[rows_w, :], NT)
            part[quarter, rows_w] = total + mm1(gba[quarter, :], wba[rows_w, :], NT)
            return 0

        lax.fori_loop(0, part.shape[1] // 512, partial, 0)
        sc.start(k)

    def compute(a, b, put):
        hid = jnp.concatenate([hid_ref[:, a], hid_ref[:, b]], axis=1)
        put(slice(0, 768), mm1(left[0:768, :], hid, NN))
        put(slice(768, 1552), mm1(left[768:1552, :], hid, NN))
        put(slice(1552, 2256), mm1(left[1552:, :], jnp.concatenate([og_ref[:, a], og_ref[:, b]], axis=1), NN))

    dp = DpScatter(ring, dscr, compute)
    left[0:256, :] = gq[...].T
    left[256:512, :] = gk[...].T
    left[512:1024, :] = gv[...].T
    left[1024:1536, :] = gt[...].T
    left[1536:1552, :] = gba[...].T[0:16]
    left[1552:, :] = inner_ref[...].T
    outs = go.middle()
    run(outs, 1)
    together(sc, dp)
    run(outs, 2)
    fetch.wait()
    sc.finish()
    g_own[...] = gains_ref[...]

    def finish(i, total):
        r = pl.multiple_of(i * 16, 16)
        x = xown[pl.ds(r, 16), :].astype(F32)
        back = sc.value(r)
        scale = lax.rsqrt(jnp.mean(x * x, axis=-1, keepdims=True) + 1e-05)
        nn = x * scale
        total = total + jnp.sum(back * nn, axis=0, keepdims=True)
        b = back * gain_ref[0:1, :]
        g = gres_ref[pl.ds(r, 16), :] + scale * (b - nn * jnp.mean(b * nn, axis=-1, keepdims=True))
        shard[pl.ds(r, 16), :] = g.astype(BF16).astype(F32)
        return total

    total = lax.fori_loop(0, own // 16, finish, jnp.zeros((1, x_ref.shape[1]), F32))
    for j in range(16):
        g_own[j:j + 1, :] = total[:, j * 128:(j + 1) * 128]
    place = pltpu.make_async_copy(shard, whole.at[mine], csem.at[2])
    place.start()
    place.wait()
    small = Sends(ssem, srsem)
    for j, dev in enumerate(t_peers):
        small.go(j, g_own, g_recv.at[j], dev)
    ga = Gather(ring, whole, gsem, own)
    ga.start()
    run(outs)
    dp.second()
    steps = ga.middle()
    run(steps, 1)
    for j, dev in enumerate(t_peers):
        small.got(j, g_recv.at[j], dev)
    gains = g_own[...]
    for j in range(NT_ - 1):
        gains = gains + g_recv[j]
    s_own[0:SMALL, :] = gains
    s_own[SMALL:, :] = taps_ref[...]
    for j, dev in enumerate(d_peers):
        small.go(7 + j, s_own, s_recv.at[j], dev)
    run(steps)
    dp.third()
    for j, dev in enumerate(d_peers):
        small.got(7 + j, s_recv.at[j], dev)
    both = s_own[...]
    for j in range(15):
        both = both + s_recv[j]
    gains_out[...] = both[:SMALL]
    taps_out[...] = both[SMALL:]
    go.finish()
    ga.finish()
    dp.finish(grads_ref)
    small.drain()
    go.s.drain()
    sc.s.drain()
    ga.s.drain()


def in_exchange(grads, inner, weights, hid, og, gres, inputs, gain, gains, taps, oshard):
    T, D = inputs.shape
    own = T // NT_
    n = 1552 + inner.shape[1]
    sd = jax.ShapeDtypeStruct
    vm = lambda *s: pltpu.VMEM(s, F32)
    return pl.pallas_call(
        in_kernel,
        out_shape=(sd((T, D), F32), sd((T, D), F32), sd((n, 128), F32), sd((SMALL, 128), F32), sd((TAPS, 128), F32)),
        in_specs=[VM] * 14 + [ANY] + [VM] * 4, out_specs=[ANY, ANY, VM, VM, VM],
        scratch_shapes=[vm(T, D), vm(own, D), pltpu.VMEM((n, T), BF16), pltpu.VMEM((own, D), BF16),
                        vm(SMALL, 128), vm(7, SMALL, 128), vm(SMALL + TAPS, 128), vm(15, SMALL + TAPS, 128),
                        pltpu.SemaphoreType.DMA((3,)), pltpu.SemaphoreType.DMA((22,)), pltpu.SemaphoreType.DMA((22,))]
        + scatter_scratch(own) + gather_sems() + gather_sems() + dp_scratch(n, 4),
        compiler_params=params(3, 60),
        name="in_exchange",
    )(*grads, inner, *weights, hid, og, gres, inputs, gain, gains, taps, oshard)


def matmul(left, right):
    return jnp.dot(left, right, preferred_element_type=F32)


def rows8(v):
    return jnp.broadcast_to(v[None, :], (8, v.shape[0]))


def per_device(inputs, segments, attn_gain, w_query, w_key, w_value, w_gate, w_beta, w_alpha, conv_query, conv_key, conv_value,
               decay_log, decay_bias, head_gain, w_out, ffn_gain, w_up_gate, w_up, w_down, out_grad):
    T, D = inputs.shape
    blocks = T // L
    tokens_in = inputs.astype(F32)
    scale_in = lax.rsqrt(jnp.mean(tokens_in * tokens_in, axis=-1, keepdims=True) + 1e-05)
    hidden_in = (tokens_in * scale_in * attn_gain).astype(BF16)
    w_ba = jnp.concatenate([w_beta, w_alpha, jnp.zeros((D, 124), BF16)], axis=1)
    qp, kp, vp, gp = (matmul(hidden_in, w) for w in (w_query, w_key, w_value, w_gate))
    ba = matmul(hidden_in, w_ba)
    rate = jnp.zeros((8, 128), F32).at[:, 2:4].set(-jnp.exp(decay_log))
    bias = jnp.zeros((8, 128), F32).at[:, 2:4].set(decay_bias)
    seg = segments.astype(F32).reshape(blocks, 1, L)
    prev = jnp.concatenate([seg[:1, :, :1], seg[:-1, :, L - 1:]], axis=0)
    seg3 = jnp.concatenate([seg, jnp.broadcast_to(prev, seg.shape), jnp.zeros((blocks, 6, L), F32)], axis=1)
    gain8 = rows8(head_gain)
    low, q, k, x, u, s, o = mixer_fwd(seg3, qp, kp, vp, gp, ba, conv_query, conv_key, conv_value, rate, bias, gain8)
    hidden_mid, resid = attn_exchange(low, w_out, inputs, rows8(ffn_gain))
    grad_attn, inner, ffn, grad_resid, ffn_gain_part, grads_mid = mid_exchange(
        w_up_gate.T, w_up.T, w_down, hidden_mid, out_grad, resid, rows8(ffn_gain))
    gq, gk, gv, gt, gba, taps, small, hgain, oshard, grads_out = mixer_bwd(
        seg3, grad_attn, w_out, low, ffn, resid, qp, kp, vp, gp, ba, conv_query, conv_key, conv_value, rate, bias, gain8, q, k, x, u, s, o)
    gains_in = jnp.concatenate([jnp.zeros((16, 128), F32), jnp.sum(ffn_gain_part, axis=0).reshape(16, 128), hgain[0].reshape(2, 128),
                                jnp.zeros((SMALL - 34, 128), F32)], axis=0)
    taps_in = jnp.concatenate([taps[:4].reshape(32, 128), small], axis=0)
    ig, out32, grads_in, gains, taps_sum = in_exchange(
        (gq, gk, gv, gt, gba), inner, (w_query, w_key, w_value, w_gate, w_ba), hidden_in, out_grad, grad_resid, inputs,
        rows8(attn_gain), gains_in, taps_in, oshard)
    input_grad = ig.astype(BF16)
    outputs = out32.astype(BF16)
    n = w_up.shape[1]
    ct = taps_sum[:32].reshape(4, 1024)
    return (outputs, input_grad, gains[:16].reshape(D), grads_in[0:256].T, grads_in[256:512].T, grads_in[512:1024].T, grads_in[1024:1536].T,
            grads_in[1536:1538].T, grads_in[1538:1540].T, ct[:, 0:256], ct[:, 256:512], ct[:, 512:],
            taps_sum[33, 2:4], taps_sum[32, 2:4], gains[32:34].reshape(256), grads_out, gains[16:32].reshape(D),
            grads_mid[0:n].T, grads_mid[n:2 * n].T, grads_in[1552:])


def solution(mesh):
    col, row, rep = P(None, "tensor"), P("tensor", None), P()
    tok, both, head = P("dp", None), P("dp", "tensor"), P("tensor")
    return jax.shard_map(
        per_device,
        mesh=mesh,
        in_specs=(tok, tok, rep, col, col, col, col, col, col, col, col, col, head, head, rep, row, rep, col, col, row, tok),
        out_specs=(tok, tok, rep, both, both, both, both, both, both, col, col, col, head, head, rep, P("tensor", "dp"), rep, both, both, P("tensor", "dp")),
        check_vma=False,
    )
```

```python
import functools
import jax, jax.numpy as jnp
from jax import lax
from jax.experimental import pallas as pl
from jax.experimental.pallas import tpu as pltpu
from jax.sharding import PartitionSpec as P

F32 = jnp.float32
BF16 = jnp.bfloat16
L = 128
PAD = 8
NN = (((1,), (0,)), ((), ()))
NT = (((1,), (1,)), ((), ()))
TN = (((0,), (0,)), ((), ()))


def split(x):
    hi = x.astype(BF16)
    return hi, (x - hi.astype(F32)).astype(BF16)


def mm1(a, b, dims):
    return lax.dot_general(a, b, dims, preferred_element_type=F32)


def mm3(a, b, dims=NN):
    (ia,), (ib,) = dims[0]
    if a[0].shape[ia] > 128:
        return mm1(a[0], b[0], dims) + (mm1(a[0], b[1], dims) + mm1(a[1], b[0], dims))
    return mm1(jnp.concatenate(a, axis=ia), jnp.concatenate([b[0], b[0]], axis=ib), dims) + mm1(a[0], b[1], dims)


def sigmoid(x):
    d = 1.0 + jnp.exp(-jnp.maximum(x, -80.0))
    r = pl.reciprocal(d, approx=True)
    r = r * (2.0 - d * r)
    return r * (2.0 - d * r)


def rows(ref, b, n=L, lead=0):
    return ref[pl.ds(pl.multiple_of(b * L, L) + lead, n)]


def decay_tile(ba, rate, bias):
    lane = lax.broadcasted_iota(jnp.int32, ba.shape, 1)
    shifted = ba + bias
    soft = jnp.maximum(shifted, 0.0) + jnp.log1p(jnp.exp(-jnp.abs(shifted)))
    return jnp.where(lane < 2, sigmoid(ba), rate * soft)


def tri_sum(tile, dims):
    r = lax.broadcasted_iota(jnp.int32, (L, L), 0)
    c = lax.broadcasted_iota(jnp.int32, (L, L), 1)
    tri = (r >= c).astype(BF16)
    p0 = tile.astype(BF16)
    rest = tile - p0.astype(F32)
    p1 = rest.astype(BF16)
    p2 = (rest - p1.astype(F32)).astype(BF16)
    return mm1(tri, p0, dims) + (mm1(tri, p1, dims) + mm1(tri, p2, dims))


def block_decay(b, seg_ref, ba_ref, rate, bias):
    tile = decay_tile(rows(ba_ref, b), rate, bias)
    cum = tri_sum(tile, NN)
    lane = lax.broadcasted_iota(jnp.int32, (L, L), 1)
    both = jnp.where(lane < 2, tile, cum)
    flat = both.T
    seg_row = seg_ref[b, 0:1, :]
    seg_col = jnp.broadcast_to(seg_row, (L, L)).T
    prev = seg_ref[b, 1:2, 0:1]
    r = lax.broadcasted_iota(jnp.int32, (L, L), 0)
    keep = (seg_col == seg_row) & (r >= lane)
    strict_keep = r > lane
    carry_keep = seg_col[:, 0:1] == prev
    out = []
    for h in range(2):
        c_col = cum[:, 2 + h:3 + h]
        c_row = flat[2 + h:3 + h, :]
        beta_row = flat[h:h + 1, :]
        decay = jnp.where(keep, jnp.exp(jnp.where(keep, c_col - c_row, 0.0)), 0.0)
        carry = jnp.where(carry_keep, jnp.exp(c_col), 0.0)
        last_keep = seg_col[:, 0:1] == seg_row[:, L - 1:L]
        last_decay = jnp.where(last_keep, jnp.exp(jnp.where(last_keep, c_col[L - 1:L, :] - c_col, 0.0)), 0.0)
        beta_col = tile[:, h:h + 1]
        out.append((decay, carry, beta_row, beta_col, last_decay))
    return out, strict_keep, (tile, seg_col)


MESH = pl.DeviceIdType.MESH
NT_ = 8
ZH, YH = 512, 512


def run(steps, count=None):
    if count is None:
        for _ in steps:
            pass
    else:
        for _ in range(count):
            next(steps)


class Ring:
    def __init__(self):
        self.d = lax.axis_index("dp")
        self.t = lax.axis_index("tensor")
        self.y = lax.rem(self.t, 2)
        self.z = self.t // 2
        self.right = (self.d, self.at(1) * 2 + self.y)
        self.left = (self.d, self.at(3) * 2 + self.y)
        self.flip = (self.d, self.z * 2 + 1 - self.y)

    def at(self, k):
        return lax.rem(self.z + k, 4)

    def rows(self, k, other, own):
        side = 1 - self.y if other else self.y
        return pl.ds(pl.multiple_of((self.at(k) * 2 + side) * own, own), own)

    def quarter(self, k, own):
        return pl.ds(pl.multiple_of(self.at(k) * 2 * own, 2 * own), 2 * own)


class Sends:
    def __init__(self, ssem, rsem):
        self.ssem, self.rsem, self.made = ssem, rsem, []

    def make(self, i, src, dst, device):
        return pltpu.make_async_remote_copy(src_ref=src, dst_ref=dst, send_sem=self.ssem.at[i], recv_sem=self.rsem.at[i],
                                            device_id=device, device_id_type=MESH)

    def go(self, i, src, dst, device):
        c = self.make(i, src, dst, device)
        c.start()
        self.made.append(c)

    def got(self, i, dst, device):
        self.make(i, dst, dst, device).wait_recv()

    def drain(self):
        for c in self.made:
            c.wait_send()


def greet(devices):
    barrier = pltpu.get_barrier_semaphore()
    for dev in devices:
        pl.semaphore_signal(barrier, inc=1, device_id=dev, device_id_type=MESH)
    pl.semaphore_wait(barrier, len(devices))


ZA, ZB, ZZ = pl.ds(0, ZH), pl.ds(ZH, ZH), pl.ds(0, 2 * ZH)
YA, YB, YY = pl.ds(2 * ZH, YH), pl.ds(2 * ZH + YH, YH), pl.ds(2 * ZH, 2 * YH)
GZH, GYH = 768, 256
GZA, GZB, GZZ = pl.ds(0, GZH), pl.ds(GZH, GZH), pl.ds(0, 2 * GZH)
GYA, GYB, GYY = pl.ds(2 * GZH, GYH), pl.ds(2 * GZH + GYH, GYH), pl.ds(2 * GZH, 2 * GYH)
ZLO, ZHI, YLO, YHI = pl.ds(0, ZH), pl.ds(ZH, ZH), pl.ds(0, YH), pl.ds(YH, YH)


def scatter_scratch(own):
    return [pltpu.VMEM((4, own, 2 * YH), F32), pltpu.VMEM((6, 2 * own, ZH), F32), pltpu.VMEM((6, own, YH), F32),
            pltpu.VMEM((own, 2 * ZH), F32), pltpu.VMEM((own, 2 * ZH), F32),
            pltpu.SemaphoreType.DMA((17,)), pltpu.SemaphoreType.DMA((17,))]


def add_rows(dst, src_of, n):
    def one(i, _):
        r = pl.multiple_of(i * 16, 16)
        dst[pl.ds(r, 16), :] = dst[pl.ds(r, 16), :] + src_of(r)
        return 0
    lax.fori_loop(0, n // 16, one, 0)


def sub(ref, rows, cols):
    return lambda r: ref[pl.ds(pl.multiple_of(rows.start + r, 16), 16), cols]


class Scatter:
    def __init__(self, ring, part, scratch, own, source=None):
        self.ring, self.part, self.own = ring, part, own
        self.source = part if source is None else source
        self.yb, self.zb, self.yr, self.zsend, self.zf, ssem, rsem = scratch
        self.s = Sends(ssem, rsem)

    ORDER = (2, 1, 3, 0)

    def start(self, k):
        g, s, p, own = self.ring, self.s, self.source, self.own
        if k == 2:
            s.go(0, p.at[g.quarter(2, own), ZB], self.zb.at[0], g.right)
            s.go(1, p.at[g.quarter(2, own), ZA], self.zb.at[1], g.left)
        if k == 1:
            s.go(2, p.at[g.quarter(1, own), ZA], self.zb.at[2], g.right)
        if k == 3:
            s.go(3, p.at[g.quarter(3, own), ZB], self.zb.at[3], g.left)
        s.go({2: 6, 1: 7, 3: 8, 0: 9}[k], p.at[g.rows(k, True, own), YY], self.yb.at[k], g.flip)

    def middle(self):
        g, s, p, own = self.ring, self.s, self.part, self.own
        yb, zb, yr = self.yb, self.zb, self.yr
        s.got(6, yb.at[2], g.flip)
        add_rows(yb.at[2], sub(p, g.rows(2, False, own), YY), own)
        s.go(10, yb.at[2, :, YHI], yr.at[0], g.right)
        s.go(11, yb.at[2, :, YLO], yr.at[1], g.left)
        yield
        s.got(0, zb.at[0], g.left)
        add_rows(zb.at[0], sub(p, g.quarter(1, own), ZB), 2 * own)
        s.go(4, zb.at[0], zb.at[4], g.right)
        s.got(1, zb.at[1], g.right)
        add_rows(zb.at[1], sub(p, g.quarter(3, own), ZA), 2 * own)
        s.go(5, zb.at[1], zb.at[5], g.left)
        yield
        s.got(7, yb.at[1], g.flip)
        add_rows(yb.at[1], sub(p, g.rows(1, False, own), YY), own)
        s.go(12, yb.at[1, :, YLO], yr.at[2], g.right)
        s.got(10, yr.at[0], g.left)
        add_rows(yr.at[0], lambda r: yb[1, pl.ds(r, 16), YHI], own)
        s.go(14, yr.at[0], yr.at[4], g.right)
        yield
        s.got(8, yb.at[3], g.flip)
        add_rows(yb.at[3], sub(p, g.rows(3, False, own), YY), own)
        s.go(13, yb.at[3, :, YHI], yr.at[3], g.left)
        s.got(11, yr.at[1], g.right)
        add_rows(yr.at[1], lambda r: yb[3, pl.ds(r, 16), YLO], own)
        s.go(15, yr.at[1], yr.at[5], g.left)
        yield
        s.got(2, zb.at[2], g.left)
        s.got(3, zb.at[3], g.right)
        s.got(4, zb.at[4], g.left)
        s.got(5, zb.at[5], g.right)
        base = g.rows(0, True, own).start
        lead = (1 - g.y) * own

        def one(i, _):
            r = pl.multiple_of(i * 16, 16)
            at = pl.ds(pl.multiple_of(lead + r, 16), 16)
            mine = pl.ds(pl.multiple_of(base + r, 16), 16)
            self.zsend[pl.ds(r, 16), ZLO] = p[mine, ZA] + (zb[2, at, :] + zb[5, at, :])
            self.zsend[pl.ds(r, 16), ZHI] = p[mine, ZB] + (zb[3, at, :] + zb[4, at, :])
            return 0

        lax.fori_loop(0, own // 16, one, 0)
        s.go(16, self.zsend, self.zf, g.flip)
        yield

    def finish(self):
        g, s = self.ring, self.s
        s.got(9, self.yb.at[0], g.flip)
        s.got(12, self.yr.at[2], g.left)
        s.got(13, self.yr.at[3], g.right)
        s.got(14, self.yr.at[4], g.left)
        s.got(15, self.yr.at[5], g.right)
        s.got(16, self.zf, g.flip)

    def value(self, r):
        g, p, own = self.ring, self.part, self.own
        zb, yr = self.zb, self.yr
        at = pl.ds(pl.multiple_of(g.y * own + r, 16), 16)
        here = pl.ds(r, 16)
        mine = pl.ds(pl.multiple_of(g.rows(0, False, own).start + r, 16), 16)
        za = p[mine, ZA] + (zb[2, at, :] + zb[5, at, :]) + self.zf[here, ZLO]
        zz = p[mine, ZB] + (zb[3, at, :] + zb[4, at, :]) + self.zf[here, ZHI]
        ya = p[mine, YA] + self.yb[0, here, YLO] + (yr[2, here, :] + yr[5, here, :])
        yz = p[mine, YB] + self.yb[0, here, YHI] + (yr[3, here, :] + yr[4, here, :])
        return jnp.concatenate([za, zz, ya, yz], axis=1)


def gather_sems():
    return [pltpu.SemaphoreType.DMA((17,)), pltpu.SemaphoreType.DMA((17,))]


class Gather:
    def __init__(self, ring, whole, sems, own):
        self.ring, self.whole, self.own = ring, whole, own
        self.s = Sends(*sems)

    def _go(self, i, rows, cols, device):
        ref = self.whole.at[rows, cols]
        self.s.go(i, ref, ref, device)

    def _got(self, i, rows, cols, device):
        self.s.got(i, self.whole.at[rows, cols], device)

    def start(self):
        g, own = self.ring, self.own
        mine = g.rows(0, False, own)
        self._go(0, mine, GYY, g.right)
        self._go(1, mine, GYY, g.left)
        self._go(2, mine, GZZ, g.flip)
        self._go(3, mine, GZZ, g.right)
        self._go(4, mine, GZZ, g.left)
        self._go(5, mine, GYY, g.flip)

    def middle(self):
        g, own = self.ring, self.own
        lf, rt = g.rows(3, False, own), g.rows(1, False, own)
        lo, ro = g.rows(3, True, own), g.rows(1, True, own)
        far, faro, other = g.rows(2, False, own), g.rows(2, True, own), g.rows(0, True, own)
        self._got(0, lf, GYY, g.left)
        self._go(6, lf, GYB, g.right)
        self._go(7, lf, GYY, g.flip)
        self._got(1, rt, GYY, g.right)
        self._go(8, rt, GYA, g.left)
        self._go(9, rt, GYY, g.flip)
        self._got(2, other, GZZ, g.flip)
        self._go(10, other, GZZ, g.right)
        self._go(11, other, GZZ, g.left)
        yield
        self._got(6, far, GYB, g.left)
        self._got(8, far, GYA, g.right)
        self._go(12, far, GYY, g.flip)
        yield
        self._got(3, lf, GZZ, g.left)
        self._go(13, lf, GZB, g.right)
        self._got(4, rt, GZZ, g.right)
        self._go(14, rt, GZA, g.left)
        yield
        self._got(10, lo, GZZ, g.left)
        self._go(15, lo, GZB, g.right)
        self._got(11, ro, GZZ, g.right)
        self._go(16, ro, GZA, g.left)
        yield

    def finish(self):
        g, own = self.ring, self.own
        far, faro, other = g.rows(2, False, own), g.rows(2, True, own), g.rows(0, True, own)
        self._got(5, other, GYY, g.flip)
        self._got(7, g.rows(3, True, own), GYY, g.flip)
        self._got(9, g.rows(1, True, own), GYY, g.flip)
        self._got(12, faro, GYY, g.flip)
        self._got(13, far, GZB, g.left)
        self._got(14, far, GZA, g.right)
        self._got(15, faro, GZB, g.left)
        self._got(16, faro, GZA, g.right)


class DpScatter:
    ORDER = (2, 1, 3, 0)

    def __init__(self, ring, scratch, compute):
        d, t = ring.d, ring.t
        self.c, self.x, self.y = lax.rem(d, 2), lax.rem(d // 2, 4), d // 8
        self.pair = (d + 1 - 2 * self.c, t)
        self.right = ((self.y * 4 + self.step(1)) * 2 + self.c, t)
        self.left = ((self.y * 4 + self.step(3)) * 2 + self.c, t)
        self.far = (((1 - self.y) * 4 + self.x) * 2 + self.c, t)
        self.csend, self.crecv, self.xr, self.yr, ssem, rsem = scratch
        self.s = Sends(ssem, rsem)
        self.compute = compute

    def step(self, k):
        return lax.rem(self.x + k, 4)

    def devices(self):
        return [self.pair, self.right, self.left, self.far]

    def cols(self, k, side, core):
        return pl.ds(pl.multiple_of(((side * 4 + self.step(k)) * 2 + core) * 128, 128), 128)

    def cores(self):
        slots, sent = self.csend.shape[0], []
        for n, k in enumerate(self.ORDER):
            slot = 2 * n % slots
            for c in sent[:2] if 2 * n >= slots else []:
                c.wait_send()
            sent = sent[2:] if 2 * n >= slots else sent

            def put(rows, both):
                self.csend[slot, rows, :] = both[:, :128]
                self.csend[slot + 1, rows, :] = both[:, 128:]

            self.compute(self.cols(k, 0, 1 - self.c), self.cols(k, 1, 1 - self.c), put)
            for side in range(2):
                c = self.s.make(2 * k + side, self.csend.at[slot + side], self.crecv.at[2 * k + side], self.pair)
                c.start()
                sent.append(c)
            yield
        self.s.made += sent

    def along(self):
        s, acc, xr = self.s, self.crecv, self.xr
        for k in self.ORDER:
            for side in range(2):
                s.got(2 * k + side, acc.at[2 * k + side], self.pair)

            def put(rows, both):
                acc[2 * k, rows, :] = acc[2 * k, rows, :] + both[:, :128]
                acc[2 * k + 1, rows, :] = acc[2 * k + 1, rows, :] + both[:, 128:]

            self.compute(self.cols(k, 0, self.c), self.cols(k, 1, self.c), put)
            if k == 2:
                s.go(8, acc.at[5], xr.at[0], self.right)
                s.go(9, acc.at[4], xr.at[1], self.left)
            if k == 1:
                s.go(10, acc.at[2], xr.at[2], self.right)
            if k == 3:
                s.go(11, acc.at[7], xr.at[3], self.left)
            yield

    def second(self):
        s, acc, xr = self.s, self.crecv, self.xr
        n = acc.shape[1]
        s.got(8, xr.at[0], self.left)
        add_rows(xr.at[0], lambda r: acc[3, pl.ds(r, 16), :], n)
        s.go(12, xr.at[0], xr.at[4], self.right)
        s.got(9, xr.at[1], self.right)
        add_rows(xr.at[1], lambda r: acc[6, pl.ds(r, 16), :], n)
        s.go(13, xr.at[1], xr.at[5], self.left)

    def third(self):
        s, acc, xr = self.s, self.crecv, self.xr
        n = acc.shape[1]
        s.got(10, xr.at[2], self.left)
        s.got(13, xr.at[5], self.right)
        add_rows(acc.at[0], lambda r: xr[2, pl.ds(r, 16), :] + xr[5, pl.ds(r, 16), :], n)
        s.got(11, xr.at[3], self.right)
        s.got(12, xr.at[4], self.left)
        add_rows(acc.at[1], lambda r: xr[3, pl.ds(r, 16), :] + xr[4, pl.ds(r, 16), :], n)
        s.go(14, acc.at[1 - self.y], self.yr, self.far)

    def finish(self, out_ref):
        self.s.got(14, self.yr, self.far)
        n = self.yr.shape[0]

        def one(i, _):
            r = pl.ds(pl.multiple_of(i * 16, 16), 16)
            out_ref[r, :] = self.crecv[self.y, r, :] + self.yr[r, :]
            return 0

        lax.fori_loop(0, n // 16, one, 0)
        self.s.drain()


def together(sc, dp):
    steps, cores, along = sc.middle(), dp.cores(), dp.along()
    run(cores, 2)
    run(steps, 2)
    run(along, 1)
    run(cores)
    run(steps, 1)
    run(along, 2)
    run(steps, 1)
    run(along)
    run(steps)


def dp_scratch(n, slots=8):
    return [pltpu.VMEM((slots, n, 128), F32), pltpu.VMEM((8, n, 128), F32), pltpu.VMEM((6, n, 128), F32), pltpu.VMEM((n, 128), F32),
            pltpu.SemaphoreType.DMA((15,)), pltpu.SemaphoreType.DMA((15,))]


def params(cid, mib):
    return pltpu.CompilerParams(collective_id=cid, has_side_effects=True, vmem_limit_bytes=mib * 2 ** 20)


VM = pl.BlockSpec(memory_space=pltpu.VMEM)
ANY = pl.BlockSpec(memory_space=pl.ANY)


def decay_rows(dlog_ref, dbias_ref):
    lane = lax.broadcasted_iota(jnp.int32, (1, L), 1)

    def place(ref):
        return jnp.where(lane == 2, ref[0:1, 0:1], jnp.where(lane == 3, ref[0:1, 1:2], 0.0))

    return jnp.where((lane == 2) | (lane == 3), -jnp.exp(place(dlog_ref)), 0.0), place(dbias_ref)


def doc_masks(segpad, base, n, ahead):
    s = segpad[pl.ds(base + (PAD if ahead else 0), n + PAD), :]
    if ahead:
        return [(s[k:k + n] == s[:n]).astype(F32) for k in range(1, 4)]
    return [(s[PAD - k:PAD - k + n] == s[PAD:]).astype(F32) for k in range(1, 4)]


def conv_block(base, pre_ref, taps_ref, cols, masks, n=L):
    z = pre_ref[pl.ds(base, n + PAD), cols]
    total = z[PAD:] * taps_ref[0:1, cols]
    for k in range(1, 4):
        total = total + z[PAD - k:PAD - k + n] * (masks[k - 1] * taps_ref[k:k + 1, cols])
    return total


def inverse_many(mats):
    r = lax.broadcasted_iota(jnp.int32, (L, L), 0)
    c = lax.broadcasted_iota(jnp.int32, (L, L), 1)
    eye = (r == c).astype(F32)
    xs = [eye - jnp.where((r // 2 == c // 2), a, 0.0) for a in mats]
    s = 2
    while s < L:
        pick = (r // (2 * s) == c // (2 * s)) & (r // s != c // s)
        sx = [split(x) for x in xs]
        sa = [split(jnp.where(pick, a, 0.0)) for a in mats]
        t = [mm3(x, a) for x, a in zip(sx, sa)]
        xs = [x - mm3(split(y), z) for x, y, z in zip(xs, t, sx)]
        s *= 2
    return xs


def front_kernel(blocks, group, x_ref, again_ref, wq_any, wk_any, wv_any, wt_any, wba_any, wout_any, segments_ref, cq_ref, ck_ref, cv_ref,
                 dlog_ref, dbias_ref, gain_ref, fgain_ref,
                 hidmid_ref, resid_ref, *rest):
    outs, rest = rest[:23], rest[23:]
    saved, rest = rest[:23], rest[23:]
    (hid, low_ref, qpad, kpad, vpad, segpad, gp_ref, ba_ref, q_ref, k_ref, x_s, u_ref, s_ref, o_ref,
     fq, fk, fv, pp, kkp, db, z_s, cols_s, brow) = saved
    wq, wk, wv, wt, wba, wout, w_s, u0_s, kw_s, part, whole, seg_ref, wsem, osem = rest[:14]
    scr, gsem = rest[14:21], rest[21:23]
    T = blocks * L
    own = resid_ref.shape[0]
    fetch = [pltpu.make_async_copy(src, dst, wsem.at[i]) for i, (src, dst) in enumerate(
        ((wq_any, wq), (wk_any, wk), (wv_any, wv), (wt_any, wt), (wba_any, wba), (wout_any, wout)))]
    leave = [pltpu.make_async_copy(src, dst, osem.at[i]) for i, (src, dst) in enumerate(zip(saved, outs))]
    for f in fetch:
        f.start()
    rate, bias = decay_rows(dlog_ref, dbias_ref)

    def norm(i, _):
        r = pl.ds(pl.multiple_of(i * 32, 32), 32)
        v = x_ref[r, :].astype(F32)
        n = v * lax.rsqrt(jnp.mean(v * v, axis=-1, keepdims=True) + 1e-05)
        hid[r, :] = (n * again_ref[0:1, :]).astype(BF16)
        return 0

    lax.fori_loop(0, T // 32, norm, 0)
    for pad in (qpad, kpad, vpad):
        pad[0:PAD, :] = jnp.zeros((PAD, pad.shape[1]), F32)
    segpad[0:PAD, :] = jnp.full((PAD, L), -1.0, F32)
    segpad[PAD + T:, :] = jnp.full((PAD, L), -1.0, F32)
    for b in range(blocks):
        seg_ref[b, 0:1, :] = segments_ref[0:1, b * L:(b + 1) * L].astype(F32)
        seg_ref[b, 1:2, :] = jnp.broadcast_to(segments_ref[0:1, max(b * L - 1, 0):max(b * L - 1, 0) + 1].astype(F32), (1, L))
        segpad[PAD + b * L:PAD + (b + 1) * L, :] = jnp.broadcast_to(seg_ref[b, 0:1, :], (L, L)).T
    for i, (w, dst, lead) in enumerate(((wq, qpad, PAD), (wk, kpad, PAD), (wv, vpad, PAD), (wt, gp_ref, 0), (wba, ba_ref, 0))):
        fetch[i].wait()

        def project(j, _):
            r = pl.multiple_of(j * 256, 256)
            dst[pl.ds(r + lead, 256), :] = mm1(hid[pl.ds(r, 256), :], w[...], NT if w is wba else NN)
            return 0

        lax.fori_loop(0, T // 256, project, 0)
    for i in range(8):
        if i != 1:
            leave[i].start()

    def phase_a(g, _):
        a_mats, keepers = [], []
        for i in range(group):
            b = g * group + i
            base = pl.multiple_of(b * L, L)
            here = pl.ds(base, L)
            per_head, strict_keep, _u = block_decay(b, seg_ref, ba_ref, rate, bias)
            masks = doc_masks(segpad, base, L, False)
            for h in range(2):
                decay, carry, beta_row, beta_col, last_decay = per_head[h]
                kc = slice(h * 128, h * 128 + 128)
                vc = slice(h * 256, h * 256 + 256)
                y = conv_block(base, qpad, cq_ref, kc, masks)
                sg = sigmoid(y)
                q = y * sg
                r = lax.rsqrt(jnp.sum(q * q, axis=-1, keepdims=True) + 1e-06) * (128 ** -0.5)
                q_ref[here, kc] = q * r
                fq[here, kc] = r * (sg + q * (1.0 - sg))
                y = conv_block(base, kpad, ck_ref, kc, masks)
                sg = sigmoid(y)
                k = y * sg
                r = lax.rsqrt(jnp.sum(k * k, axis=-1, keepdims=True) + 1e-06)
                fk[here, kc] = r * (sg + k * (1.0 - sg))
                k = k * r
                k_ref[here, kc] = k
                halves = []
                for j in range(2):
                    c = slice(h * 256 + j * 128, h * 256 + j * 128 + 128)
                    y = conv_block(base, vpad, cv_ref, c, masks)
                    sg = sigmoid(y)
                    v = y * sg
                    fv[here, c] = sg + v * (1.0 - sg)
                    halves.append(v)
                ks = split(k)
                kk = jnp.where(strict_keep, decay, 0.0) * mm3(ks, ks, NT)
                kkp[here, kc] = kk
                a_mats.append(kk * beta_row)
                kw_s[here, kc] = k * (last_decay * beta_col)
                keepers.append((here, kc, vc, jnp.concatenate(halves, axis=1), k * carry))
        xs = inverse_many(a_mats)
        for x, (here, kc, vc, v, gk) in zip(xs, keepers):
            x_s[here, kc] = x
            sx = split(x)
            u0_s[here, vc] = mm3(sx, split(v))
            w_s[here, kc] = mm3(sx, split(gk))
        return 0

    lax.fori_loop(0, blocks // group, phase_a, 0)

    def phase_b(b, state):
        base = pl.multiple_of(b * L, L)
        here = pl.ds(base, L)
        per_head, strict_keep, _u = block_decay(b, seg_ref, ba_ref, rate, bias)
        new = []
        for h in range(2):
            decay, carry, beta_row, beta_col, last_decay = per_head[h]
            kc = slice(h * 128, h * 128 + 128)
            vc = slice(h * 256, h * 256 + 256)
            s = state[h]
            s_ref[here, vc] = s
            u = u0_s[here, vc] - mm3(split(w_s[here, kc]), split(s))
            u_ref[here, vc] = u
            new.append(carry[L - 1:L, :] * s + mm3(split(kw_s[here, kc]), split(u), TN))
        return tuple(new)

    zero = jnp.zeros((128, 256), F32)
    lax.fori_loop(0, blocks, phase_b, (zero, zero))

    def phase_c(b, _):
        base = pl.multiple_of(b * L, L)
        here = pl.ds(base, L)
        per_head, strict_keep, _u = block_decay(b, seg_ref, ba_ref, rate, bias)
        for h in range(2):
            decay, carry, beta_row, beta_col, last_decay = per_head[h]
            kc = slice(h * 128, h * 128 + 128)
            vc = slice(h * 256, h * 256 + 256)
            q = q_ref[here, kc]
            qk = decay * mm3(split(q), split(k_ref[here, kc]), NT)
            pp[here, kc] = qk
            o = mm3(split(q * carry), split(s_ref[here, vc])) + mm3(split(qk * beta_row), split(u_ref[here, vc]))
            o_ref[here, vc] = o
            gp = gp_ref[here, vc]
            n = o * lax.rsqrt(jnp.mean(o * o, axis=-1, keepdims=True) + 1e-05)
            low_ref[here, vc] = (n * gain_ref[0:1, :] * (gp * sigmoid(gp))).astype(BF16)
        return 0

    lax.fori_loop(0, blocks, phase_c, 0)

    ring = Ring()
    mine = ring.rows(0, False, own)
    fetch[5].wait()
    greet([ring.right, ring.left, ring.flip])
    sc = Scatter(ring, part, scr, own)
    for k in sc.ORDER:
        quarter = ring.quarter(k, own)

        def partial(n, _):
            c = pl.ds(pl.multiple_of(n * 512, 512), 512)
            part[quarter, c] = mm1(low_ref[quarter, :], wout[:, c], NN)
            return 0

        lax.fori_loop(0, part.shape[1] // 512, partial, 0)
        sc.start(k)
    for i in (1, 8, 9, 10, 11, 12, 13, 14, 15, 16, 17, 18):
        leave[i].start()

    def prepare(b, _):
        base = pl.multiple_of(b * L, L)
        here = pl.ds(base, L)
        per_head, strict_keep, _u = block_decay(b, seg_ref, ba_ref, rate, bias)
        lane = lax.broadcasted_iota(jnp.int32, (L, L), 1)
        row = lax.broadcasted_iota(jnp.int32, (8, L), 0)
        tile, flat = jnp.zeros((L, L), F32), jnp.zeros((8, L), F32)
        for h in range(2):
            decay, carry, beta_row, beta_col, last_decay = per_head[h]
            kc = slice(h * 128, h * 128 + 128)
            db[here, kc] = decay * beta_row
            z_s[here, kc] = mm3(split(x_s[here, kc]), split(kw_s[here, kc]), TN)
            tile = tile + (jnp.where(lane == h, carry, 0.0) + jnp.where(lane == 2 + h, last_decay * beta_col, 0.0)
                           + jnp.where(lane == 4 + h, last_decay, 0.0))
            flat = flat + jnp.where(row == h, beta_row, 0.0)
        cols_s[here, :] = tile
        brow[b] = flat
        return 0

    steps = sc.middle()
    run(steps, 1)
    lax.fori_loop(0, blocks // 2, prepare, 0)
    run(steps, 1)
    lax.fori_loop(blocks // 2, blocks, prepare, 0)
    for i in range(19, 23):
        leave[i].start()
    run(steps)
    sc.finish()

    def finish(i, _):
        r = pl.multiple_of(i * 16, 16)
        at = pl.ds(pl.multiple_of(mine.start + r, 16), 16)
        resid = x_ref[at, :].astype(F32) + sc.value(r)
        resid_ref[pl.ds(r, 16), :] = resid
        n = resid * lax.rsqrt(jnp.mean(resid * resid, axis=-1, keepdims=True) + 1e-05)
        whole[at, :] = (n * fgain_ref[0:1, :]).astype(BF16).astype(F32)
        return 0

    lax.fori_loop(0, own // 16, finish, 0)
    ga = Gather(ring, whole, gsem, own)
    ga.start()
    run(ga.middle())
    ga.finish()

    def cast(i, _):
        r = pl.ds(pl.multiple_of(i * 32, 32), 32)
        hidmid_ref[r, :] = whole[r, :].astype(BF16)
        return 0

    lax.fori_loop(0, whole.shape[0] // 32, cast, 0)
    sc.s.drain()
    ga.s.drain()
    for c in leave:
        c.wait()


def front(x, again, wq, wk, wv, wt, wba, wout, segments, cq, ck, cv, dlog, dbias, gain, fgain, group=2):
    T, D = x.shape
    blocks = T // L
    own = T // NT_
    sd = jax.ShapeDtypeStruct
    saved = [((T, D), BF16), ((T, 512), BF16), ((T + PAD, 256), F32), ((T + PAD, 256), F32), ((T + PAD, 512), F32), ((T + 2 * PAD, L), F32),
             ((T, 512), F32), ((T, 128), F32), ((T, 256), F32), ((T, 256), F32), ((T, 256), F32), ((T, 512), F32), ((T, 512), F32), ((T, 512), F32),
             ((T, 256), F32), ((T, 256), F32), ((T, 512), F32), ((T, 256), F32), ((T, 256), F32), ((T, 256), F32), ((T, 256), F32),
             ((T, 128), F32), ((blocks, 8, L), F32)]
    vm = lambda s, t: pltpu.VMEM(s, t)
    return pl.pallas_call(
        functools.partial(front_kernel, blocks, group),
        out_shape=[sd((T, D), BF16), sd((own, D), F32)] + [sd(*s) for s in saved],
        in_specs=[VM, VM] + [ANY] * 6 + [VM] * 8, out_specs=[VM, VM] + [ANY] * 23,
        scratch_shapes=[vm(*s) for s in saved] + [vm(w.shape, BF16) for w in (wq, wk, wv, wt, wba, wout)]
        + [vm((T, 256), F32), vm((T, 512), F32), vm((T, 256), F32), vm((T, D), F32), vm((T, D), F32), vm((blocks, 8, L), F32),
           pltpu.SemaphoreType.DMA((6,)), pltpu.SemaphoreType.DMA((23,))] + scatter_scratch(own) + gather_sems(),
        compiler_params=params(1, 62),
        name="front",
    )(x, again, wq, wk, wv, wt, wba, wout, segments, cq, ck, cv, dlog, dbias, gain, fgain)


SMALL = 40
TAPS = 40


BACK = ("ga", "wout", "low", "ffn", "o", "gp", "pp", "x", "q", "cols", "brow", "k", "z", "u", "s", "db", "kkp", "ba",
        "qpad", "kpad", "vpad", "segpad", "fq", "fk", "fv")


def bwd_kernel(blocks, *refs):
    count = len(BACK)
    sources, rest = refs[:count], refs[count:]
    (resid_ref, cq_ref, ck_ref, cv_ref, dlog_ref, dbias_ref, gain_ref,
     dqp_ref, dkp_ref, dvp_ref, dgp_ref, dba_ref, dtap_ref, dgain_ref, oshard_ref, grads_ref) = rest[:16]
    held, rest = rest[16:16 + count], rest[16 + count:]
    fsem, gm_ref, do_s, y_s, ds_s, dq_s, dk_s, left, tap_s = rest[:9]
    rest = rest[9:]
    (ga_ref, wout_ref, low_ref, ffn_ref, o_ref, gp_ref, pp, x_ref, q_ref, cols_s, brow, k_ref, z_s, u_ref, s_ref, db, kkp, ba_ref,
     qpad, kpad, vpad, segpad, fq, fk, fv) = held
    fetch = [pltpu.make_async_copy(src, dst, fsem.at[i]) for i, (src, dst) in enumerate(zip(sources, held))]
    for c in fetch:
        c.start()

    def need(first, last):
        for c in fetch[first:last]:
            c.wait()

    T = blocks * L
    scr, dscr = rest[:7], rest[7:]
    own = resid_ref.shape[0]
    ring = Ring()

    def compute(a, b, put):
        put(slice(0, 512), mm1(left[...], jnp.concatenate([ga_ref[:, a], ga_ref[:, b]], axis=1), NN))

    dp = DpScatter(ring, dscr, compute)
    greet([ring.right, ring.left, ring.flip] + dp.devices())
    sc = Scatter(ring, ffn_ref, scr, own, sources[3])
    for k in sc.ORDER:
        sc.start(k)
    need(0, 3)
    left[...] = low_ref[...].T
    steps, cores, along = sc.middle(), dp.cores(), dp.along()
    run(cores)

    def mixed_back(i, _):
        r = pl.ds(pl.multiple_of(i * 256, 256), 256)
        gm_ref[r, :] = mm1(ga_ref[r, :], wout_ref[...], NT)
        return 0

    lax.fori_loop(0, T // 256, mixed_back, 0)
    run(along, 1)
    need(3, 4)
    run(steps, 2)
    run(along)
    need(4, 11)
    rate, bias = decay_rows(dlog_ref, dbias_ref)
    dgain_ref[...] = jnp.zeros_like(dgain_ref)
    dtap_ref[32:40, :] = jnp.zeros((8, 128), F32)
    tap_s[...] = jnp.zeros_like(tap_s)

    def phase_1(b, _):
        base = pl.multiple_of(b * L, L)
        for h in range(2):
            carry = cols_s[pl.ds(base, L), h:h + 1]
            kc = slice(h * 128, h * 128 + 128)
            vc = slice(h * 256, h * 256 + 256)
            o = o_ref[pl.ds(base, L), vc]
            gp = gp_ref[pl.ds(base, L), vc]
            gm = gm_ref[pl.ds(base, L), vc]
            gain = gain_ref[0:1, :]
            sg = sigmoid(gp)
            r = lax.rsqrt(jnp.mean(o * o, axis=-1, keepdims=True) + 1e-05)
            n = o * r
            act = gp * sg
            gn = gm * n
            dgain_ref[0:1, :] = dgain_ref[0:1, :] + jnp.sum(gn * act, axis=0, keepdims=True)
            dgp_ref[pl.ds(base, L), vc] = (gn * gain * (sg + act * (1.0 - sg))).astype(BF16)
            dn = gm * gain * act
            do = r * (dn - n * jnp.mean(dn * n, axis=-1, keepdims=True))
            do_s[pl.ds(base, L), vc] = do
            q = q_ref[pl.ds(base, L), kc]
            p = pp[pl.ds(base, L), kc] * brow[b, h:h + 1, :]
            sdo = split(do)
            sx = split(x_ref[pl.ds(base, L), kc])
            y0 = mm3(sx, split(mm3(split(p), sdo, TN)), TN)
            y_s[pl.ds(base, L), vc] = y0
            ds_s[pl.ds(base, L), vc] = mm3(split(q * carry), sdo, TN)
        return 0

    lax.fori_loop(0, blocks // 2, phase_1, 0)
    run(steps, 1)
    lax.fori_loop(blocks // 2, blocks, phase_1, 0)
    run(steps, 1)
    dp.second()
    need(11, 13)

    def phase_2(i, grads):
        b = blocks - 1 - i
        base = pl.multiple_of(b * L, L)
        new = []
        for h in range(2):
            carry = cols_s[pl.ds(base, L), h:h + 1]
            kc = slice(h * 128, h * 128 + 128)
            vc = slice(h * 256, h * 256 + 256)
            ds = grads[h]
            kept = ds_s[pl.ds(base, L), vc]
            ds_s[pl.ds(base, L), vc] = ds
            y = y_s[pl.ds(base, L), vc] + mm3(split(z_s[pl.ds(base, L), kc]), split(ds))
            y_s[pl.ds(base, L), vc] = y
            new.append(carry[L - 1:L, :] * ds + kept
                       - mm3(split(k_ref[pl.ds(base, L), kc] * carry), split(y), TN))
        return tuple(new)

    zero = jnp.zeros((128, 256), F32)
    lax.fori_loop(0, blocks, phase_2, (zero, zero))
    run(steps)
    dp.third()
    need(13, 18)

    def phase_3(b, _):
        base = pl.multiple_of(b * L, L)
        lane = lax.broadcasted_iota(jnp.int32, (L, L), 1)
        rowi = lax.broadcasted_iota(jnp.int32, (L, L), 0)
        row_tile = jnp.zeros((L, L), F32)
        col_tile = jnp.zeros((L, L), F32)
        for h in range(2):
            carry, weight, last_decay = (cols_s[pl.ds(base, L), j:j + 1] for j in (h, 2 + h, 4 + h))
            beta_row = brow[b, h:h + 1, :]
            kc = slice(h * 128, h * 128 + 128)
            vc = slice(h * 256, h * 256 + 256)
            q, k = q_ref[pl.ds(base, L), kc], k_ref[pl.ds(base, L), kc]
            sq, sk = split(q), split(k)
            decay_beta = db[pl.ds(base, L), kc]
            s, u = s_ref[pl.ds(base, L), vc], u_ref[pl.ds(base, L), vc]
            do, y, ds = do_s[pl.ds(base, L), vc], y_s[pl.ds(base, L), vc], ds_s[pl.ds(base, L), vc]
            ss, su, sdo, sy, sds = split(s), split(u), split(do), split(y), split(ds)
            do_st = mm3(sdo, ss, NT)
            y_st = mm3(sy, ss, NT)
            u_dst = mm3(su, sds, NT)
            dp = mm3(sdo, su, NT)
            da = -mm3(sy, su, NT)
            dcarry = jnp.sum(q * do_st - k * y_st, axis=-1, keepdims=True)
            dcarry_last = jnp.sum(jnp.sum(ds * s, axis=0, keepdims=True), axis=1, keepdims=True)
            dw = jnp.sum(u_dst * k, axis=-1, keepdims=True)
            dqk = dp * decay_beta
            dkk = jnp.where(rowi > lane, da * decay_beta, 0.0)
            prod = dp * pp[pl.ds(base, L), kc] + da * kkp[pl.ds(base, L), kc]
            dbeta_row = jnp.sum(prod, axis=0, keepdims=True)
            dec_grad = prod * beta_row
            dc_col = jnp.sum(dec_grad, axis=1, keepdims=True) + dcarry * carry
            dc_row = -jnp.sum(dec_grad, axis=0, keepdims=True)
            dlast = dw * weight
            row1 = rowi[:, 0:1]
            dc_col = dc_col - dlast
            dc_col = dc_col + jnp.where(row1 == L - 1, jnp.sum(dlast, axis=0, keepdims=True) + dcarry_last * carry, 0.0)
            dbeta_col = dw * last_decay
            row_tile = row_tile + jnp.where(rowi == h, dbeta_row, 0.0) + jnp.where(rowi == 2 + h, dc_row, 0.0)
            col_tile = col_tile + jnp.where(lane == h, dbeta_col, 0.0) + jnp.where(lane == 2 + h, dc_col, 0.0)
            sdqk, sdkk = split(dqk), split(dkk + dkk.T)
            dq_s[pl.ds(base, L), kc] = carry * do_st + mm3(sdqk, sk)
            dk_s[pl.ds(base, L), kc] = (mm3(sdqk, sq, TN) + mm3(sdkk, sk) - carry * y_st
                                        + weight * u_dst)
        grad = col_tile + row_tile.T
        dld = tri_sum(grad, TN)
        ba = rows(ba_ref, b)
        tile = decay_tile(ba, rate, bias)
        sig_alpha = sigmoid(ba + bias)
        dalpha = dld * rate * sig_alpha
        dpre = jnp.where(lane < 2, grad * tile * (1.0 - tile), jnp.where(lane < 4, dalpha, 0.0))
        dba_ref[pl.ds(base, L), :] = dpre.astype(BF16)
        dtap_ref[32:33, :] = dtap_ref[32:33, :] + jnp.sum(dpre, axis=0, keepdims=True)
        dtap_ref[33:34, :] = dtap_ref[33:34, :] + jnp.sum(dld * tile, axis=0, keepdims=True)
        return 0

    lax.fori_loop(0, blocks, phase_3, 0)

    need(18, count)

    R = 64
    groups = []
    for h in range(2):
        c = slice(h * 128, h * 128 + 128)
        groups.append((qpad, cq_ref, dq_s, dqp_ref, fq, c, h * 128, q_ref, 128.0))
        groups.append((kpad, ck_ref, dk_s, dkp_ref, fk, c, 256 + h * 128, k_ref, 1.0))
    for j in range(4):
        groups.append((vpad, cv_ref, y_s, dvp_ref, fv, slice(j * 128, j * 128 + 128), 512 + j * 128, None, None))
    for src in (dq_s, dk_s, y_s):
        src[T:, :] = jnp.zeros((PAD, src.shape[1]), F32)

    def conv_back(i, _):
        base = pl.multiple_of((T // R - 1 - i) * R, R)
        here = pl.ds(base, R)
        behind, ahead = doc_masks(segpad, base, R, False), doc_masks(segpad, base, R, True)
        for pre, taps, src, out_ref, factor, c, tc, unit, size in groups:
            d = src[here, c]
            if unit is not None:
                v = unit[here, c]
                d = d - v * (size * jnp.sum(d * v, axis=-1, keepdims=True))
            dy = factor[here, c] * d
            src[here, c] = dy
            z = pre[pl.ds(base, R + PAD), c]
            both = src[pl.ds(base, R + PAD), c]
            tc = slice(tc, tc + 128)
            total = dy * taps[0:1, c]
            tap_s[0, :, tc] = tap_s[0, :, tc] + jnp.sum((dy * z[PAD:]).reshape(R // 8, 8, 128), axis=0)
            for t in range(1, 4):
                total = total + both[t:t + R] * (ahead[t - 1] * taps[t:t + 1, c])
                tap_s[t, :, tc] = tap_s[t, :, tc] + jnp.sum((dy * (z[PAD - t:PAD - t + R] * behind[t - 1])).reshape(R // 8, 8, 128), axis=0)
            out_ref[here, c] = total.astype(BF16)
        return 0

    lax.fori_loop(0, T // R, conv_back, 0)
    for t in range(4):
        for j in range(8):
            dtap_ref[t * 8 + j:t * 8 + j + 1, :] = jnp.sum(tap_s[t, :, j * 128:(j + 1) * 128], axis=0, keepdims=True)
    sc.finish()

    def finish(i, _):
        r = pl.ds(pl.multiple_of(i * 16, 16), 16)
        oshard_ref[r, :] = (resid_ref[r, :] + sc.value(pl.multiple_of(i * 16, 16))).astype(BF16).astype(F32)
        return 0

    lax.fori_loop(0, own // 16, finish, 0)
    dp.finish(grads_ref)
    sc.s.drain()


def mixer_bwd(resid, cq, ck, cv, dlog, dbias, gain, **held):
    T, D = held["ga"].shape
    blocks = T // L
    own = resid.shape[0]
    n = held["low"].shape[1]
    sd = jax.ShapeDtypeStruct
    vm = lambda *r: pltpu.VMEM(r, F32)
    return pl.pallas_call(
        functools.partial(bwd_kernel, blocks),
        out_shape=(sd((T, 256), BF16), sd((T, 256), BF16), sd((T, 512), BF16), sd((T, 512), BF16), sd((T, 128), BF16),
                   sd((TAPS, 128), F32), sd((8, 256), F32), sd((own, D), F32), sd((n, 128), F32)),
        in_specs=[ANY] * len(BACK) + [VM] * 7, out_specs=[VM] * 9,
        scratch_shapes=[pltpu.VMEM(held[name].shape, held[name].dtype) for name in BACK]
        + [pltpu.SemaphoreType.DMA((len(BACK),)), vm(T, 512), vm(T, 512), vm(T + PAD, 512), vm(T, 512), vm(T + PAD, 256), vm(T + PAD, 256),
           pltpu.VMEM((n, T), BF16), vm(4, 8, 1024)] + scatter_scratch(own) + dp_scratch(n, 4),
        compiler_params=params(4, 62),
        name="mixer_backward",
    )(*[held[name] for name in BACK], resid, cq, ck, cv, dlog, dbias, gain)


def mid_kernel(wg_ref, wu_ref, wd_any, hid_ref, og_any, resid_any, gain_ref,
               ga_ref, inner_ref, ffn_any, gres_ref, dgain_ref, grads_ref,
               part, whole, left, gg_ref, gu_ref, wd_ref, og_ref, resid_in, csem, *rest):
    scr, gsem, dscr = rest[:7], rest[7:9], rest[9:]
    fetches = [pltpu.make_async_copy(src, dst, csem.at[i]) for i, (src, dst) in enumerate(
        ((wd_any, wd_ref), (og_any, og_ref), (resid_any, resid_in)))]
    for f in fetches:
        f.start()
    ring = Ring()
    own = gres_ref.shape[0]
    n = gg_ref.shape[1]
    mine = ring.rows(0, False, own)

    def compute(a, b, put):
        hid = jnp.concatenate([hid_ref[:, a], hid_ref[:, b]], axis=1)
        put(slice(0, n), mm1(left[0:n, :], hid, NN))
        put(slice(n, 2 * n), mm1(left[n:2 * n, :], hid, NN))

    dp = DpScatter(ring, dscr, compute)
    greet([ring.right, ring.left, ring.flip] + dp.devices())
    sc = Scatter(ring, part, scr, own)
    for k in sc.ORDER:
        quarter = ring.quarter(k, own)
        hid = hid_ref[quarter, :]
        gate = mm1(hid, wg_ref[...], NT)
        up = mm1(hid, wu_ref[...], NT)
        sig = sigmoid(gate)
        act = gate * sig
        inner_ref[quarter, :] = (act * up).astype(BF16)
        if k == 2:
            fetches[0].wait()
            fetches[1].wait()
        back = mm1(og_ref[quarter, :], wd_ref[...], NT)
        gg_ref[quarter, :] = (back * up * sig * (1.0 + gate * (1.0 - sig))).astype(BF16)
        gu_ref[quarter, :] = (back * act).astype(BF16)

        def partial(i, _):
            cols = pl.ds(pl.multiple_of(i * 512, 512), 512)
            part[quarter, cols] = mm1(gg_ref[quarter, :], wg_ref[:, cols], NN) + mm1(gu_ref[quarter, :], wu_ref[:, cols], NN)
            return 0

        lax.fori_loop(0, part.shape[1] // 512, partial, 0)
        sc.start(k)
    left[0:n, :] = gg_ref[...].T
    left[n:2 * n, :] = gu_ref[...].T
    together(sc, dp)
    fetches[2].wait()
    sc.finish()
    dgain_ref[...] = jnp.zeros_like(dgain_ref)

    def finish(i, _):
        r = pl.multiple_of(i * 16, 16)
        resid = resid_in[pl.ds(r, 16), :]
        back = sc.value(r)
        scale = lax.rsqrt(jnp.mean(resid * resid, axis=-1, keepdims=True) + 1e-05)
        nn = resid * scale
        bn = back * nn
        dgain_ref[...] = dgain_ref[...] + bn[0:8] + bn[8:16]
        b = back * gain_ref[0:1, :]
        g = og_ref[pl.ds(pl.multiple_of(mine.start + r, 16), 16), :].astype(F32) + scale * (b - nn * jnp.mean(b * nn, axis=-1, keepdims=True))
        gres_ref[pl.ds(r, 16), :] = g
        whole[pl.ds(pl.multiple_of(mine.start + r, 16), 16), :] = g.astype(BF16).astype(F32)
        return 0

    lax.fori_loop(0, own // 16, finish, 0)
    ga = Gather(ring, whole, gsem, own)
    ga.start()
    sc.s.drain()
    steps = ga.middle()
    run(steps, 1)
    dp.second()
    run(steps, 1)

    def down(i, _):
        cols = pl.ds(pl.multiple_of(i * 256, 256), 256)
        part[:, cols] = mm1(inner_ref[...], wd_ref[:, cols], NN)
        return 0

    lax.fori_loop(0, part.shape[1] // 256, down, 0)
    leave = pltpu.make_async_copy(part, ffn_any, csem.at[3])
    leave.start()
    run(steps)
    dp.third()
    ga.finish()

    def cast(i, _):
        r = pl.ds(pl.multiple_of(i * 32, 32), 32)
        ga_ref[r, :] = whole[r, :].astype(BF16)
        return 0

    lax.fori_loop(0, whole.shape[0] // 32, cast, 0)
    dp.finish(grads_ref)
    leave.wait()
    ga.s.drain()


def mid_exchange(wg, wu, wd, hid, og, resid, gain):
    T, D = og.shape
    own = T // NT_
    m = wg.shape[0]
    sd = jax.ShapeDtypeStruct
    return pl.pallas_call(
        mid_kernel,
        out_shape=(sd((T, D), BF16), sd((T, m), BF16), sd((T, D), F32), sd((own, D), F32), sd((8, D), F32), sd((2 * m, 128), F32)),
        in_specs=[VM, VM, ANY, VM, ANY, ANY, VM], out_specs=[VM, VM, ANY, VM, VM, VM],
        scratch_shapes=[pltpu.VMEM((T, D), F32), pltpu.VMEM((T, D), F32), pltpu.VMEM((2 * m, T), BF16),
                        pltpu.VMEM((T, m), BF16), pltpu.VMEM((T, m), BF16), pltpu.VMEM((m, D), BF16), pltpu.VMEM((T, D), BF16),
                        pltpu.VMEM((own, D), F32), pltpu.SemaphoreType.DMA((4,))]
        + scatter_scratch(own) + gather_sems() + dp_scratch(2 * m, 4),
        compiler_params=params(2, 62),
        name="mid_exchange",
    )(wg, wu, wd, hid, og, resid, gain)


def in_kernel(*refs):
    sources, (gres_ref, x_ref, gain_ref, fpart_ref, hgain_ref, taps_ref, oshard_ref), rest = refs[:13], refs[13:20], refs[20:]
    whole, out_whole, grads_ref, gains_out, taps_out = rest[:5]
    held, rest = rest[5:18], rest[18:]
    gq, gk, gv, gt, gba, wq, wk, wv, wt, wba, inner_ref, hid_ref, og_ref = held
    part, shard, left, xown, g_own, g_recv, s_own, s_recv, fsem, csem, ssem, srsem = rest[:12]
    rest = rest[12:]
    scr, gsem, osem, dscr = rest[:7], rest[7:9], rest[9:11], rest[11:]
    loads = [pltpu.make_async_copy(src, dst, fsem.at[i]) for i, (src, dst) in enumerate(zip(sources, held))]
    ring = Ring()
    own = gres_ref.shape[0]
    mine = ring.rows(0, False, own)
    fetch = pltpu.make_async_copy(x_ref.at[mine], xown, csem.at[0])
    fetch.start()
    place_out = pltpu.make_async_copy(oshard_ref, out_whole.at[mine], csem.at[1])
    place_out.start()
    for c in loads:
        c.start()
    t_peers = [(ring.d, lax.rem(ring.t + j, NT_)) for j in range(1, NT_)]
    d_peers = [(lax.rem(ring.d + j, 16), ring.t) for j in range(1, 16)]
    greet(t_peers + d_peers)
    place_out.wait()
    go = Gather(ring, out_whole, osem, own)
    go.start()
    for c in loads[:10]:
        c.wait()
    sc = Scatter(ring, part, scr, own)
    for k in sc.ORDER:
        quarter = ring.quarter(k, own)

        def partial(i, _):
            rows_w = pl.ds(pl.multiple_of(i * 512, 512), 512)
            total = mm1(gq[quarter, :], wq[rows_w, :], NT) + mm1(gk[quarter, :], wk[rows_w, :], NT)
            total = total + mm1(gv[quarter, :], wv[rows_w, :], NT) + mm1(gt[quarter, :], wt[rows_w, :], NT)
            part[quarter, rows_w] = total + mm1(gba[quarter, :], wba[:, rows_w], NN)
            return 0

        lax.fori_loop(0, part.shape[1] // 512, partial, 0)
        sc.start(k)

    def compute(a, b, put):
        hid = jnp.concatenate([hid_ref[:, a], hid_ref[:, b]], axis=1)
        put(slice(0, 768), mm1(left[0:768, :], hid, NN))
        put(slice(768, 1552), mm1(left[768:1552, :], hid, NN))
        put(slice(1552, 2256), mm1(left[1552:, :], jnp.concatenate([og_ref[:, a], og_ref[:, b]], axis=1), NN))

    dp = DpScatter(ring, dscr, compute)
    left[0:256, :] = gq[...].T
    left[256:512, :] = gk[...].T
    left[512:1024, :] = gv[...].T
    left[1024:1536, :] = gt[...].T
    left[1536:1552, :] = gba[...].T[0:16]
    for c in loads[10:]:
        c.wait()
    left[1552:, :] = inner_ref[...].T
    outs = go.middle()
    run(outs, 1)
    together(sc, dp)
    run(outs, 2)
    fetch.wait()
    sc.finish()
    g_own[...] = jnp.zeros_like(g_own)
    ffn_gain = jnp.sum(fpart_ref[...], axis=0, keepdims=True)
    for j in range(16):
        g_own[16 + j:17 + j, :] = ffn_gain[:, j * 128:(j + 1) * 128]
    for j in range(2):
        g_own[32 + j:33 + j, :] = hgain_ref[0:1, j * 128:(j + 1) * 128]

    def finish(i, total):
        r = pl.multiple_of(i * 16, 16)
        x = xown[pl.ds(r, 16), :].astype(F32)
        back = sc.value(r)
        scale = lax.rsqrt(jnp.mean(x * x, axis=-1, keepdims=True) + 1e-05)
        nn = x * scale
        total = total + jnp.sum(back * nn, axis=0, keepdims=True)
        b = back * gain_ref[0:1, :]
        g = gres_ref[pl.ds(r, 16), :] + scale * (b - nn * jnp.mean(b * nn, axis=-1, keepdims=True))
        shard[pl.ds(r, 16), :] = g.astype(BF16).astype(F32)
        return total

    total = lax.fori_loop(0, own // 16, finish, jnp.zeros((1, x_ref.shape[1]), F32))
    for j in range(16):
        g_own[j:j + 1, :] = total[:, j * 128:(j + 1) * 128]
    place = pltpu.make_async_copy(shard, whole.at[mine], csem.at[2])
    place.start()
    place.wait()
    small = Sends(ssem, srsem)
    for j, dev in enumerate(t_peers):
        small.go(j, g_own, g_recv.at[j], dev)
    ga = Gather(ring, whole, gsem, own)
    ga.start()
    run(outs)
    dp.second()
    steps = ga.middle()
    run(steps, 1)
    for j, dev in enumerate(t_peers):
        small.got(j, g_recv.at[j], dev)
    gains = g_own[...]
    for j in range(NT_ - 1):
        gains = gains + g_recv[j]
    s_own[0:SMALL, :] = gains
    s_own[SMALL:, :] = taps_ref[...]
    for j, dev in enumerate(d_peers):
        small.go(7 + j, s_own, s_recv.at[j], dev)
    run(steps)
    dp.third()
    for j, dev in enumerate(d_peers):
        small.got(7 + j, s_recv.at[j], dev)
    both = s_own[...]
    for j in range(15):
        both = both + s_recv[j]
    gains_out[...] = both[:SMALL]
    taps_out[...] = both[SMALL:]
    go.finish()
    ga.finish()
    dp.finish(grads_ref)
    small.drain()
    go.s.drain()
    sc.s.drain()
    ga.s.drain()


def in_exchange(grads, weights, inner, hid, og, gres, inputs, gain, ffn_part, hgain, taps, oshard):
    T, D = inputs.shape
    own = T // NT_
    n = 1552 + inner.shape[1]
    sd = jax.ShapeDtypeStruct
    vm = lambda *s: pltpu.VMEM(s, F32)
    held = (*grads, *weights, inner, hid, og)
    return pl.pallas_call(
        in_kernel,
        out_shape=(sd((T, D), F32), sd((T, D), F32), sd((n, 128), F32), sd((SMALL, 128), F32), sd((TAPS, 128), F32)),
        in_specs=[ANY] * 13 + [VM, ANY] + [VM] * 5, out_specs=[ANY, ANY, VM, VM, VM],
        scratch_shapes=[pltpu.VMEM(h.shape, h.dtype) for h in held]
        + [vm(T, D), vm(own, D), pltpu.VMEM((n, T), BF16), pltpu.VMEM((own, D), BF16),
           vm(SMALL, 128), vm(7, SMALL, 128), vm(SMALL + TAPS, 128), vm(15, SMALL + TAPS, 128),
           pltpu.SemaphoreType.DMA((13,)), pltpu.SemaphoreType.DMA((3,)), pltpu.SemaphoreType.DMA((22,)), pltpu.SemaphoreType.DMA((22,))]
        + scatter_scratch(own) + gather_sems() + gather_sems() + dp_scratch(n, 4),
        compiler_params=params(3, 62),
        name="in_exchange",
    )(*held, gres, inputs, gain, ffn_part, hgain, taps, oshard)


def last_kernel(ig_ref, out_ref, gin_ref, gmid_ref, gout_ref, gains_ref, taps_ref,
                ig_low, out_low, gq, gk, gv, gt, gbeta, galpha, cq, ck, cv, dlog, dbias, hgain, again, fgain, gug, gup, gdown, gout):
    ig_low[...] = ig_ref[...].astype(BF16)
    out_low[...] = out_ref[...].astype(BF16)

    @pl.when(pl.program_id(0) == 0)
    def _():
        gq[...] = gin_ref[0:256, :].T
        gk[...] = gin_ref[256:512, :].T
        gv[...] = gin_ref[512:1024, :].T
        gt[...] = gin_ref[1024:1536, :].T
        gbeta[...] = gin_ref[1536:1538, :]
        galpha[...] = gin_ref[1538:1540, :]
        gdown[...] = gin_ref[1552:, :]
        n = gug.shape[0]
        gug[...] = gmid_ref[0:n, :]
        gup[...] = gmid_ref[n:, :]
        gout[...] = gout_ref[...]
        for t in range(4):
            for j in range(8):
                row = taps_ref[t * 8 + j:t * 8 + j + 1, :]
                ref, at = ((cq, j), (ck, j - 2), (cv, j - 4))[0 if j < 2 else 1 if j < 4 else 2]
                ref[t:t + 1, at * 128:(at + 1) * 128] = row
        dbias[...] = taps_ref[32:33, 2:4]
        dlog[...] = taps_ref[33:34, 2:4]
        again[...] = gains_ref[0:16, :]
        fgain[...] = gains_ref[16:32, :]
        hgain[...] = gains_ref[32:34, :]


def last(ig, out, gin, gmid, gout, gains, taps):
    T, D = ig.shape
    n = gmid.shape[0] // 2
    sd = lambda *s: jax.ShapeDtypeStruct(s, F32)
    step = lambda: pl.BlockSpec((128, D), lambda i: (i, 0))
    fixed = lambda s: pl.BlockSpec(s, lambda i: (0, 0))
    small = [sd(128, 256), sd(128, 256), sd(128, 512), sd(128, 512), sd(2, 128), sd(2, 128), sd(4, 256), sd(4, 256), sd(4, 512),
             sd(1, 2), sd(1, 2), sd(2, 128), sd(16, 128), sd(16, 128), sd(n, 128), sd(n, 128), sd(gin.shape[0] - 1552, 128), sd(gout.shape[0], 128)]
    return pl.pallas_call(
        last_kernel,
        grid=(T // 128,),
        out_shape=[jax.ShapeDtypeStruct((T, D), BF16)] * 2 + small,
        in_specs=[step(), step()] + [fixed(a.shape) for a in (gin, gmid, gout, gains, taps)],
        out_specs=[step(), step()] + [fixed(a.shape) for a in small],
        compiler_params=pltpu.CompilerParams(vmem_limit_bytes=48 * 2 ** 20),
        name="last",
    )(ig, out, gin, gmid, gout, gains, taps)


def row(v):
    return v.reshape(1, v.shape[0])


def per_device(inputs, segments, attn_gain, w_query, w_key, w_value, w_gate, w_beta, w_alpha, conv_query, conv_key, conv_value,
               decay_log, decay_bias, head_gain, w_out, ffn_gain, w_up_gate, w_up, w_down, out_grad):
    D = inputs.shape[1]
    w_ba = jnp.concatenate([w_beta.T, w_alpha.T, jnp.zeros((124, D), BF16)], axis=0)
    dlog, dbias, hgain = row(decay_log), row(decay_bias), row(head_gain)
    hidden_mid, resid, hidden_in, low, *saved = front(
        inputs, row(attn_gain), w_query, w_key, w_value, w_gate, w_ba, w_out, segments, conv_query, conv_key, conv_value,
        dlog, dbias, hgain, row(ffn_gain))
    names = ("qpad", "kpad", "vpad", "segpad", "gp", "ba", "q", "k", "x", "u", "s", "o", "fq", "fk", "fv", "pp", "kkp", "db", "z", "cols", "brow")
    grad_attn, inner, ffn, grad_resid, ffn_gain_part, grads_mid = mid_exchange(
        w_up_gate.T, w_up.T, w_down, hidden_mid, out_grad, resid, row(ffn_gain))
    *grads, taps, hgain_part, oshard, grads_out = mixer_bwd(
        resid, conv_query, conv_key, conv_value, dlog, dbias, hgain, ga=grad_attn, wout=w_out, low=low, ffn=ffn, **dict(zip(names, saved)))
    ig, out, grads_in, gains, taps = in_exchange(
        grads, (w_query, w_key, w_value, w_gate, w_ba), inner, hidden_in, out_grad, grad_resid, inputs,
        row(attn_gain), ffn_gain_part, hgain_part, taps, oshard)
    (input_grad, outputs, gq, gk, gv, gt, gbeta, galpha, cq, ck, cv, g_dlog, g_dbias, g_hgain, g_again, g_fgain,
     gug, gup, gdown, gout) = last(ig, out, grads_in, grads_mid, grads_out, gains, taps)
    return (outputs, input_grad, g_again.reshape(D), gq, gk, gv, gt, gbeta.T, galpha.T, cq, ck, cv,
            g_dlog.reshape(2), g_dbias.reshape(2), g_hgain.reshape(head_gain.shape), gout, g_fgain.reshape(D), gug.T, gup.T, gdown)


def solution(mesh):
    col, rows_t, rep = P(None, "tensor"), P("tensor", None), P()
    tok, both, head = P("dp", None), P("dp", "tensor"), P("tensor")
    return jax.shard_map(
        per_device,
        mesh=mesh,
        in_specs=(tok, tok, rep, col, col, col, col, col, col, col, col, col, head, head, rep, rows_t, rep, col, col, rows_t, tok),
        out_specs=(tok, tok, rep, both, both, both, both, both, both, col, col, col, head, head, rep, P("tensor", "dp"), rep, both, both, P("tensor", "dp")),
        check_vma=False,
    )
```

```python
import functools
import jax, jax.numpy as jnp
from jax import lax
from jax.experimental import pallas as pl
from jax.experimental.pallas import tpu as pltpu
from jax.sharding import PartitionSpec as P

F32 = jnp.float32
BF16 = jnp.bfloat16
L = 128
PAD = 8
NN = (((1,), (0,)), ((), ()))
NT = (((1,), (1,)), ((), ()))
TN = (((0,), (0,)), ((), ()))


def split(x):
    hi = x.astype(BF16)
    return hi, (x - hi.astype(F32)).astype(BF16)


def mm1(a, b, dims):
    return lax.dot_general(a, b, dims, preferred_element_type=F32)


def mm3(a, b, dims=NN):
    (ia,), (ib,) = dims[0]
    if a[0].shape[ia] > 128:
        return mm1(a[0], b[0], dims) + (mm1(a[0], b[1], dims) + mm1(a[1], b[0], dims))
    return mm1(jnp.concatenate(a, axis=ia), jnp.concatenate([b[0], b[0]], axis=ib), dims) + mm1(a[0], b[1], dims)


def sigmoid(x):
    d = 1.0 + jnp.exp(-jnp.maximum(x, -80.0))
    r = pl.reciprocal(d, approx=True)
    r = r * (2.0 - d * r)
    return r * (2.0 - d * r)


def rows(ref, b, n=L, lead=0):
    return ref[pl.ds(pl.multiple_of(b * L, L) + lead, n)]


def decay_tile(ba, rate, bias):
    lane = lax.broadcasted_iota(jnp.int32, ba.shape, 1)
    shifted = ba + bias
    soft = jnp.maximum(shifted, 0.0) + jnp.log1p(jnp.exp(-jnp.abs(shifted)))
    return jnp.where(lane < 2, sigmoid(ba), rate * soft)


def tri_sum(tile, dims):
    r = lax.broadcasted_iota(jnp.int32, (L, L), 0)
    c = lax.broadcasted_iota(jnp.int32, (L, L), 1)
    tri = (r >= c).astype(BF16)
    p0 = tile.astype(BF16)
    rest = tile - p0.astype(F32)
    p1 = rest.astype(BF16)
    p2 = (rest - p1.astype(F32)).astype(BF16)
    return mm1(tri, p0, dims) + (mm1(tri, p1, dims) + mm1(tri, p2, dims))


def block_decay(b, seg_ref, ba_ref, rate, bias):
    tile = decay_tile(rows(ba_ref, b), rate, bias)
    cum = tri_sum(tile, NN)
    lane = lax.broadcasted_iota(jnp.int32, (L, L), 1)
    both = jnp.where(lane < 2, tile, cum)
    flat = both.T
    seg_row = seg_ref[b, 0:1, :]
    seg_col = jnp.broadcast_to(seg_row, (L, L)).T
    prev = seg_ref[b, 1:2, 0:1]
    r = lax.broadcasted_iota(jnp.int32, (L, L), 0)
    keep = (seg_col == seg_row) & (r >= lane)
    strict_keep = r > lane
    carry_keep = seg_col[:, 0:1] == prev
    out = []
    for h in range(2):
        c_col = cum[:, 2 + h:3 + h]
        c_row = flat[2 + h:3 + h, :]
        beta_row = flat[h:h + 1, :]
        decay = jnp.where(keep, jnp.exp(jnp.where(keep, c_col - c_row, 0.0)), 0.0)
        carry = jnp.where(carry_keep, jnp.exp(c_col), 0.0)
        last_keep = seg_col[:, 0:1] == seg_row[:, L - 1:L]
        last_decay = jnp.where(last_keep, jnp.exp(jnp.where(last_keep, c_col[L - 1:L, :] - c_col, 0.0)), 0.0)
        beta_col = tile[:, h:h + 1]
        out.append((decay, carry, beta_row, beta_col, last_decay))
    return out, strict_keep, (tile, seg_col)


MESH = pl.DeviceIdType.MESH
NT_ = 8
ZH, YH = 512, 512


def run(steps, count=None):
    if count is None:
        for _ in steps:
            pass
    else:
        for _ in range(count):
            next(steps)


class Ring:
    def __init__(self):
        self.d = lax.axis_index("dp")
        self.t = lax.axis_index("tensor")
        self.y = lax.rem(self.t, 2)
        self.z = self.t // 2
        self.right = (self.d, self.at(1) * 2 + self.y)
        self.left = (self.d, self.at(3) * 2 + self.y)
        self.flip = (self.d, self.z * 2 + 1 - self.y)

    def at(self, k):
        return lax.rem(self.z + k, 4)

    def rows(self, k, other, own):
        side = 1 - self.y if other else self.y
        return pl.ds(pl.multiple_of((self.at(k) * 2 + side) * own, own), own)

    def quarter(self, k, own):
        return pl.ds(pl.multiple_of(self.at(k) * 2 * own, 2 * own), 2 * own)


class Sends:
    def __init__(self, ssem, rsem):
        self.ssem, self.rsem, self.made = ssem, rsem, []

    def make(self, i, src, dst, device):
        return pltpu.make_async_remote_copy(src_ref=src, dst_ref=dst, send_sem=self.ssem.at[i], recv_sem=self.rsem.at[i],
                                            device_id=device, device_id_type=MESH)

    def go(self, i, src, dst, device):
        c = self.make(i, src, dst, device)
        c.start()
        self.made.append(c)

    def got(self, i, dst, device):
        self.make(i, dst, dst, device).wait_recv()

    def drain(self):
        for c in self.made:
            c.wait_send()


def greet(devices):
    barrier = pltpu.get_barrier_semaphore()
    for dev in devices:
        pl.semaphore_signal(barrier, inc=1, device_id=dev, device_id_type=MESH)
    pl.semaphore_wait(barrier, len(devices))


ZA, ZB, ZZ = pl.ds(0, ZH), pl.ds(ZH, ZH), pl.ds(0, 2 * ZH)
YA, YB, YY = pl.ds(2 * ZH, YH), pl.ds(2 * ZH + YH, YH), pl.ds(2 * ZH, 2 * YH)
ZLO, ZHI, YLO, YHI = pl.ds(0, ZH), pl.ds(ZH, ZH), pl.ds(0, YH), pl.ds(YH, YH)


def scatter_scratch(own):
    return [pltpu.VMEM((4, own, 2 * YH), F32), pltpu.VMEM((6, 2 * own, ZH), F32), pltpu.VMEM((6, own, YH), F32),
            pltpu.VMEM((own, 2 * ZH), F32), pltpu.VMEM((own, 2 * ZH), F32),
            pltpu.SemaphoreType.DMA((17,)), pltpu.SemaphoreType.DMA((17,))]


def add_rows(dst, src_of, n):
    def one(i, _):
        r = pl.multiple_of(i * 16, 16)
        dst[pl.ds(r, 16), :] = dst[pl.ds(r, 16), :] + src_of(r)
        return 0
    lax.fori_loop(0, n // 16, one, 0)


def sub(ref, rows, cols):
    return lambda r: ref[pl.ds(pl.multiple_of(rows.start + r, 16), 16), cols]


class Scatter:
    def __init__(self, ring, part, scratch, own, source=None):
        self.ring, self.part, self.own = ring, part, own
        self.source = part if source is None else source
        self.yb, self.zb, self.yr, self.zsend, self.zf, ssem, rsem = scratch
        self.s = Sends(ssem, rsem)

    ORDER = (2, 1, 3, 0)

    def start(self, k):
        g, s, p, own = self.ring, self.s, self.source, self.own
        if k == 2:
            s.go(0, p.at[g.quarter(2, own), ZB], self.zb.at[0], g.right)
            s.go(1, p.at[g.quarter(2, own), ZA], self.zb.at[1], g.left)
        if k == 1:
            s.go(2, p.at[g.quarter(1, own), ZA], self.zb.at[2], g.right)
        if k == 3:
            s.go(3, p.at[g.quarter(3, own), ZB], self.zb.at[3], g.left)
        s.go({2: 6, 1: 7, 3: 8, 0: 9}[k], p.at[g.rows(k, True, own), YY], self.yb.at[k], g.flip)

    def middle(self):
        g, s, p, own = self.ring, self.s, self.part, self.own
        yb, zb, yr = self.yb, self.zb, self.yr
        s.got(6, yb.at[2], g.flip)
        add_rows(yb.at[2], sub(p, g.rows(2, False, own), YY), own)
        s.go(10, yb.at[2, :, YHI], yr.at[0], g.right)
        s.go(11, yb.at[2, :, YLO], yr.at[1], g.left)
        yield
        s.got(0, zb.at[0], g.left)
        add_rows(zb.at[0], sub(p, g.quarter(1, own), ZB), 2 * own)
        s.go(4, zb.at[0], zb.at[4], g.right)
        s.got(1, zb.at[1], g.right)
        add_rows(zb.at[1], sub(p, g.quarter(3, own), ZA), 2 * own)
        s.go(5, zb.at[1], zb.at[5], g.left)
        yield
        s.got(7, yb.at[1], g.flip)
        add_rows(yb.at[1], sub(p, g.rows(1, False, own), YY), own)
        s.go(12, yb.at[1, :, YLO], yr.at[2], g.right)
        s.got(10, yr.at[0], g.left)
        add_rows(yr.at[0], lambda r: yb[1, pl.ds(r, 16), YHI], own)
        s.go(14, yr.at[0], yr.at[4], g.right)
        yield
        s.got(8, yb.at[3], g.flip)
        add_rows(yb.at[3], sub(p, g.rows(3, False, own), YY), own)
        s.go(13, yb.at[3, :, YHI], yr.at[3], g.left)
        s.got(11, yr.at[1], g.right)
        add_rows(yr.at[1], lambda r: yb[3, pl.ds(r, 16), YLO], own)
        s.go(15, yr.at[1], yr.at[5], g.left)
        yield
        s.got(2, zb.at[2], g.left)
        s.got(3, zb.at[3], g.right)
        s.got(4, zb.at[4], g.left)
        s.got(5, zb.at[5], g.right)
        base = g.rows(0, True, own).start
        lead = (1 - g.y) * own

        def one(i, _):
            r = pl.multiple_of(i * 16, 16)
            at = pl.ds(pl.multiple_of(lead + r, 16), 16)
            mine = pl.ds(pl.multiple_of(base + r, 16), 16)
            self.zsend[pl.ds(r, 16), ZLO] = p[mine, ZA] + (zb[2, at, :] + zb[5, at, :])
            self.zsend[pl.ds(r, 16), ZHI] = p[mine, ZB] + (zb[3, at, :] + zb[4, at, :])
            return 0

        lax.fori_loop(0, own // 16, one, 0)
        s.go(16, self.zsend, self.zf, g.flip)
        yield

    def finish(self):
        g, s = self.ring, self.s
        s.got(9, self.yb.at[0], g.flip)
        s.got(12, self.yr.at[2], g.left)
        s.got(13, self.yr.at[3], g.right)
        s.got(14, self.yr.at[4], g.left)
        s.got(15, self.yr.at[5], g.right)
        s.got(16, self.zf, g.flip)

    def value(self, r):
        g, p, own = self.ring, self.part, self.own
        zb, yr = self.zb, self.yr
        at = pl.ds(pl.multiple_of(g.y * own + r, 16), 16)
        here = pl.ds(r, 16)
        mine = pl.ds(pl.multiple_of(g.rows(0, False, own).start + r, 16), 16)
        za = p[mine, ZA] + (zb[2, at, :] + zb[5, at, :]) + self.zf[here, ZLO]
        zz = p[mine, ZB] + (zb[3, at, :] + zb[4, at, :]) + self.zf[here, ZHI]
        ya = p[mine, YA] + self.yb[0, here, YLO] + (yr[2, here, :] + yr[5, here, :])
        yz = p[mine, YB] + self.yb[0, here, YHI] + (yr[3, here, :] + yr[4, here, :])
        return jnp.concatenate([za, zz, ya, yz], axis=1)


def gather_sems():
    return [pltpu.SemaphoreType.DMA((17,)), pltpu.SemaphoreType.DMA((17,))]


class Gather:
    def __init__(self, ring, whole, sems, own, yh=256):
        self.ring, self.whole, self.own = ring, whole, own
        zh = whole.shape[1] // 2 - yh
        self.za, self.zb, self.zz = pl.ds(0, zh), pl.ds(zh, zh), pl.ds(0, 2 * zh)
        self.ya, self.yb, self.yy = pl.ds(2 * zh, yh), pl.ds(2 * zh + yh, yh), pl.ds(2 * zh, 2 * yh)
        self.s = Sends(*sems)

    def _go(self, i, rows, cols, device):
        ref = self.whole.at[rows, cols]
        self.s.go(i, ref, ref, device)

    def _got(self, i, rows, cols, device):
        self.s.got(i, self.whole.at[rows, cols], device)

    def start(self):
        g, own = self.ring, self.own
        mine = g.rows(0, False, own)
        self._go(0, mine, self.yy, g.right)
        self._go(1, mine, self.yy, g.left)
        self._go(2, mine, self.zz, g.flip)
        self._go(3, mine, self.zz, g.right)
        self._go(4, mine, self.zz, g.left)
        self._go(5, mine, self.yy, g.flip)

    def middle(self):
        g, own = self.ring, self.own
        lf, rt = g.rows(3, False, own), g.rows(1, False, own)
        lo, ro = g.rows(3, True, own), g.rows(1, True, own)
        far, faro, other = g.rows(2, False, own), g.rows(2, True, own), g.rows(0, True, own)
        self._got(0, lf, self.yy, g.left)
        self._go(6, lf, self.yb, g.right)
        self._go(7, lf, self.yy, g.flip)
        self._got(1, rt, self.yy, g.right)
        self._go(8, rt, self.ya, g.left)
        self._go(9, rt, self.yy, g.flip)
        self._got(2, other, self.zz, g.flip)
        self._go(10, other, self.zz, g.right)
        self._go(11, other, self.zz, g.left)
        yield
        self._got(6, far, self.yb, g.left)
        self._got(8, far, self.ya, g.right)
        self._go(12, far, self.yy, g.flip)
        yield
        self._got(3, lf, self.zz, g.left)
        self._go(13, lf, self.zb, g.right)
        self._got(4, rt, self.zz, g.right)
        self._go(14, rt, self.za, g.left)
        yield
        self._got(10, lo, self.zz, g.left)
        self._go(15, lo, self.zb, g.right)
        self._got(11, ro, self.zz, g.right)
        self._go(16, ro, self.za, g.left)
        yield

    def finish(self):
        g, own = self.ring, self.own
        far, faro, other = g.rows(2, False, own), g.rows(2, True, own), g.rows(0, True, own)
        self._got(5, other, self.yy, g.flip)
        self._got(7, g.rows(3, True, own), self.yy, g.flip)
        self._got(9, g.rows(1, True, own), self.yy, g.flip)
        self._got(12, faro, self.yy, g.flip)
        self._got(13, far, self.zb, g.left)
        self._got(14, far, self.za, g.right)
        self._got(15, faro, self.zb, g.left)
        self._got(16, faro, self.za, g.right)


class DpScatter:
    ORDER = (2, 1, 3, 0)

    def __init__(self, ring, scratch, compute):
        d, t = ring.d, ring.t
        self.c, self.x, self.y = lax.rem(d, 2), lax.rem(d // 2, 4), d // 8
        self.pair = (d + 1 - 2 * self.c, t)
        self.right = ((self.y * 4 + self.step(1)) * 2 + self.c, t)
        self.left = ((self.y * 4 + self.step(3)) * 2 + self.c, t)
        self.far = (((1 - self.y) * 4 + self.x) * 2 + self.c, t)
        self.csend, self.crecv, self.xr, self.yr, ssem, rsem = scratch
        self.s = Sends(ssem, rsem)
        self.compute = compute

    def step(self, k):
        return lax.rem(self.x + k, 4)

    def devices(self):
        return [self.pair, self.right, self.left, self.far]

    def cols(self, k, side, core):
        return pl.ds(pl.multiple_of(((side * 4 + self.step(k)) * 2 + core) * 128, 128), 128)

    def cores(self):
        slots, sent = self.csend.shape[0], []
        for n, k in enumerate(self.ORDER):
            slot = 2 * n % slots
            for c in sent[:2] if 2 * n >= slots else []:
                c.wait_send()
            sent = sent[2:] if 2 * n >= slots else sent

            def put(rows, both):
                self.csend[slot, rows, :] = both[:, :128]
                self.csend[slot + 1, rows, :] = both[:, 128:]

            self.compute(self.cols(k, 0, 1 - self.c), self.cols(k, 1, 1 - self.c), put)
            for side in range(2):
                c = self.s.make(2 * k + side, self.csend.at[slot + side], self.crecv.at[2 * k + side], self.pair)
                c.start()
                sent.append(c)
            yield
        self.s.made += sent

    def along(self):
        s, acc, xr = self.s, self.crecv, self.xr
        for k in self.ORDER:
            for side in range(2):
                s.got(2 * k + side, acc.at[2 * k + side], self.pair)

            def put(rows, both):
                acc[2 * k, rows, :] = acc[2 * k, rows, :] + both[:, :128]
                acc[2 * k + 1, rows, :] = acc[2 * k + 1, rows, :] + both[:, 128:]

            self.compute(self.cols(k, 0, self.c), self.cols(k, 1, self.c), put)
            if k == 2:
                s.go(8, acc.at[5], xr.at[0], self.right)
                s.go(9, acc.at[4], xr.at[1], self.left)
            if k == 1:
                s.go(10, acc.at[2], xr.at[2], self.right)
            if k == 3:
                s.go(11, acc.at[7], xr.at[3], self.left)
            yield

    def second(self):
        s, acc, xr = self.s, self.crecv, self.xr
        n = acc.shape[1]
        s.got(8, xr.at[0], self.left)
        add_rows(xr.at[0], lambda r: acc[3, pl.ds(r, 16), :], n)
        s.go(12, xr.at[0], xr.at[4], self.right)
        s.got(9, xr.at[1], self.right)
        add_rows(xr.at[1], lambda r: acc[6, pl.ds(r, 16), :], n)
        s.go(13, xr.at[1], xr.at[5], self.left)

    def third(self):
        s, acc, xr = self.s, self.crecv, self.xr
        n = acc.shape[1]
        s.got(10, xr.at[2], self.left)
        s.got(13, xr.at[5], self.right)
        add_rows(acc.at[0], lambda r: xr[2, pl.ds(r, 16), :] + xr[5, pl.ds(r, 16), :], n)
        s.got(11, xr.at[3], self.right)
        s.got(12, xr.at[4], self.left)
        add_rows(acc.at[1], lambda r: xr[3, pl.ds(r, 16), :] + xr[4, pl.ds(r, 16), :], n)
        s.go(14, acc.at[1 - self.y], self.yr, self.far)

    def finish(self, out_ref):
        self.s.got(14, self.yr, self.far)
        n = self.yr.shape[0]

        def one(i, _):
            r = pl.ds(pl.multiple_of(i * 16, 16), 16)
            out_ref[r, :] = self.crecv[self.y, r, :] + self.yr[r, :]
            return 0

        lax.fori_loop(0, n // 16, one, 0)
        self.s.drain()


def together(sc, dp):
    steps, cores, along = sc.middle(), dp.cores(), dp.along()
    run(cores, 2)
    run(steps, 2)
    run(along, 1)
    run(cores)
    run(steps, 1)
    run(along, 2)
    run(steps, 1)
    run(along)
    run(steps)


def dp_scratch(n, slots=8):
    return [pltpu.VMEM((slots, n, 128), F32), pltpu.VMEM((8, n, 128), F32), pltpu.VMEM((6, n, 128), F32), pltpu.VMEM((n, 128), F32),
            pltpu.SemaphoreType.DMA((15,)), pltpu.SemaphoreType.DMA((15,))]


def params(cid, mib):
    return pltpu.CompilerParams(collective_id=cid, has_side_effects=True, vmem_limit_bytes=mib * 2 ** 20)


VM = pl.BlockSpec(memory_space=pltpu.VMEM)
ANY = pl.BlockSpec(memory_space=pl.ANY)


def decay_rows(dlog_ref, dbias_ref):
    lane = lax.broadcasted_iota(jnp.int32, (1, L), 1)

    def place(ref):
        return jnp.where(lane == 2, ref[0:1, 0:1], jnp.where(lane == 3, ref[0:1, 1:2], 0.0))

    return jnp.where((lane == 2) | (lane == 3), -jnp.exp(place(dlog_ref)), 0.0), place(dbias_ref)


def doc_masks(segpad, base, n, ahead):
    s = segpad[pl.ds(base + (PAD if ahead else 0), n + PAD), :]
    if ahead:
        return [(s[k:k + n] == s[:n]).astype(F32) for k in range(1, 4)]
    return [(s[PAD - k:PAD - k + n] == s[PAD:]).astype(F32) for k in range(1, 4)]


def conv_block(base, pre_ref, taps_ref, cols, masks, n=L):
    z = pre_ref[pl.ds(base, n + PAD), cols]
    total = z[PAD:] * taps_ref[0:1, cols]
    for k in range(1, 4):
        total = total + z[PAD - k:PAD - k + n] * (masks[k - 1] * taps_ref[k:k + 1, cols])
    return total


def inverse_many(mats):
    r = lax.broadcasted_iota(jnp.int32, (L, L), 0)
    c = lax.broadcasted_iota(jnp.int32, (L, L), 1)
    eye = (r == c).astype(F32)
    xs = [eye - jnp.where((r // 2 == c // 2), a, 0.0) for a in mats]
    s = 2
    while s < L:
        pick = (r // (2 * s) == c // (2 * s)) & (r // s != c // s)
        sx = [split(x) for x in xs]
        sa = [split(jnp.where(pick, a, 0.0)) for a in mats]
        t = [mm3(x, a) for x, a in zip(sx, sa)]
        xs = [x - mm3(split(y), z) for x, y, z in zip(xs, t, sx)]
        s *= 2
    return xs


PARTS = 3


def place_of(t, g):
    return t * 96 + g * 32


def natural_of(t, g):
    return g * 256 + t * 32


def front_kernel(blocks, x_ref, again_ref, wq_any, wk_any, wv_any, wt_any, wba_any, wout_any, segments_ref, cq_ref, ck_ref, cv_ref,
                 dlog_ref, dbias_ref, gain_ref, fgain_ref,
                 hidmid_ref, resid_ref, *rest):
    outs, rest = rest[:23], rest[23:]
    saved, rest = rest[:23], rest[23:]
    (hid, low_ref, qpad, kpad, vpad, segpad, gp_ref, ba_ref, q_ref, k_ref, x_s, u_ref, s_ref, o_ref,
     fq, fk, fv, pp, kkp, db, z_s, cols_s, brow) = saved
    wq, wk, wv, wt, wba, wout, w_s, kw_s, seg_ref, state, wsem, osem = rest[:12]
    parts, wholes, rest = rest[12:15], rest[15:18], rest[18:]
    T = blocks * L
    span = T // PARTS
    own = span // NT_
    group = span // L
    fetch = [pltpu.make_async_copy(src, dst, wsem.at[i]) for i, (src, dst) in enumerate(
        ((wq_any, wq), (wk_any, wk), (wv_any, wv), (wt_any, wt), (wba_any, wba), (wout_any, wout)))]
    leave = [pltpu.make_async_copy(src, dst, osem.at[i]) for i, (src, dst) in enumerate(zip(saved, outs))]
    for f in fetch:
        f.start()
    rate, bias = decay_rows(dlog_ref, dbias_ref)
    ring = Ring()
    scatters = [Scatter(ring, parts[g], rest[7 * g:7 * g + 7], own) for g in range(PARTS)]
    gathers = [Gather(ring, wholes[g], rest[7 * PARTS + 2 * g:7 * PARTS + 2 * g + 2], own, 384) for g in range(PARTS)]
    for pad in (qpad, kpad, vpad):
        pad[0:PAD, :] = jnp.zeros((PAD, pad.shape[1]), F32)
    segpad[0:PAD, :] = jnp.full((PAD, L), -1.0, F32)
    segpad[PAD + T:, :] = jnp.full((PAD, L), -1.0, F32)
    for b in range(blocks):
        seg_ref[b, 0:1, :] = segments_ref[0:1, b * L:(b + 1) * L].astype(F32)
        seg_ref[b, 1:2, :] = jnp.broadcast_to(segments_ref[0:1, max(b * L - 1, 0):max(b * L - 1, 0) + 1].astype(F32), (1, L))
        segpad[PAD + b * L:PAD + (b + 1) * L, :] = jnp.broadcast_to(seg_ref[b, 0:1, :], (L, L)).T
    state[...] = jnp.zeros_like(state)

    def project(g):
        def norm(i, _):
            r = pl.ds(pl.multiple_of(g * span + i * 32, 32), 32)
            v = x_ref[r, :].astype(F32)
            n = v * lax.rsqrt(jnp.mean(v * v, axis=-1, keepdims=True) + 1e-05)
            hid[r, :] = (n * again_ref[0:1, :]).astype(BF16)
            return 0

        lax.fori_loop(0, span // 32, norm, 0)
        for i, (w, dst, lead) in enumerate(((wq, qpad, PAD), (wk, kpad, PAD), (wv, vpad, PAD), (wt, gp_ref, 0), (wba, ba_ref, 0))):
            if g == 0:
                fetch[i].wait()
            dst[g * span + lead:(g + 1) * span + lead, :] = mm1(hid[g * span:(g + 1) * span, :], w[...], NT if w is wba else NN)

    def phase_a(g):
        a_mats, keepers = [], []
        for i in range(group):
            b = g * group + i
            base = b * L
            here = pl.ds(base, L)
            per_head, strict_keep, _u = block_decay(b, seg_ref, ba_ref, rate, bias)
            masks = doc_masks(segpad, base, L, False)
            for h in range(2):
                decay, carry, beta_row, beta_col, last_decay = per_head[h]
                kc = slice(h * 128, h * 128 + 128)
                vc = slice(h * 256, h * 256 + 256)
                y = conv_block(base, qpad, cq_ref, kc, masks)
                sg = sigmoid(y)
                q = y * sg
                r = lax.rsqrt(jnp.sum(q * q, axis=-1, keepdims=True) + 1e-06) * (128 ** -0.5)
                q_ref[here, kc] = q * r
                fq[here, kc] = r * (sg + q * (1.0 - sg))
                y = conv_block(base, kpad, ck_ref, kc, masks)
                sg = sigmoid(y)
                k = y * sg
                r = lax.rsqrt(jnp.sum(k * k, axis=-1, keepdims=True) + 1e-06)
                fk[here, kc] = r * (sg + k * (1.0 - sg))
                k = k * r
                k_ref[here, kc] = k
                halves = []
                for j in range(2):
                    c = slice(h * 256 + j * 128, h * 256 + j * 128 + 128)
                    y = conv_block(base, vpad, cv_ref, c, masks)
                    sg = sigmoid(y)
                    v = y * sg
                    fv[here, c] = sg + v * (1.0 - sg)
                    halves.append(v)
                ks = split(k)
                kk = jnp.where(strict_keep, decay, 0.0) * mm3(ks, ks, NT)
                kkp[here, kc] = kk
                a_mats.append(kk * beta_row)
                kw_s[here, kc] = k * (last_decay * beta_col)
                keepers.append((here, kc, vc, jnp.concatenate(halves, axis=1), k * carry))
        xs = inverse_many(a_mats)
        for x, (here, kc, vc, v, gk) in zip(xs, keepers):
            x_s[here, kc] = x
            sx = split(x)
            u_ref[here, vc] = mm3(sx, split(v))
            w_s[here, kc] = mm3(sx, split(gk))

    def phase_b(b, _):
        base = pl.multiple_of(b * L, L)
        here = pl.ds(base, L)
        per_head, strict_keep, _u = block_decay(b, seg_ref, ba_ref, rate, bias)
        for h in range(2):
            decay, carry, beta_row, beta_col, last_decay = per_head[h]
            kc = slice(h * 128, h * 128 + 128)
            vc = slice(h * 256, h * 256 + 256)
            s = state[h]
            s_ref[here, vc] = s
            u = u_ref[here, vc] - mm3(split(w_s[here, kc]), split(s))
            u_ref[here, vc] = u
            state[h] = carry[L - 1:L, :] * s + mm3(split(kw_s[here, kc]), split(u), TN)
        return 0

    def phase_c(b, _):
        base = pl.multiple_of(b * L, L)
        here = pl.ds(base, L)
        per_head, strict_keep, _u = block_decay(b, seg_ref, ba_ref, rate, bias)
        for h in range(2):
            decay, carry, beta_row, beta_col, last_decay = per_head[h]
            kc = slice(h * 128, h * 128 + 128)
            vc = slice(h * 256, h * 256 + 256)
            q = q_ref[here, kc]
            qk = decay * mm3(split(q), split(k_ref[here, kc]), NT)
            pp[here, kc] = qk
            o = mm3(split(q * carry), split(s_ref[here, vc])) + mm3(split(qk * beta_row), split(u_ref[here, vc]))
            o_ref[here, vc] = o
            gp = gp_ref[here, vc]
            n = o * lax.rsqrt(jnp.mean(o * o, axis=-1, keepdims=True) + 1e-05)
            low_ref[here, vc] = (n * gain_ref[0:1, :] * (gp * sigmoid(gp))).astype(BF16)
        return 0

    def mix(g):
        phase_a(g)
        lax.fori_loop(g * group, (g + 1) * group, phase_b, 0)
        lax.fori_loop(g * group, (g + 1) * group, phase_c, 0)
        if g == 0:
            fetch[5].wait()

        def partial(n, _):
            c = pl.ds(pl.multiple_of(n * 512, 512), 512)
            parts[g][:, c] = mm1(low_ref[g * span:(g + 1) * span, :], wout[:, c], NN)
            return 0

        lax.fori_loop(0, wout.shape[1] // 512, partial, 0)
        for k in Scatter.ORDER:
            scatters[g].start(k)

    def normed(g):
        sc, whole = scatters[g], wholes[g]
        sc.finish()

        def finish(i, _):
            r = pl.multiple_of(i * 16, 16)
            at = pl.multiple_of(ring.t * own + r, 16)
            resid = x_ref[pl.ds(pl.multiple_of(g * span + at, 16), 16), :].astype(F32) + sc.value(r)
            resid_ref[pl.ds(pl.multiple_of(g * own + r, 16), 16), :] = resid
            n = resid * lax.rsqrt(jnp.mean(resid * resid, axis=-1, keepdims=True) + 1e-05)
            whole[pl.ds(at, 16), :] = (n * fgain_ref[0:1, :]).astype(BF16).astype(F32)
            return 0

        lax.fori_loop(0, own // 16, finish, 0)
        gathers[g].start()

    def prepare(b, _):
        base = pl.multiple_of(b * L, L)
        here = pl.ds(base, L)
        per_head, strict_keep, _u = block_decay(b, seg_ref, ba_ref, rate, bias)
        lane = lax.broadcasted_iota(jnp.int32, (L, L), 1)
        row = lax.broadcasted_iota(jnp.int32, (8, L), 0)
        tile, flat = jnp.zeros((L, L), F32), jnp.zeros((8, L), F32)
        for h in range(2):
            decay, carry, beta_row, beta_col, last_decay = per_head[h]
            kc = slice(h * 128, h * 128 + 128)
            db[here, kc] = decay * beta_row
            z_s[here, kc] = mm3(split(x_s[here, kc]), split(kw_s[here, kc]), TN)
            tile = tile + (jnp.where(lane == h, carry, 0.0) + jnp.where(lane == 2 + h, last_decay * beta_col, 0.0)
                           + jnp.where(lane == 4 + h, last_decay, 0.0))
            flat = flat + jnp.where(row == h, beta_row, 0.0)
        cols_s[here, :] = tile
        brow[b] = flat
        return 0

    def cast(g):
        def one(t, _):
            r = pl.multiple_of(t * own, own)
            hidmid_ref[pl.ds(pl.multiple_of(place_of(t, g), own), own), :] = wholes[g][pl.ds(r, own), :].astype(BF16)
            return 0

        lax.fori_loop(0, NT_, one, 0)

    first, second, third = (sc.middle() for sc in scatters)
    project(0)
    greet([ring.right, ring.left, ring.flip])
    mix(0)
    project(1)
    mix(1)
    run(first, 2)
    project(2)
    for i in (0, 2, 3, 4, 5, 6, 7):
        leave[i].start()
    mix(2)
    for i in (1, 8, 9, 10, 11, 12, 13, 14, 15, 16, 17, 18):
        leave[i].start()
    run(first)
    run(second, 2)
    lax.fori_loop(0, blocks, prepare, 0)
    for i in range(19, 23):
        leave[i].start()
    normed(0)
    run(second)
    run(third, 2)
    normed(1)
    ahead = [ga.middle() for ga in gathers]
    run(ahead[0], 1)
    run(third)
    run(ahead[0])
    run(ahead[1], 1)
    normed(2)
    run(ahead[1])
    run(ahead[2])
    for g in range(PARTS):
        gathers[g].finish()
        cast(g)
    for c in scatters + gathers:
        c.s.drain()
    for c in leave:
        c.wait()


def front(x, again, wq, wk, wv, wt, wba, wout, segments, cq, ck, cv, dlog, dbias, gain, fgain):
    T, D = x.shape
    blocks = T // L
    own, span = T // NT_, T // PARTS
    sd = jax.ShapeDtypeStruct
    saved = [((T, D), BF16), ((T, 512), BF16), ((T + PAD, 256), F32), ((T + PAD, 256), F32), ((T + PAD, 512), F32), ((T + 2 * PAD, L), F32),
             ((T, 512), F32), ((T, 128), F32), ((T, 256), F32), ((T, 256), F32), ((T, 256), F32), ((T, 512), F32), ((T, 512), F32), ((T, 512), F32),
             ((T, 256), F32), ((T, 256), F32), ((T, 512), F32), ((T, 256), F32), ((T, 256), F32), ((T, 256), F32), ((T, 256), F32),
             ((T, 128), F32), ((blocks, 8, L), F32)]
    vm = lambda s, t: pltpu.VMEM(s, t)
    scratch = [vm(*s) for s in saved] + [vm(w.shape, BF16) for w in (wq, wk, wv, wt, wba, wout)]
    scratch += [vm((T, 256), F32), vm((T, 256), F32), vm((blocks, 8, L), F32), vm((2, 128, 256), F32),
                pltpu.SemaphoreType.DMA((6,)), pltpu.SemaphoreType.DMA((23,))]
    scratch += [vm((span, D), F32)] * (2 * PARTS)
    for _ in range(PARTS):
        scratch += scatter_scratch(span // NT_)
    for _ in range(PARTS):
        scratch += gather_sems()
    return pl.pallas_call(
        functools.partial(front_kernel, blocks),
        out_shape=[sd((T, D), BF16), sd((own, D), F32)] + [sd(*s) for s in saved],
        in_specs=[VM, VM] + [ANY] * 6 + [VM] * 8, out_specs=[VM, VM] + [ANY] * 23,
        scratch_shapes=scratch,
        compiler_params=params(1, 62),
        name="front",
    )(x, again, wq, wk, wv, wt, wba, wout, segments, cq, ck, cv, dlog, dbias, gain, fgain)


SMALL = 40
TAPS = 40


BACK = ("ga", "wout", "low", "ffn", "o", "gp", "pp", "x", "q", "cols", "brow", "k", "z", "u", "s", "db", "kkp", "ba",
        "qpad", "kpad", "vpad", "segpad", "fq", "fk", "fv")


def bwd_kernel(blocks, *refs):
    count = len(BACK)
    sources, rest = refs[:count], refs[count:]
    (resid_ref, cq_ref, ck_ref, cv_ref, dlog_ref, dbias_ref, gain_ref,
     dqp_ref, dkp_ref, dvp_ref, dgp_ref, dba_ref, dtap_ref, dgain_ref, oshard_ref, grads_ref) = rest[:16]
    held, rest = rest[16:16 + count], rest[16 + count:]
    fsem, gm_ref, do_s, y_s, ds_s, dq_s, dk_s, left, tap_s = rest[:9]
    rest = rest[9:]
    (ga_ref, wout_ref, low_ref, ffn_ref, o_ref, gp_ref, pp, x_ref, q_ref, cols_s, brow, k_ref, z_s, u_ref, s_ref, db, kkp, ba_ref,
     qpad, kpad, vpad, segpad, fq, fk, fv) = held
    fetch = [pltpu.make_async_copy(src, dst, fsem.at[i]) for i, (src, dst) in enumerate(zip(sources, held))]
    for c in fetch:
        c.start()

    def need(first, last):
        for c in fetch[first:last]:
            c.wait()

    T = blocks * L
    scr, dscr = rest[:7], rest[7:]
    own = resid_ref.shape[0]
    ring = Ring()

    def compute(a, b, put):
        put(slice(0, 512), mm1(left[...], jnp.concatenate([ga_ref[:, a], ga_ref[:, b]], axis=1), NN))

    dp = DpScatter(ring, dscr, compute)
    greet([ring.right, ring.left, ring.flip] + dp.devices())
    sc = Scatter(ring, ffn_ref, scr, own, sources[3])
    for k in sc.ORDER:
        sc.start(k)
    need(0, 3)
    left[...] = low_ref[...].T
    steps, cores, along = sc.middle(), dp.cores(), dp.along()
    run(cores)

    def mixed_back(i, _):
        r = pl.ds(pl.multiple_of(i * 256, 256), 256)
        gm_ref[r, :] = mm1(ga_ref[r, :], wout_ref[...], NT)
        return 0

    lax.fori_loop(0, T // 256, mixed_back, 0)
    run(along, 1)
    need(3, 4)
    run(steps, 2)
    run(along)
    need(4, 11)
    rate, bias = decay_rows(dlog_ref, dbias_ref)
    dgain_ref[...] = jnp.zeros_like(dgain_ref)
    dtap_ref[32:40, :] = jnp.zeros((8, 128), F32)
    tap_s[...] = jnp.zeros_like(tap_s)

    def phase_1(b, _):
        base = pl.multiple_of(b * L, L)
        for h in range(2):
            carry = cols_s[pl.ds(base, L), h:h + 1]
            kc = slice(h * 128, h * 128 + 128)
            vc = slice(h * 256, h * 256 + 256)
            o = o_ref[pl.ds(base, L), vc]
            gp = gp_ref[pl.ds(base, L), vc]
            gm = gm_ref[pl.ds(base, L), vc]
            gain = gain_ref[0:1, :]
            sg = sigmoid(gp)
            r = lax.rsqrt(jnp.mean(o * o, axis=-1, keepdims=True) + 1e-05)
            n = o * r
            act = gp * sg
            gn = gm * n
            dgain_ref[0:1, :] = dgain_ref[0:1, :] + jnp.sum(gn * act, axis=0, keepdims=True)
            dgp_ref[pl.ds(base, L), vc] = (gn * gain * (sg + act * (1.0 - sg))).astype(BF16)
            dn = gm * gain * act
            do = r * (dn - n * jnp.mean(dn * n, axis=-1, keepdims=True))
            do_s[pl.ds(base, L), vc] = do
            q = q_ref[pl.ds(base, L), kc]
            p = pp[pl.ds(base, L), kc] * brow[b, h:h + 1, :]
            sdo = split(do)
            sx = split(x_ref[pl.ds(base, L), kc])
            y0 = mm3(sx, split(mm3(split(p), sdo, TN)), TN)
            y_s[pl.ds(base, L), vc] = y0
            ds_s[pl.ds(base, L), vc] = mm3(split(q * carry), sdo, TN)
        return 0

    lax.fori_loop(0, blocks // 2, phase_1, 0)
    run(steps, 1)
    lax.fori_loop(blocks // 2, blocks, phase_1, 0)
    run(steps, 1)
    dp.second()
    need(11, 13)

    def phase_2(i, grads):
        b = blocks - 1 - i
        base = pl.multiple_of(b * L, L)
        new = []
        for h in range(2):
            carry = cols_s[pl.ds(base, L), h:h + 1]
            kc = slice(h * 128, h * 128 + 128)
            vc = slice(h * 256, h * 256 + 256)
            ds = grads[h]
            kept = ds_s[pl.ds(base, L), vc]
            ds_s[pl.ds(base, L), vc] = ds
            y = y_s[pl.ds(base, L), vc] + mm3(split(z_s[pl.ds(base, L), kc]), split(ds))
            y_s[pl.ds(base, L), vc] = y
            new.append(carry[L - 1:L, :] * ds + kept
                       - mm3(split(k_ref[pl.ds(base, L), kc] * carry), split(y), TN))
        return tuple(new)

    zero = jnp.zeros((128, 256), F32)
    lax.fori_loop(0, blocks, phase_2, (zero, zero))
    run(steps)
    dp.third()
    need(13, 18)

    def phase_3(b, _):
        base = pl.multiple_of(b * L, L)
        lane = lax.broadcasted_iota(jnp.int32, (L, L), 1)
        rowi = lax.broadcasted_iota(jnp.int32, (L, L), 0)
        row_tile = jnp.zeros((L, L), F32)
        col_tile = jnp.zeros((L, L), F32)
        for h in range(2):
            carry, weight, last_decay = (cols_s[pl.ds(base, L), j:j + 1] for j in (h, 2 + h, 4 + h))
            beta_row = brow[b, h:h + 1, :]
            kc = slice(h * 128, h * 128 + 128)
            vc = slice(h * 256, h * 256 + 256)
            q, k = q_ref[pl.ds(base, L), kc], k_ref[pl.ds(base, L), kc]
            sq, sk = split(q), split(k)
            decay_beta = db[pl.ds(base, L), kc]
            s, u = s_ref[pl.ds(base, L), vc], u_ref[pl.ds(base, L), vc]
            do, y, ds = do_s[pl.ds(base, L), vc], y_s[pl.ds(base, L), vc], ds_s[pl.ds(base, L), vc]
            ss, su, sdo, sy, sds = split(s), split(u), split(do), split(y), split(ds)
            do_st = mm3(sdo, ss, NT)
            y_st = mm3(sy, ss, NT)
            u_dst = mm3(su, sds, NT)
            dp = mm3(sdo, su, NT)
            da = -mm3(sy, su, NT)
            dcarry = jnp.sum(q * do_st - k * y_st, axis=-1, keepdims=True)
            dcarry_last = jnp.sum(jnp.sum(ds * s, axis=0, keepdims=True), axis=1, keepdims=True)
            dw = jnp.sum(u_dst * k, axis=-1, keepdims=True)
            dqk = dp * decay_beta
            dkk = jnp.where(rowi > lane, da * decay_beta, 0.0)
            prod = dp * pp[pl.ds(base, L), kc] + da * kkp[pl.ds(base, L), kc]
            dbeta_row = jnp.sum(prod, axis=0, keepdims=True)
            dec_grad = prod * beta_row
            dc_col = jnp.sum(dec_grad, axis=1, keepdims=True) + dcarry * carry
            dc_row = -jnp.sum(dec_grad, axis=0, keepdims=True)
            dlast = dw * weight
            row1 = rowi[:, 0:1]
            dc_col = dc_col - dlast
            dc_col = dc_col + jnp.where(row1 == L - 1, jnp.sum(dlast, axis=0, keepdims=True) + dcarry_last * carry, 0.0)
            dbeta_col = dw * last_decay
            row_tile = row_tile + jnp.where(rowi == h, dbeta_row, 0.0) + jnp.where(rowi == 2 + h, dc_row, 0.0)
            col_tile = col_tile + jnp.where(lane == h, dbeta_col, 0.0) + jnp.where(lane == 2 + h, dc_col, 0.0)
            sdqk, sdkk = split(dqk), split(dkk + dkk.T)
            dq_s[pl.ds(base, L), kc] = carry * do_st + mm3(sdqk, sk)
            dk_s[pl.ds(base, L), kc] = (mm3(sdqk, sq, TN) + mm3(sdkk, sk) - carry * y_st
                                        + weight * u_dst)
        grad = col_tile + row_tile.T
        dld = tri_sum(grad, TN)
        ba = rows(ba_ref, b)
        tile = decay_tile(ba, rate, bias)
        sig_alpha = sigmoid(ba + bias)
        dalpha = dld * rate * sig_alpha
        dpre = jnp.where(lane < 2, grad * tile * (1.0 - tile), jnp.where(lane < 4, dalpha, 0.0))
        dba_ref[pl.ds(base, L), :] = dpre.astype(BF16)
        dtap_ref[32:33, :] = dtap_ref[32:33, :] + jnp.sum(dpre, axis=0, keepdims=True)
        dtap_ref[33:34, :] = dtap_ref[33:34, :] + jnp.sum(dld * tile, axis=0, keepdims=True)
        return 0

    lax.fori_loop(0, blocks, phase_3, 0)

    need(18, count)

    R = 64
    groups = []
    for h in range(2):
        c = slice(h * 128, h * 128 + 128)
        groups.append((qpad, cq_ref, dq_s, dqp_ref, fq, c, h * 128, q_ref, 128.0))
        groups.append((kpad, ck_ref, dk_s, dkp_ref, fk, c, 256 + h * 128, k_ref, 1.0))
    for j in range(4):
        groups.append((vpad, cv_ref, y_s, dvp_ref, fv, slice(j * 128, j * 128 + 128), 512 + j * 128, None, None))
    for src in (dq_s, dk_s, y_s):
        src[T:, :] = jnp.zeros((PAD, src.shape[1]), F32)

    def conv_back(i, _):
        base = pl.multiple_of((T // R - 1 - i) * R, R)
        here = pl.ds(base, R)
        behind, ahead = doc_masks(segpad, base, R, False), doc_masks(segpad, base, R, True)
        for pre, taps, src, out_ref, factor, c, tc, unit, size in groups:
            d = src[here, c]
            if unit is not None:
                v = unit[here, c]
                d = d - v * (size * jnp.sum(d * v, axis=-1, keepdims=True))
            dy = factor[here, c] * d
            src[here, c] = dy
            z = pre[pl.ds(base, R + PAD), c]
            both = src[pl.ds(base, R + PAD), c]
            tc = slice(tc, tc + 128)
            total = dy * taps[0:1, c]
            tap_s[0, :, tc] = tap_s[0, :, tc] + jnp.sum((dy * z[PAD:]).reshape(R // 8, 8, 128), axis=0)
            for t in range(1, 4):
                total = total + both[t:t + R] * (ahead[t - 1] * taps[t:t + 1, c])
                tap_s[t, :, tc] = tap_s[t, :, tc] + jnp.sum((dy * (z[PAD - t:PAD - t + R] * behind[t - 1])).reshape(R // 8, 8, 128), axis=0)
            out_ref[here, c] = total.astype(BF16)
        return 0

    lax.fori_loop(0, T // R, conv_back, 0)
    for t in range(4):
        for j in range(8):
            dtap_ref[t * 8 + j:t * 8 + j + 1, :] = jnp.sum(tap_s[t, :, j * 128:(j + 1) * 128], axis=0, keepdims=True)
    sc.finish()

    def finish(i, _):
        r = pl.ds(pl.multiple_of(i * 16, 16), 16)
        oshard_ref[r, :] = (resid_ref[r, :] + sc.value(pl.multiple_of(i * 16, 16))).astype(BF16).astype(F32)
        return 0

    lax.fori_loop(0, own // 16, finish, 0)
    dp.finish(grads_ref)
    sc.s.drain()


def mixer_bwd(resid, cq, ck, cv, dlog, dbias, gain, **held):
    T, D = held["ga"].shape
    blocks = T // L
    own = resid.shape[0]
    n = held["low"].shape[1]
    sd = jax.ShapeDtypeStruct
    vm = lambda *r: pltpu.VMEM(r, F32)
    return pl.pallas_call(
        functools.partial(bwd_kernel, blocks),
        out_shape=(sd((T, 256), BF16), sd((T, 256), BF16), sd((T, 512), BF16), sd((T, 512), BF16), sd((T, 128), BF16),
                   sd((TAPS, 128), F32), sd((8, 256), F32), sd((own, D), F32), sd((n, 128), F32)),
        in_specs=[ANY] * len(BACK) + [VM] * 7, out_specs=[VM] * 9,
        scratch_shapes=[pltpu.VMEM(held[name].shape, held[name].dtype) for name in BACK]
        + [pltpu.SemaphoreType.DMA((len(BACK),)), vm(T, 512), vm(T, 512), vm(T + PAD, 512), vm(T, 512), vm(T + PAD, 256), vm(T + PAD, 256),
           pltpu.VMEM((n, T), BF16), vm(4, 8, 1024)] + scatter_scratch(own) + dp_scratch(n, 4),
        compiler_params=params(4, 62),
        name="mixer_backward",
    )(*[held[name] for name in BACK], resid, cq, ck, cv, dlog, dbias, gain)


def in_places(source, dest, sems):
    return [pltpu.make_async_copy(source.at[pl.ds(natural_of(t, g), 32)], dest.at[pl.ds(place_of(t, g), 32)], sems.at[t * PARTS + g])
            for t in range(NT_) for g in range(PARTS)]


def mid_kernel(wg_ref, wu_ref, wd_any, hid_ref, og_any, resid_any, gain_ref,
               ga_ref, inner_ref, ffn_any, gres_ref, dgain_ref, grads_ref,
               part, whole, left, gg_ref, gu_ref, wd_ref, og_ref, resid_in, csem, gsem_og, *rest):
    scr, gsem, dscr = rest[:7], rest[7:9], rest[9:]
    fetches = [pltpu.make_async_copy(wd_any, wd_ref, csem.at[0]), pltpu.make_async_copy(resid_any, resid_in, csem.at[1])]
    reorder = in_places(og_any, og_ref, gsem_og)
    for f in fetches + reorder:
        f.start()
    ring = Ring()
    own = gres_ref.shape[0]
    n = gg_ref.shape[1]
    mine = ring.rows(0, False, own)

    def compute(a, b, put):
        hid = jnp.concatenate([hid_ref[:, a], hid_ref[:, b]], axis=1)
        put(slice(0, n), mm1(left[0:n, :], hid, NN))
        put(slice(n, 2 * n), mm1(left[n:2 * n, :], hid, NN))

    dp = DpScatter(ring, dscr, compute)
    greet([ring.right, ring.left, ring.flip] + dp.devices())
    sc = Scatter(ring, part, scr, own)
    for k in sc.ORDER:
        quarter = ring.quarter(k, own)
        hid = hid_ref[quarter, :]
        gate = mm1(hid, wg_ref[...], NT)
        up = mm1(hid, wu_ref[...], NT)
        sig = sigmoid(gate)
        act = gate * sig
        inner_ref[quarter, :] = (act * up).astype(BF16)
        if k == 2:
            for f in fetches[:1] + reorder:
                f.wait()
        back = mm1(og_ref[quarter, :], wd_ref[...], NT)
        gg_ref[quarter, :] = (back * up * sig * (1.0 + gate * (1.0 - sig))).astype(BF16)
        gu_ref[quarter, :] = (back * act).astype(BF16)

        def partial(i, _):
            cols = pl.ds(pl.multiple_of(i * 512, 512), 512)
            part[quarter, cols] = mm1(gg_ref[quarter, :], wg_ref[:, cols], NN) + mm1(gu_ref[quarter, :], wu_ref[:, cols], NN)
            return 0

        lax.fori_loop(0, part.shape[1] // 512, partial, 0)
        sc.start(k)
    left[0:n, :] = gg_ref[...].T
    left[n:2 * n, :] = gu_ref[...].T
    together(sc, dp)
    fetches[1].wait()
    sc.finish()
    dgain_ref[...] = jnp.zeros_like(dgain_ref)

    def finish(i, _):
        r = pl.multiple_of(i * 16, 16)
        resid = resid_in[pl.ds(r, 16), :]
        back = sc.value(r)
        scale = lax.rsqrt(jnp.mean(resid * resid, axis=-1, keepdims=True) + 1e-05)
        nn = resid * scale
        bn = back * nn
        dgain_ref[...] = dgain_ref[...] + bn[0:8] + bn[8:16]
        b = back * gain_ref[0:1, :]
        g = og_ref[pl.ds(pl.multiple_of(mine.start + r, 16), 16), :].astype(F32) + scale * (b - nn * jnp.mean(b * nn, axis=-1, keepdims=True))
        gres_ref[pl.ds(r, 16), :] = g
        whole[pl.ds(pl.multiple_of(mine.start + r, 16), 16), :] = g.astype(BF16).astype(F32)
        return 0

    lax.fori_loop(0, own // 16, finish, 0)
    ga = Gather(ring, whole, gsem, own)
    ga.start()
    sc.s.drain()
    steps = ga.middle()
    run(steps, 1)
    dp.second()
    run(steps, 1)

    def down(i, _):
        cols = pl.ds(pl.multiple_of(i * 256, 256), 256)
        part[:, cols] = mm1(inner_ref[...], wd_ref[:, cols], NN)
        return 0

    lax.fori_loop(0, part.shape[1] // 256, down, 0)
    leave = pltpu.make_async_copy(part, ffn_any, csem.at[3])
    leave.start()
    run(steps)
    dp.third()
    ga.finish()

    def cast(i, _):
        t, g = i // PARTS, lax.rem(i, PARTS)
        ga_ref[pl.ds(pl.multiple_of(natural_of(t, g), 32), 32), :] = whole[pl.ds(pl.multiple_of(place_of(t, g), 32), 32), :].astype(BF16)
        return 0

    lax.fori_loop(0, NT_ * PARTS, cast, 0)
    dp.finish(grads_ref)
    leave.wait()
    ga.s.drain()


def mid_exchange(wg, wu, wd, hid, og, resid, gain):
    T, D = og.shape
    own = T // NT_
    m = wg.shape[0]
    sd = jax.ShapeDtypeStruct
    return pl.pallas_call(
        mid_kernel,
        out_shape=(sd((T, D), BF16), sd((T, m), BF16), sd((T, D), F32), sd((own, D), F32), sd((8, D), F32), sd((2 * m, 128), F32)),
        in_specs=[VM, VM, ANY, VM, ANY, ANY, VM], out_specs=[VM, VM, ANY, VM, VM, VM],
        scratch_shapes=[pltpu.VMEM((T, D), F32), pltpu.VMEM((T, D), F32), pltpu.VMEM((2 * m, T), BF16),
                        pltpu.VMEM((T, m), BF16), pltpu.VMEM((T, m), BF16), pltpu.VMEM((m, D), BF16), pltpu.VMEM((T, D), BF16),
                        pltpu.VMEM((own, D), F32), pltpu.SemaphoreType.DMA((4,)), pltpu.SemaphoreType.DMA((NT_ * PARTS,))]
        + scatter_scratch(own) + gather_sems() + dp_scratch(2 * m, 4),
        compiler_params=params(2, 62),
        name="mid_exchange",
    )(wg, wu, wd, hid, og, resid, gain)


def in_kernel(*refs):
    sources, (gres_ref, x_ref, gain_ref, fpart_ref, hgain_ref, taps_ref, oshard_ref), rest = refs[:13], refs[13:20], refs[20:]
    whole, out_whole, grads_ref, gains_out, taps_out = rest[:5]
    held, rest = rest[5:18], rest[18:]
    gq, gk, gv, gt, gba, wq, wk, wv, wt, wba, inner_ref, hid_ref, og_ref = held
    part, shard, left, xown, g_own, g_recv, s_own, s_recv, fsem, csem, ssem, srsem, gsem_og = rest[:13]
    rest = rest[13:]
    scr, gsem, osem, dscr = rest[:7], rest[7:9], rest[9:11], rest[11:]
    loads = [pltpu.make_async_copy(src, dst, fsem.at[i]) for i, (src, dst) in enumerate(zip(sources[:12], held))]
    loads += in_places(sources[12], og_ref, gsem_og)
    ring = Ring()
    own = gres_ref.shape[0]
    mine = ring.rows(0, False, own)
    fetch = [pltpu.make_async_copy(x_ref.at[pl.ds(pl.multiple_of(natural_of(ring.t, g), 32), 32)], xown.at[pl.ds(g * 32, 32)], csem.at[3 + g])
             for g in range(PARTS)]
    for c in fetch:
        c.start()
    place_out = pltpu.make_async_copy(oshard_ref, out_whole.at[mine], csem.at[1])
    place_out.start()
    for c in loads:
        c.start()
    t_peers = [(ring.d, lax.rem(ring.t + j, NT_)) for j in range(1, NT_)]
    d_peers = [(lax.rem(ring.d + j, 16), ring.t) for j in range(1, 16)]
    greet(t_peers + d_peers)
    place_out.wait()
    go = Gather(ring, out_whole, osem, own)
    go.start()
    for c in loads[:10]:
        c.wait()
    sc = Scatter(ring, part, scr, own)
    for k in sc.ORDER:
        quarter = ring.quarter(k, own)

        def chosen(ref):
            return jnp.concatenate([ref[pl.ds(pl.multiple_of(natural_of(ring.at(k) * 2 + y, g), 32), 32), :] for y in range(2) for g in range(PARTS)],
                                   axis=0)

        def partial(i, _):
            rows_w = pl.ds(pl.multiple_of(i * 512, 512), 512)
            total = mm1(chosen(gq), wq[rows_w, :], NT) + mm1(chosen(gk), wk[rows_w, :], NT)
            total = total + mm1(chosen(gv), wv[rows_w, :], NT) + mm1(chosen(gt), wt[rows_w, :], NT)
            part[quarter, rows_w] = total + mm1(chosen(gba), wba[:, rows_w], NN)
            return 0

        lax.fori_loop(0, part.shape[1] // 512, partial, 0)
        sc.start(k)

    def compute(a, b, put):
        hid = jnp.concatenate([hid_ref[:, a], hid_ref[:, b]], axis=1)
        put(slice(0, 768), mm1(left[0:768, :], hid, NN))
        put(slice(768, 1552), mm1(left[768:1552, :], hid, NN))
        put(slice(1552, 2256), mm1(left[1552:, :], jnp.concatenate([og_ref[:, a], og_ref[:, b]], axis=1), NN))

    dp = DpScatter(ring, dscr, compute)
    left[0:256, :] = gq[...].T
    left[256:512, :] = gk[...].T
    left[512:1024, :] = gv[...].T
    left[1024:1536, :] = gt[...].T
    left[1536:1552, :] = gba[...].T[0:16]
    for c in loads[10:]:
        c.wait()
    left[1552:, :] = inner_ref[...].T
    outs = go.middle()
    run(outs, 1)
    together(sc, dp)
    run(outs, 2)
    for c in fetch:
        c.wait()
    sc.finish()
    g_own[...] = jnp.zeros_like(g_own)
    ffn_gain = jnp.sum(fpart_ref[...], axis=0, keepdims=True)
    for j in range(16):
        g_own[16 + j:17 + j, :] = ffn_gain[:, j * 128:(j + 1) * 128]
    for j in range(2):
        g_own[32 + j:33 + j, :] = hgain_ref[0:1, j * 128:(j + 1) * 128]

    def finish(i, total):
        r = pl.multiple_of(i * 16, 16)
        x = xown[pl.ds(r, 16), :].astype(F32)
        back = sc.value(r)
        scale = lax.rsqrt(jnp.mean(x * x, axis=-1, keepdims=True) + 1e-05)
        nn = x * scale
        total = total + jnp.sum(back * nn, axis=0, keepdims=True)
        b = back * gain_ref[0:1, :]
        g = gres_ref[pl.ds(r, 16), :] + scale * (b - nn * jnp.mean(b * nn, axis=-1, keepdims=True))
        shard[pl.ds(r, 16), :] = g.astype(BF16).astype(F32)
        return total

    total = lax.fori_loop(0, own // 16, finish, jnp.zeros((1, x_ref.shape[1]), F32))
    for j in range(16):
        g_own[j:j + 1, :] = total[:, j * 128:(j + 1) * 128]
    place = pltpu.make_async_copy(shard, whole.at[mine], csem.at[2])
    place.start()
    place.wait()
    small = Sends(ssem, srsem)
    for j, dev in enumerate(t_peers):
        small.go(j, g_own, g_recv.at[j], dev)
    ga = Gather(ring, whole, gsem, own)
    ga.start()
    run(outs)
    dp.second()
    steps = ga.middle()
    run(steps, 1)
    for j, dev in enumerate(t_peers):
        small.got(j, g_recv.at[j], dev)
    gains = g_own[...]
    for j in range(NT_ - 1):
        gains = gains + g_recv[j]
    s_own[0:SMALL, :] = gains
    s_own[SMALL:, :] = taps_ref[...]
    for j, dev in enumerate(d_peers):
        small.go(7 + j, s_own, s_recv.at[j], dev)
    run(steps)
    dp.third()
    for j, dev in enumerate(d_peers):
        small.got(7 + j, s_recv.at[j], dev)
    both = s_own[...]
    for j in range(15):
        both = both + s_recv[j]
    gains_out[...] = both[:SMALL]
    taps_out[...] = both[SMALL:]
    go.finish()
    ga.finish()
    dp.finish(grads_ref)
    small.drain()
    go.s.drain()
    sc.s.drain()
    ga.s.drain()


def in_exchange(grads, weights, inner, hid, og, gres, inputs, gain, ffn_part, hgain, taps, oshard):
    T, D = inputs.shape
    own = T // NT_
    n = 1552 + inner.shape[1]
    sd = jax.ShapeDtypeStruct
    vm = lambda *s: pltpu.VMEM(s, F32)
    held = (*grads, *weights, inner, hid, og)
    return pl.pallas_call(
        in_kernel,
        out_shape=(sd((T, D), F32), sd((T, D), F32), sd((n, 128), F32), sd((SMALL, 128), F32), sd((TAPS, 128), F32)),
        in_specs=[ANY] * 13 + [VM, ANY] + [VM] * 5, out_specs=[ANY, ANY, VM, VM, VM],
        scratch_shapes=[pltpu.VMEM(h.shape, h.dtype) for h in held]
        + [vm(T, D), vm(own, D), pltpu.VMEM((n, T), BF16), pltpu.VMEM((own, D), BF16),
           vm(SMALL, 128), vm(7, SMALL, 128), vm(SMALL + TAPS, 128), vm(15, SMALL + TAPS, 128),
           pltpu.SemaphoreType.DMA((12,)), pltpu.SemaphoreType.DMA((3 + PARTS,)), pltpu.SemaphoreType.DMA((22,)), pltpu.SemaphoreType.DMA((22,)),
           pltpu.SemaphoreType.DMA((NT_ * PARTS,))]
        + scatter_scratch(own) + gather_sems() + gather_sems() + dp_scratch(n, 4),
        compiler_params=params(3, 62),
        name="in_exchange",
    )(*held, gres, inputs, gain, ffn_part, hgain, taps, oshard)


def last_kernel(ig_ref, out_ref, gin_ref, gmid_ref, gout_ref, gains_ref, taps_ref,
                ig_low, out_low, gq, gk, gv, gt, gbeta, galpha, cq, ck, cv, dlog, dbias, hgain, again, fgain, gug, gup, gdown, gout):
    for t in range(NT_):
        ig_low[t * 32:(t + 1) * 32, :] = ig_ref[t, 0].astype(BF16)
        out_low[t * 32:(t + 1) * 32, :] = out_ref[t, 0].astype(BF16)

    @pl.when(pl.program_id(0) == 0)
    def _():
        gq[...] = gin_ref[0:256, :].T
        gk[...] = gin_ref[256:512, :].T
        gv[...] = gin_ref[512:1024, :].T
        gt[...] = gin_ref[1024:1536, :].T
        gbeta[...] = gin_ref[1536:1538, :]
        galpha[...] = gin_ref[1538:1540, :]
        gdown[...] = gin_ref[1552:, :]
        n = gug.shape[0]
        gug[...] = gmid_ref[0:n, :]
        gup[...] = gmid_ref[n:, :]
        gout[...] = gout_ref[...]
        for t in range(4):
            for j in range(8):
                row = taps_ref[t * 8 + j:t * 8 + j + 1, :]
                ref, at = ((cq, j), (ck, j - 2), (cv, j - 4))[0 if j < 2 else 1 if j < 4 else 2]
                ref[t:t + 1, at * 128:(at + 1) * 128] = row
        dbias[...] = taps_ref[32:33, 2:4]
        dlog[...] = taps_ref[33:34, 2:4]
        again[...] = gains_ref[0:16, :]
        fgain[...] = gains_ref[16:32, :]
        hgain[...] = gains_ref[32:34, :]


def last(ig, out, gin, gmid, gout, gains, taps):
    T, D = ig.shape
    n = gmid.shape[0] // 2
    sd = lambda *s: jax.ShapeDtypeStruct(s, F32)
    step = lambda: pl.BlockSpec((T // PARTS, D), lambda i: (i, 0))
    shares = lambda: pl.BlockSpec((NT_, 1, 32, D), lambda i: (0, i, 0, 0))
    fixed = lambda s: pl.BlockSpec(s, lambda i: (0, 0))
    small = [sd(128, 256), sd(128, 256), sd(128, 512), sd(128, 512), sd(2, 128), sd(2, 128), sd(4, 256), sd(4, 256), sd(4, 512),
             sd(1, 2), sd(1, 2), sd(2, 128), sd(16, 128), sd(16, 128), sd(n, 128), sd(n, 128), sd(gin.shape[0] - 1552, 128), sd(gout.shape[0], 128)]
    return pl.pallas_call(
        last_kernel,
        grid=(PARTS,),
        out_shape=[jax.ShapeDtypeStruct((T, D), BF16)] * 2 + small,
        in_specs=[shares(), shares()] + [fixed(a.shape) for a in (gin, gmid, gout, gains, taps)],
        out_specs=[step(), step()] + [fixed(a.shape) for a in small],
        compiler_params=pltpu.CompilerParams(vmem_limit_bytes=48 * 2 ** 20),
        name="last",
    )(*(a.reshape(NT_, PARTS, 32, D) for a in (ig, out)), gin, gmid, gout, gains, taps)


def row(v):
    return v.reshape(1, v.shape[0])


def per_device(inputs, segments, attn_gain, w_query, w_key, w_value, w_gate, w_beta, w_alpha, conv_query, conv_key, conv_value,
               decay_log, decay_bias, head_gain, w_out, ffn_gain, w_up_gate, w_up, w_down, out_grad):
    D = inputs.shape[1]
    w_ba = jnp.concatenate([w_beta.T, w_alpha.T, jnp.zeros((124, D), BF16)], axis=0)
    dlog, dbias, hgain = row(decay_log), row(decay_bias), row(head_gain)
    hidden_mid, resid, hidden_in, low, *saved = front(
        inputs, row(attn_gain), w_query, w_key, w_value, w_gate, w_ba, w_out, segments, conv_query, conv_key, conv_value,
        dlog, dbias, hgain, row(ffn_gain))
    names = ("qpad", "kpad", "vpad", "segpad", "gp", "ba", "q", "k", "x", "u", "s", "o", "fq", "fk", "fv", "pp", "kkp", "db", "z", "cols", "brow")
    grad_attn, inner, ffn, grad_resid, ffn_gain_part, grads_mid = mid_exchange(
        w_up_gate.T, w_up.T, w_down, hidden_mid, out_grad, resid, row(ffn_gain))
    *grads, taps, hgain_part, oshard, grads_out = mixer_bwd(
        resid, conv_query, conv_key, conv_value, dlog, dbias, hgain, ga=grad_attn, wout=w_out, low=low, ffn=ffn, **dict(zip(names, saved)))
    ig, out, grads_in, gains, taps = in_exchange(
        grads, (w_query, w_key, w_value, w_gate, w_ba), inner, hidden_in, out_grad, grad_resid, inputs,
        row(attn_gain), ffn_gain_part, hgain_part, taps, oshard)
    (input_grad, outputs, gq, gk, gv, gt, gbeta, galpha, cq, ck, cv, g_dlog, g_dbias, g_hgain, g_again, g_fgain,
     gug, gup, gdown, gout) = last(ig, out, grads_in, grads_mid, grads_out, gains, taps)
    return (outputs, input_grad, g_again.reshape(D), gq, gk, gv, gt, gbeta.T, galpha.T, cq, ck, cv,
            g_dlog.reshape(2), g_dbias.reshape(2), g_hgain.reshape(head_gain.shape), gout, g_fgain.reshape(D), gug.T, gup.T, gdown)


def solution(mesh):
    col, rows_t, rep = P(None, "tensor"), P("tensor", None), P()
    tok, both, head = P("dp", None), P("dp", "tensor"), P("tensor")
    return jax.shard_map(
        per_device,
        mesh=mesh,
        in_specs=(tok, tok, rep, col, col, col, col, col, col, col, col, col, head, head, rep, rows_t, rep, col, col, rows_t, tok),
        out_specs=(tok, tok, rep, both, both, both, both, both, both, col, col, col, head, head, rep, P("tensor", "dp"), rep, both, both, P("tensor", "dp")),
        check_vma=False,
    )
```

```python
import functools
import jax, jax.numpy as jnp
from jax import lax
from jax.experimental import pallas as pl
from jax.experimental.pallas import tpu as pltpu
from jax.sharding import PartitionSpec as P

F32 = jnp.float32
BF16 = jnp.bfloat16
L = 128
PAD = 8
NN = (((1,), (0,)), ((), ()))
NT = (((1,), (1,)), ((), ()))
TN = (((0,), (0,)), ((), ()))


def split(x):
    hi = x.astype(BF16)
    return hi, (x - hi.astype(F32)).astype(BF16)


def mm1(a, b, dims):
    return lax.dot_general(a, b, dims, preferred_element_type=F32)


def mm3(a, b, dims=NN):
    (ia,), (ib,) = dims[0]
    if a[0].shape[ia] > 128:
        return mm1(a[0], b[0], dims) + (mm1(a[0], b[1], dims) + mm1(a[1], b[0], dims))
    return mm1(jnp.concatenate(a, axis=ia), jnp.concatenate([b[0], b[0]], axis=ib), dims) + mm1(a[0], b[1], dims)


def sigmoid(x):
    d = 1.0 + jnp.exp(-jnp.maximum(x, -80.0))
    r = pl.reciprocal(d, approx=True)
    r = r * (2.0 - d * r)
    return r * (2.0 - d * r)


def rows(ref, b, n=L, lead=0):
    return ref[pl.ds(pl.multiple_of(b * L, L) + lead, n)]


def decay_tile(ba, rate, bias):
    lane = lax.broadcasted_iota(jnp.int32, ba.shape, 1)
    shifted = ba + bias
    soft = jnp.maximum(shifted, 0.0) + jnp.log1p(jnp.exp(-jnp.abs(shifted)))
    return jnp.where(lane < 2, sigmoid(ba), rate * soft)


def tri_sum(tile, dims):
    r = lax.broadcasted_iota(jnp.int32, (L, L), 0)
    c = lax.broadcasted_iota(jnp.int32, (L, L), 1)
    tri = (r >= c).astype(BF16)
    p0 = tile.astype(BF16)
    rest = tile - p0.astype(F32)
    p1 = rest.astype(BF16)
    p2 = (rest - p1.astype(F32)).astype(BF16)
    return mm1(tri, p0, dims) + (mm1(tri, p1, dims) + mm1(tri, p2, dims))


def block_decay(b, seg_ref, ba_ref, rate, bias):
    tile = decay_tile(rows(ba_ref, b), rate, bias)
    cum = tri_sum(tile, NN)
    lane = lax.broadcasted_iota(jnp.int32, (L, L), 1)
    both = jnp.where(lane < 2, tile, cum)
    flat = both.T
    seg_row = seg_ref[b, 0:1, :]
    seg_col = jnp.broadcast_to(seg_row, (L, L)).T
    prev = seg_ref[b, 1:2, 0:1]
    r = lax.broadcasted_iota(jnp.int32, (L, L), 0)
    keep = (seg_col == seg_row) & (r >= lane)
    strict_keep = r > lane
    carry_keep = seg_col[:, 0:1] == prev
    out = []
    for h in range(2):
        c_col = cum[:, 2 + h:3 + h]
        c_row = flat[2 + h:3 + h, :]
        beta_row = flat[h:h + 1, :]
        decay = jnp.where(keep, jnp.exp(jnp.where(keep, c_col - c_row, 0.0)), 0.0)
        carry = jnp.where(carry_keep, jnp.exp(c_col), 0.0)
        last_keep = seg_col[:, 0:1] == seg_row[:, L - 1:L]
        last_decay = jnp.where(last_keep, jnp.exp(jnp.where(last_keep, c_col[L - 1:L, :] - c_col, 0.0)), 0.0)
        beta_col = tile[:, h:h + 1]
        out.append((decay, carry, beta_row, beta_col, last_decay))
    return out, strict_keep, (tile, seg_col)


MESH = pl.DeviceIdType.MESH
NT_ = 8
ZH, YH = 512, 512


def run(steps, count=None):
    if count is None:
        for _ in steps:
            pass
    else:
        for _ in range(count):
            next(steps)


class Ring:
    def __init__(self):
        self.d = lax.axis_index("dp")
        self.t = lax.axis_index("tensor")
        self.y = lax.rem(self.t, 2)
        self.z = self.t // 2
        self.right = (self.d, self.at(1) * 2 + self.y)
        self.left = (self.d, self.at(3) * 2 + self.y)
        self.flip = (self.d, self.z * 2 + 1 - self.y)

    def at(self, k):
        return lax.rem(self.z + k, 4)

    def rows(self, k, other, own):
        side = 1 - self.y if other else self.y
        return pl.ds(pl.multiple_of((self.at(k) * 2 + side) * own, own), own)

    def quarter(self, k, own):
        return pl.ds(pl.multiple_of(self.at(k) * 2 * own, 2 * own), 2 * own)


class Sends:
    def __init__(self, ssem, rsem):
        self.ssem, self.rsem, self.made = ssem, rsem, []

    def make(self, i, src, dst, device):
        return pltpu.make_async_remote_copy(src_ref=src, dst_ref=dst, send_sem=self.ssem.at[i], recv_sem=self.rsem.at[i],
                                            device_id=device, device_id_type=MESH)

    def go(self, i, src, dst, device):
        c = self.make(i, src, dst, device)
        c.start()
        self.made.append(c)

    def got(self, i, dst, device):
        self.make(i, dst, dst, device).wait_recv()

    def drain(self):
        for c in self.made:
            c.wait_send()


def greet(devices):
    barrier = pltpu.get_barrier_semaphore()
    for dev in devices:
        pl.semaphore_signal(barrier, inc=1, device_id=dev, device_id_type=MESH)
    pl.semaphore_wait(barrier, len(devices))


ZA, ZB, ZZ = pl.ds(0, ZH), pl.ds(ZH, ZH), pl.ds(0, 2 * ZH)
YA, YB, YY = pl.ds(2 * ZH, YH), pl.ds(2 * ZH + YH, YH), pl.ds(2 * ZH, 2 * YH)
ZLO, ZHI, YLO, YHI = pl.ds(0, ZH), pl.ds(ZH, ZH), pl.ds(0, YH), pl.ds(YH, YH)


def scatter_scratch(own):
    return [pltpu.VMEM((4, own, 2 * YH), F32), pltpu.VMEM((6, 2 * own, ZH), F32), pltpu.VMEM((6, own, YH), F32),
            pltpu.VMEM((own, 2 * ZH), F32), pltpu.VMEM((own, 2 * ZH), F32),
            pltpu.SemaphoreType.DMA((17,)), pltpu.SemaphoreType.DMA((17,))]


def add_rows(dst, src_of, n):
    def one(i, _):
        r = pl.multiple_of(i * 16, 16)
        dst[pl.ds(r, 16), :] = dst[pl.ds(r, 16), :] + src_of(r)
        return 0
    lax.fori_loop(0, n // 16, one, 0)


def sub(ref, rows, cols):
    return lambda r: ref[pl.ds(pl.multiple_of(rows.start + r, 16), 16), cols]


class Scatter:
    def __init__(self, ring, part, scratch, own, source=None):
        self.ring, self.part, self.own = ring, part, own
        self.source = part if source is None else source
        self.yb, self.zb, self.yr, self.zsend, self.zf, ssem, rsem = scratch
        self.s = Sends(ssem, rsem)

    ORDER = (2, 1, 3, 0)

    def start(self, k):
        g, s, p, own = self.ring, self.s, self.source, self.own
        if k == 2:
            s.go(0, p.at[g.quarter(2, own), ZB], self.zb.at[0], g.right)
            s.go(1, p.at[g.quarter(2, own), ZA], self.zb.at[1], g.left)
        if k == 1:
            s.go(2, p.at[g.quarter(1, own), ZA], self.zb.at[2], g.right)
        if k == 3:
            s.go(3, p.at[g.quarter(3, own), ZB], self.zb.at[3], g.left)
        s.go({2: 6, 1: 7, 3: 8, 0: 9}[k], p.at[g.rows(k, True, own), YY], self.yb.at[k], g.flip)

    def middle(self):
        g, s, p, own = self.ring, self.s, self.part, self.own
        yb, zb, yr = self.yb, self.zb, self.yr
        s.got(6, yb.at[2], g.flip)
        add_rows(yb.at[2], sub(p, g.rows(2, False, own), YY), own)
        s.go(10, yb.at[2, :, YHI], yr.at[0], g.right)
        s.go(11, yb.at[2, :, YLO], yr.at[1], g.left)
        yield
        s.got(0, zb.at[0], g.left)
        add_rows(zb.at[0], sub(p, g.quarter(1, own), ZB), 2 * own)
        s.go(4, zb.at[0], zb.at[4], g.right)
        s.got(1, zb.at[1], g.right)
        add_rows(zb.at[1], sub(p, g.quarter(3, own), ZA), 2 * own)
        s.go(5, zb.at[1], zb.at[5], g.left)
        yield
        s.got(7, yb.at[1], g.flip)
        add_rows(yb.at[1], sub(p, g.rows(1, False, own), YY), own)
        s.go(12, yb.at[1, :, YLO], yr.at[2], g.right)
        s.got(10, yr.at[0], g.left)
        add_rows(yr.at[0], lambda r: yb[1, pl.ds(r, 16), YHI], own)
        s.go(14, yr.at[0], yr.at[4], g.right)
        yield
        s.got(8, yb.at[3], g.flip)
        add_rows(yb.at[3], sub(p, g.rows(3, False, own), YY), own)
        s.go(13, yb.at[3, :, YHI], yr.at[3], g.left)
        s.got(11, yr.at[1], g.right)
        add_rows(yr.at[1], lambda r: yb[3, pl.ds(r, 16), YLO], own)
        s.go(15, yr.at[1], yr.at[5], g.left)
        yield
        s.got(2, zb.at[2], g.left)
        s.got(3, zb.at[3], g.right)
        s.got(4, zb.at[4], g.left)
        s.got(5, zb.at[5], g.right)
        base = g.rows(0, True, own).start
        lead = (1 - g.y) * own

        def one(i, _):
            r = pl.multiple_of(i * 16, 16)
            at = pl.ds(pl.multiple_of(lead + r, 16), 16)
            mine = pl.ds(pl.multiple_of(base + r, 16), 16)
            self.zsend[pl.ds(r, 16), ZLO] = p[mine, ZA] + (zb[2, at, :] + zb[5, at, :])
            self.zsend[pl.ds(r, 16), ZHI] = p[mine, ZB] + (zb[3, at, :] + zb[4, at, :])
            return 0

        lax.fori_loop(0, own // 16, one, 0)
        s.go(16, self.zsend, self.zf, g.flip)
        yield

    def finish(self):
        g, s = self.ring, self.s
        s.got(9, self.yb.at[0], g.flip)
        s.got(12, self.yr.at[2], g.left)
        s.got(13, self.yr.at[3], g.right)
        s.got(14, self.yr.at[4], g.left)
        s.got(15, self.yr.at[5], g.right)
        s.got(16, self.zf, g.flip)

    def value(self, r):
        g, p, own = self.ring, self.part, self.own
        zb, yr = self.zb, self.yr
        at = pl.ds(pl.multiple_of(g.y * own + r, 16), 16)
        here = pl.ds(r, 16)
        mine = pl.ds(pl.multiple_of(g.rows(0, False, own).start + r, 16), 16)
        za = p[mine, ZA] + (zb[2, at, :] + zb[5, at, :]) + self.zf[here, ZLO]
        zz = p[mine, ZB] + (zb[3, at, :] + zb[4, at, :]) + self.zf[here, ZHI]
        ya = p[mine, YA] + self.yb[0, here, YLO] + (yr[2, here, :] + yr[5, here, :])
        yz = p[mine, YB] + self.yb[0, here, YHI] + (yr[3, here, :] + yr[4, here, :])
        return jnp.concatenate([za, zz, ya, yz], axis=1)


def gather_sems():
    return [pltpu.SemaphoreType.DMA((17,)), pltpu.SemaphoreType.DMA((17,))]


class Gather:
    def __init__(self, ring, whole, sems, own, yh=256):
        self.ring, self.whole, self.own = ring, whole, own
        zh = whole.shape[1] // 2 - yh
        self.za, self.zb, self.zz = pl.ds(0, zh), pl.ds(zh, zh), pl.ds(0, 2 * zh)
        self.ya, self.yb, self.yy = pl.ds(2 * zh, yh), pl.ds(2 * zh + yh, yh), pl.ds(2 * zh, 2 * yh)
        self.s = Sends(*sems)

    def _go(self, i, rows, cols, device):
        ref = self.whole.at[rows, cols]
        self.s.go(i, ref, ref, device)

    def _got(self, i, rows, cols, device):
        self.s.got(i, self.whole.at[rows, cols], device)

    def start(self):
        g, own = self.ring, self.own
        mine = g.rows(0, False, own)
        self._go(0, mine, self.yy, g.right)
        self._go(1, mine, self.yy, g.left)
        self._go(2, mine, self.zz, g.flip)
        self._go(3, mine, self.zz, g.right)
        self._go(4, mine, self.zz, g.left)
        self._go(5, mine, self.yy, g.flip)

    def middle(self):
        g, own = self.ring, self.own
        lf, rt = g.rows(3, False, own), g.rows(1, False, own)
        lo, ro = g.rows(3, True, own), g.rows(1, True, own)
        far, faro, other = g.rows(2, False, own), g.rows(2, True, own), g.rows(0, True, own)
        self._got(0, lf, self.yy, g.left)
        self._go(6, lf, self.yb, g.right)
        self._go(7, lf, self.yy, g.flip)
        self._got(1, rt, self.yy, g.right)
        self._go(8, rt, self.ya, g.left)
        self._go(9, rt, self.yy, g.flip)
        self._got(2, other, self.zz, g.flip)
        self._go(10, other, self.zz, g.right)
        self._go(11, other, self.zz, g.left)
        yield
        self._got(6, far, self.yb, g.left)
        self._got(8, far, self.ya, g.right)
        self._go(12, far, self.yy, g.flip)
        yield
        self._got(3, lf, self.zz, g.left)
        self._go(13, lf, self.zb, g.right)
        self._got(4, rt, self.zz, g.right)
        self._go(14, rt, self.za, g.left)
        yield
        self._got(10, lo, self.zz, g.left)
        self._go(15, lo, self.zb, g.right)
        self._got(11, ro, self.zz, g.right)
        self._go(16, ro, self.za, g.left)
        yield

    def finish(self):
        g, own = self.ring, self.own
        far, faro, other = g.rows(2, False, own), g.rows(2, True, own), g.rows(0, True, own)
        self._got(5, other, self.yy, g.flip)
        self._got(7, g.rows(3, True, own), self.yy, g.flip)
        self._got(9, g.rows(1, True, own), self.yy, g.flip)
        self._got(12, faro, self.yy, g.flip)
        self._got(13, far, self.zb, g.left)
        self._got(14, far, self.za, g.right)
        self._got(15, faro, self.zb, g.left)
        self._got(16, faro, self.za, g.right)


class DpScatter:
    ORDER = (2, 1, 3, 0)

    def __init__(self, ring, scratch, compute):
        d, t = ring.d, ring.t
        self.c, self.x, self.y = lax.rem(d, 2), lax.rem(d // 2, 4), d // 8
        self.pair = (d + 1 - 2 * self.c, t)
        self.right = ((self.y * 4 + self.step(1)) * 2 + self.c, t)
        self.left = ((self.y * 4 + self.step(3)) * 2 + self.c, t)
        self.far = (((1 - self.y) * 4 + self.x) * 2 + self.c, t)
        self.csend, self.crecv, self.xr, self.yr, ssem, rsem = scratch
        self.s = Sends(ssem, rsem)
        self.compute = compute

    def step(self, k):
        return lax.rem(self.x + k, 4)

    def devices(self):
        return [self.pair, self.right, self.left, self.far]

    def cols(self, k, side, core):
        return pl.ds(pl.multiple_of(((side * 4 + self.step(k)) * 2 + core) * 128, 128), 128)

    def cores(self):
        slots, sent = self.csend.shape[0], []
        for n, k in enumerate(self.ORDER):
            slot = 2 * n % slots
            for c in sent[:2] if 2 * n >= slots else []:
                c.wait_send()
            sent = sent[2:] if 2 * n >= slots else sent

            def put(rows, both):
                self.csend[slot, rows, :] = both[:, :128]
                self.csend[slot + 1, rows, :] = both[:, 128:]

            self.compute(self.cols(k, 0, 1 - self.c), self.cols(k, 1, 1 - self.c), put)
            for side in range(2):
                c = self.s.make(2 * k + side, self.csend.at[slot + side], self.crecv.at[2 * k + side], self.pair)
                c.start()
                sent.append(c)
            yield
        self.s.made += sent

    def along(self):
        s, acc, xr = self.s, self.crecv, self.xr
        for k in self.ORDER:
            for side in range(2):
                s.got(2 * k + side, acc.at[2 * k + side], self.pair)

            def put(rows, both):
                acc[2 * k, rows, :] = acc[2 * k, rows, :] + both[:, :128]
                acc[2 * k + 1, rows, :] = acc[2 * k + 1, rows, :] + both[:, 128:]

            self.compute(self.cols(k, 0, self.c), self.cols(k, 1, self.c), put)
            if k == 2:
                s.go(8, acc.at[5], xr.at[0], self.right)
                s.go(9, acc.at[4], xr.at[1], self.left)
            if k == 1:
                s.go(10, acc.at[2], xr.at[2], self.right)
            if k == 3:
                s.go(11, acc.at[7], xr.at[3], self.left)
            yield

    def second(self):
        s, acc, xr = self.s, self.crecv, self.xr
        n = acc.shape[1]
        s.got(8, xr.at[0], self.left)
        add_rows(xr.at[0], lambda r: acc[3, pl.ds(r, 16), :], n)
        s.go(12, xr.at[0], xr.at[4], self.right)
        s.got(9, xr.at[1], self.right)
        add_rows(xr.at[1], lambda r: acc[6, pl.ds(r, 16), :], n)
        s.go(13, xr.at[1], xr.at[5], self.left)

    def third(self):
        s, acc, xr = self.s, self.crecv, self.xr
        n = acc.shape[1]
        s.got(10, xr.at[2], self.left)
        s.got(13, xr.at[5], self.right)
        add_rows(acc.at[0], lambda r: xr[2, pl.ds(r, 16), :] + xr[5, pl.ds(r, 16), :], n)
        s.got(11, xr.at[3], self.right)
        s.got(12, xr.at[4], self.left)
        add_rows(acc.at[1], lambda r: xr[3, pl.ds(r, 16), :] + xr[4, pl.ds(r, 16), :], n)
        s.go(14, acc.at[1 - self.y], self.yr, self.far)

    def finish(self, out_ref):
        self.s.got(14, self.yr, self.far)
        n = self.yr.shape[0]

        def one(i, _):
            r = pl.ds(pl.multiple_of(i * 16, 16), 16)
            out_ref[r, :] = self.crecv[self.y, r, :] + self.yr[r, :]
            return 0

        lax.fori_loop(0, n // 16, one, 0)
        self.s.drain()


def together(sc, dp):
    steps, cores, along = sc.middle(), dp.cores(), dp.along()
    run(cores, 2)
    run(steps, 2)
    run(along, 1)
    run(cores)
    run(steps, 1)
    run(along, 2)
    run(steps, 1)
    run(along)
    run(steps)


def dp_scratch(n, slots=8):
    return [pltpu.VMEM((slots, n, 128), F32), pltpu.VMEM((8, n, 128), F32), pltpu.VMEM((6, n, 128), F32), pltpu.VMEM((n, 128), F32),
            pltpu.SemaphoreType.DMA((15,)), pltpu.SemaphoreType.DMA((15,))]


def params(cid, mib):
    return pltpu.CompilerParams(collective_id=cid, has_side_effects=True, vmem_limit_bytes=mib * 2 ** 20)


VM = pl.BlockSpec(memory_space=pltpu.VMEM)
ANY = pl.BlockSpec(memory_space=pl.ANY)


def decay_rows(dlog_ref, dbias_ref):
    lane = lax.broadcasted_iota(jnp.int32, (1, L), 1)

    def place(ref):
        return jnp.where(lane == 2, ref[0:1, 0:1], jnp.where(lane == 3, ref[0:1, 1:2], 0.0))

    return jnp.where((lane == 2) | (lane == 3), -jnp.exp(place(dlog_ref)), 0.0), place(dbias_ref)


def doc_masks(segpad, base, n, ahead):
    s = segpad[pl.ds(base + (PAD if ahead else 0), n + PAD), :]
    if ahead:
        return [(s[k:k + n] == s[:n]).astype(F32) for k in range(1, 4)]
    return [(s[PAD - k:PAD - k + n] == s[PAD:]).astype(F32) for k in range(1, 4)]


def conv_block(base, pre_ref, taps_ref, cols, masks, n=L):
    z = pre_ref[pl.ds(base, n + PAD), cols]
    total = z[PAD:] * taps_ref[0:1, cols]
    for k in range(1, 4):
        total = total + z[PAD - k:PAD - k + n] * (masks[k - 1] * taps_ref[k:k + 1, cols])
    return total


def inverse_many(mats):
    r = lax.broadcasted_iota(jnp.int32, (L, L), 0)
    c = lax.broadcasted_iota(jnp.int32, (L, L), 1)
    eye = (r == c).astype(F32)
    xs = [eye - jnp.where((r // 2 == c // 2), a, 0.0) for a in mats]
    s = 2
    while s < L:
        pick = (r // (2 * s) == c // (2 * s)) & (r // s != c // s)
        sx = [split(x) for x in xs]
        sa = [split(jnp.where(pick, a, 0.0)) for a in mats]
        t = [mm3(x, a) for x, a in zip(sx, sa)]
        xs = [x - mm3(split(y), z) for x, y, z in zip(xs, t, sx)]
        s *= 2
    return xs


PARTS = 3


def place_of(t, g):
    return t * 96 + g * 32


def natural_of(t, g):
    return g * 256 + t * 32


def front_kernel(blocks, x_ref, again_ref, wq_any, wk_any, wv_any, wt_any, wba_any, wout_any, segments_ref, cq_ref, ck_ref, cv_ref,
                 dlog_ref, dbias_ref, gain_ref, fgain_ref,
                 hidmid_ref, resid_ref, *rest):
    outs, rest = rest[:23], rest[23:]
    saved, rest = rest[:23], rest[23:]
    (hid, low_ref, qpad, kpad, vpad, segpad, gp_ref, ba_ref, q_ref, k_ref, x_s, u_ref, s_ref, o_ref,
     fq, fk, fv, pp, kkp, db, z_s, cols_s, brow) = saved
    wq, wk, wv, wt, wba, wout, w_s, kw_s, seg_ref, state, wsem, osem = rest[:12]
    parts, wholes, rest = rest[12:15], rest[15:18], rest[18:]
    T = blocks * L
    span = T // PARTS
    own = span // NT_
    group = span // L
    fetch = [pltpu.make_async_copy(src, dst, wsem.at[i]) for i, (src, dst) in enumerate(
        ((wq_any, wq), (wk_any, wk), (wv_any, wv), (wt_any, wt), (wba_any, wba), (wout_any, wout)))]
    leave = [pltpu.make_async_copy(src, dst, osem.at[i]) for i, (src, dst) in enumerate(zip(saved, outs))]
    for f in fetch:
        f.start()
    rate, bias = decay_rows(dlog_ref, dbias_ref)
    ring = Ring()
    scatters = [Scatter(ring, parts[g], rest[7 * g:7 * g + 7], own) for g in range(PARTS)]
    gathers = [Gather(ring, wholes[g], rest[7 * PARTS + 2 * g:7 * PARTS + 2 * g + 2], own, 384) for g in range(PARTS)]
    for pad in (qpad, kpad, vpad):
        pad[0:PAD, :] = jnp.zeros((PAD, pad.shape[1]), F32)
    segpad[0:PAD, :] = jnp.full((PAD, L), -1.0, F32)
    segpad[PAD + T:, :] = jnp.full((PAD, L), -1.0, F32)
    for b in range(blocks):
        seg_ref[b, 0:1, :] = segments_ref[0:1, b * L:(b + 1) * L].astype(F32)
        seg_ref[b, 1:2, :] = jnp.broadcast_to(segments_ref[0:1, max(b * L - 1, 0):max(b * L - 1, 0) + 1].astype(F32), (1, L))
        segpad[PAD + b * L:PAD + (b + 1) * L, :] = jnp.broadcast_to(seg_ref[b, 0:1, :], (L, L)).T
    state[...] = jnp.zeros_like(state)

    def project(g):
        def norm(i, _):
            r = pl.ds(pl.multiple_of(g * span + i * 32, 32), 32)
            v = x_ref[r, :].astype(F32)
            n = v * lax.rsqrt(jnp.mean(v * v, axis=-1, keepdims=True) + 1e-05)
            hid[r, :] = (n * again_ref[0:1, :]).astype(BF16)
            return 0

        lax.fori_loop(0, span // 32, norm, 0)
        for i, (w, dst, lead) in enumerate(((wq, qpad, PAD), (wk, kpad, PAD), (wv, vpad, PAD), (wt, gp_ref, 0), (wba, ba_ref, 0))):
            if g == 0:
                fetch[i].wait()
            dst[g * span + lead:(g + 1) * span + lead, :] = mm1(hid[g * span:(g + 1) * span, :], w[...], NT if w is wba else NN)

    def phase_a(g):
        a_mats, keepers = [], []
        for i in range(group):
            b = g * group + i
            base = b * L
            here = pl.ds(base, L)
            per_head, strict_keep, _u = block_decay(b, seg_ref, ba_ref, rate, bias)
            masks = doc_masks(segpad, base, L, False)
            for h in range(2):
                decay, carry, beta_row, beta_col, last_decay = per_head[h]
                kc = slice(h * 128, h * 128 + 128)
                vc = slice(h * 256, h * 256 + 256)
                y = conv_block(base, qpad, cq_ref, kc, masks)
                sg = sigmoid(y)
                q = y * sg
                r = lax.rsqrt(jnp.sum(q * q, axis=-1, keepdims=True) + 1e-06) * (128 ** -0.5)
                q_ref[here, kc] = q * r
                fq[here, kc] = r * (sg + q * (1.0 - sg))
                y = conv_block(base, kpad, ck_ref, kc, masks)
                sg = sigmoid(y)
                k = y * sg
                r = lax.rsqrt(jnp.sum(k * k, axis=-1, keepdims=True) + 1e-06)
                fk[here, kc] = r * (sg + k * (1.0 - sg))
                k = k * r
                k_ref[here, kc] = k
                halves = []
                for j in range(2):
                    c = slice(h * 256 + j * 128, h * 256 + j * 128 + 128)
                    y = conv_block(base, vpad, cv_ref, c, masks)
                    sg = sigmoid(y)
                    v = y * sg
                    fv[here, c] = sg + v * (1.0 - sg)
                    halves.append(v)
                ks = split(k)
                kk = jnp.where(strict_keep, decay, 0.0) * mm3(ks, ks, NT)
                kkp[here, kc] = kk
                a_mats.append(kk * beta_row)
                kw_s[here, kc] = k * (last_decay * beta_col)
                keepers.append((here, kc, vc, jnp.concatenate(halves, axis=1), k * carry))
        xs = inverse_many(a_mats)
        for x, (here, kc, vc, v, gk) in zip(xs, keepers):
            x_s[here, kc] = x
            sx = split(x)
            u_ref[here, vc] = mm3(sx, split(v))
            w_s[here, kc] = mm3(sx, split(gk))

    def phase_b(b, _):
        base = pl.multiple_of(b * L, L)
        here = pl.ds(base, L)
        per_head, strict_keep, _u = block_decay(b, seg_ref, ba_ref, rate, bias)
        for h in range(2):
            decay, carry, beta_row, beta_col, last_decay = per_head[h]
            kc = slice(h * 128, h * 128 + 128)
            vc = slice(h * 256, h * 256 + 256)
            s = state[h]
            s_ref[here, vc] = s
            u = u_ref[here, vc] - mm3(split(w_s[here, kc]), split(s))
            u_ref[here, vc] = u
            state[h] = carry[L - 1:L, :] * s + mm3(split(kw_s[here, kc]), split(u), TN)
        return 0

    def phase_c(b, _):
        base = pl.multiple_of(b * L, L)
        here = pl.ds(base, L)
        per_head, strict_keep, _u = block_decay(b, seg_ref, ba_ref, rate, bias)
        for h in range(2):
            decay, carry, beta_row, beta_col, last_decay = per_head[h]
            kc = slice(h * 128, h * 128 + 128)
            vc = slice(h * 256, h * 256 + 256)
            q = q_ref[here, kc]
            qk = decay * mm3(split(q), split(k_ref[here, kc]), NT)
            pp[here, kc] = qk
            o = mm3(split(q * carry), split(s_ref[here, vc])) + mm3(split(qk * beta_row), split(u_ref[here, vc]))
            o_ref[here, vc] = o
            gp = gp_ref[here, vc]
            n = o * lax.rsqrt(jnp.mean(o * o, axis=-1, keepdims=True) + 1e-05)
            low_ref[here, vc] = (n * gain_ref[0:1, :] * (gp * sigmoid(gp))).astype(BF16)
        return 0

    def mix(g):
        phase_a(g)
        lax.fori_loop(g * group, (g + 1) * group, phase_b, 0)
        lax.fori_loop(g * group, (g + 1) * group, phase_c, 0)
        if g == 0:
            fetch[5].wait()

        def partial(n, _):
            c = pl.ds(pl.multiple_of(n * 512, 512), 512)
            parts[g][:, c] = mm1(low_ref[g * span:(g + 1) * span, :], wout[:, c], NN)
            return 0

        lax.fori_loop(0, wout.shape[1] // 512, partial, 0)
        for k in Scatter.ORDER:
            scatters[g].start(k)

    def normed(g):
        sc, whole = scatters[g], wholes[g]
        sc.finish()

        def finish(i, _):
            r = pl.multiple_of(i * 16, 16)
            at = pl.multiple_of(ring.t * own + r, 16)
            resid = x_ref[pl.ds(pl.multiple_of(g * span + at, 16), 16), :].astype(F32) + sc.value(r)
            resid_ref[pl.ds(pl.multiple_of(g * own + r, 16), 16), :] = resid
            n = resid * lax.rsqrt(jnp.mean(resid * resid, axis=-1, keepdims=True) + 1e-05)
            whole[pl.ds(at, 16), :] = (n * fgain_ref[0:1, :]).astype(BF16).astype(F32)
            return 0

        lax.fori_loop(0, own // 16, finish, 0)
        gathers[g].start()

    def prepare(b, _):
        base = pl.multiple_of(b * L, L)
        here = pl.ds(base, L)
        per_head, strict_keep, _u = block_decay(b, seg_ref, ba_ref, rate, bias)
        lane = lax.broadcasted_iota(jnp.int32, (L, L), 1)
        row = lax.broadcasted_iota(jnp.int32, (8, L), 0)
        tile, flat = jnp.zeros((L, L), F32), jnp.zeros((8, L), F32)
        for h in range(2):
            decay, carry, beta_row, beta_col, last_decay = per_head[h]
            kc = slice(h * 128, h * 128 + 128)
            db[here, kc] = decay * beta_row
            z_s[here, kc] = mm3(split(x_s[here, kc]), split(kw_s[here, kc]), TN)
            tile = tile + (jnp.where(lane == h, carry, 0.0) + jnp.where(lane == 2 + h, last_decay * beta_col, 0.0)
                           + jnp.where(lane == 4 + h, last_decay, 0.0))
            flat = flat + jnp.where(row == h, beta_row, 0.0)
        cols_s[here, :] = tile
        brow[b] = flat
        return 0

    def cast(g):
        def one(t, _):
            r = pl.multiple_of(t * own, own)
            hidmid_ref[pl.ds(pl.multiple_of(place_of(t, g), own), own), :] = wholes[g][pl.ds(r, own), :].astype(BF16)
            return 0

        lax.fori_loop(0, NT_, one, 0)

    first, second, third = (sc.middle() for sc in scatters)
    project(0)
    greet([ring.right, ring.left, ring.flip])
    mix(0)
    project(1)
    mix(1)
    run(first, 2)
    project(2)
    for i in (0, 2, 3, 4, 5, 6, 7):
        leave[i].start()
    mix(2)
    for i in (1, 8, 9, 10, 11, 12, 13, 14, 15, 16, 17, 18):
        leave[i].start()
    run(first)
    run(second, 2)
    lax.fori_loop(0, blocks, prepare, 0)
    for i in range(19, 23):
        leave[i].start()
    normed(0)
    run(second)
    run(third, 2)
    normed(1)
    ahead = [ga.middle() for ga in gathers]
    run(ahead[0], 1)
    run(third)
    run(ahead[0])
    run(ahead[1], 1)
    normed(2)
    run(ahead[1])
    run(ahead[2])
    for g in range(PARTS):
        gathers[g].finish()
        cast(g)
    for c in scatters + gathers:
        c.s.drain()
    for c in leave:
        c.wait()


def front(x, again, wq, wk, wv, wt, wba, wout, segments, cq, ck, cv, dlog, dbias, gain, fgain):
    T, D = x.shape
    blocks = T // L
    own, span = T // NT_, T // PARTS
    sd = jax.ShapeDtypeStruct
    saved = [((T, D), BF16), ((T, 512), BF16), ((T + PAD, 256), F32), ((T + PAD, 256), F32), ((T + PAD, 512), F32), ((T + 2 * PAD, L), F32),
             ((T, 512), F32), ((T, 128), F32), ((T, 256), F32), ((T, 256), F32), ((T, 256), F32), ((T, 512), F32), ((T, 512), F32), ((T, 512), F32),
             ((T, 256), F32), ((T, 256), F32), ((T, 512), F32), ((T, 256), F32), ((T, 256), F32), ((T, 256), F32), ((T, 256), F32),
             ((T, 128), F32), ((blocks, 8, L), F32)]
    vm = lambda s, t: pltpu.VMEM(s, t)
    scratch = [vm(*s) for s in saved] + [vm(w.shape, BF16) for w in (wq, wk, wv, wt, wba, wout)]
    scratch += [vm((T, 256), F32), vm((T, 256), F32), vm((blocks, 8, L), F32), vm((2, 128, 256), F32),
                pltpu.SemaphoreType.DMA((6,)), pltpu.SemaphoreType.DMA((23,))]
    scratch += [vm((span, D), F32)] * (2 * PARTS)
    for _ in range(PARTS):
        scratch += scatter_scratch(span // NT_)
    for _ in range(PARTS):
        scratch += gather_sems()
    return pl.pallas_call(
        functools.partial(front_kernel, blocks),
        out_shape=[sd((T, D), BF16), sd((own, D), F32)] + [sd(*s) for s in saved],
        in_specs=[VM, VM] + [ANY] * 6 + [VM] * 8, out_specs=[VM, VM] + [ANY] * 23,
        scratch_shapes=scratch,
        compiler_params=params(1, 62),
        name="front",
    )(x, again, wq, wk, wv, wt, wba, wout, segments, cq, ck, cv, dlog, dbias, gain, fgain)


SMALL = 40
TAPS = 40


BACK = ("ga", "wout", "low", "ffn", "o", "gp", "pp", "x", "q", "cols", "brow", "k", "z", "u", "s", "db", "kkp", "ba",
        "qpad", "kpad", "vpad", "segpad", "fq", "fk", "fv")


def bwd_kernel(blocks, *refs):
    count = len(BACK)
    sources, rest = refs[:count], refs[count:]
    (resid_ref, cq_ref, ck_ref, cv_ref, dlog_ref, dbias_ref, gain_ref,
     dqp_ref, dkp_ref, dvp_ref, dgp_ref, dba_ref, dtap_ref, dgain_ref, oshard_ref, grads_ref) = rest[:16]
    held, rest = rest[16:16 + count], rest[16 + count:]
    fsem, gm_ref, do_s, y_s, ds_s, dq_s, dk_s, left, tap_s = rest[:9]
    rest = rest[9:]
    (ga_ref, wout_ref, low_ref, ffn_ref, o_ref, gp_ref, pp, x_ref, q_ref, cols_s, brow, k_ref, z_s, u_ref, s_ref, db, kkp, ba_ref,
     qpad, kpad, vpad, segpad, fq, fk, fv) = held
    fetch = [pltpu.make_async_copy(src, dst, fsem.at[i]) for i, (src, dst) in enumerate(zip(sources, held))]
    for c in fetch:
        c.start()

    def need(first, last):
        for c in fetch[first:last]:
            c.wait()

    T = blocks * L
    scr, dscr = rest[:7], rest[7:]
    own = resid_ref.shape[0]
    ring = Ring()

    def compute(a, b, put):
        put(slice(0, 512), mm1(left[...], jnp.concatenate([ga_ref[:, a], ga_ref[:, b]], axis=1), NN))

    dp = DpScatter(ring, dscr, compute)
    greet([ring.right, ring.left, ring.flip] + dp.devices())
    sc = Scatter(ring, ffn_ref, scr, own, sources[3])
    for k in sc.ORDER:
        sc.start(k)
    need(0, 3)
    left[...] = low_ref[...].T
    steps, cores, along = sc.middle(), dp.cores(), dp.along()
    run(cores)

    def mixed_back(i, _):
        r = pl.ds(pl.multiple_of(i * 256, 256), 256)
        gm_ref[r, :] = mm1(ga_ref[r, :], wout_ref[...], NT)
        return 0

    lax.fori_loop(0, T // 256, mixed_back, 0)
    run(along, 1)
    need(3, 4)
    run(steps, 2)
    run(along)
    need(4, 11)
    rate, bias = decay_rows(dlog_ref, dbias_ref)
    dgain_ref[...] = jnp.zeros_like(dgain_ref)
    dtap_ref[32:40, :] = jnp.zeros((8, 128), F32)
    tap_s[...] = jnp.zeros_like(tap_s)

    def phase_1(b, _):
        base = pl.multiple_of(b * L, L)
        for h in range(2):
            carry = cols_s[pl.ds(base, L), h:h + 1]
            kc = slice(h * 128, h * 128 + 128)
            vc = slice(h * 256, h * 256 + 256)
            o = o_ref[pl.ds(base, L), vc]
            gp = gp_ref[pl.ds(base, L), vc]
            gm = gm_ref[pl.ds(base, L), vc]
            gain = gain_ref[0:1, :]
            sg = sigmoid(gp)
            r = lax.rsqrt(jnp.mean(o * o, axis=-1, keepdims=True) + 1e-05)
            n = o * r
            act = gp * sg
            gn = gm * n
            dgain_ref[0:1, :] = dgain_ref[0:1, :] + jnp.sum(gn * act, axis=0, keepdims=True)
            dgp_ref[pl.ds(base, L), vc] = (gn * gain * (sg + act * (1.0 - sg))).astype(BF16)
            dn = gm * gain * act
            do = r * (dn - n * jnp.mean(dn * n, axis=-1, keepdims=True))
            do_s[pl.ds(base, L), vc] = do
            q = q_ref[pl.ds(base, L), kc]
            p = pp[pl.ds(base, L), kc] * brow[b, h:h + 1, :]
            sdo = split(do)
            sx = split(x_ref[pl.ds(base, L), kc])
            y0 = mm3(sx, split(mm3(split(p), sdo, TN)), TN)
            y_s[pl.ds(base, L), vc] = y0
            ds_s[pl.ds(base, L), vc] = mm3(split(q * carry), sdo, TN)
        return 0

    lax.fori_loop(0, blocks // 2, phase_1, 0)
    run(steps, 1)
    lax.fori_loop(blocks // 2, blocks, phase_1, 0)
    run(steps, 1)
    dp.second()
    need(11, 13)

    def phase_2(i, grads):
        b = blocks - 1 - i
        base = pl.multiple_of(b * L, L)
        new = []
        for h in range(2):
            carry = cols_s[pl.ds(base, L), h:h + 1]
            kc = slice(h * 128, h * 128 + 128)
            vc = slice(h * 256, h * 256 + 256)
            ds = grads[h]
            kept = ds_s[pl.ds(base, L), vc]
            ds_s[pl.ds(base, L), vc] = ds
            y = y_s[pl.ds(base, L), vc] + mm3(split(z_s[pl.ds(base, L), kc]), split(ds))
            y_s[pl.ds(base, L), vc] = y
            new.append(carry[L - 1:L, :] * ds + kept
                       - mm3(split(k_ref[pl.ds(base, L), kc] * carry), split(y), TN))
        return tuple(new)

    zero = jnp.zeros((128, 256), F32)
    lax.fori_loop(0, blocks, phase_2, (zero, zero))
    run(steps)
    dp.third()
    need(13, 18)

    def phase_3(b, _):
        base = pl.multiple_of(b * L, L)
        lane = lax.broadcasted_iota(jnp.int32, (L, L), 1)
        rowi = lax.broadcasted_iota(jnp.int32, (L, L), 0)
        row_tile = jnp.zeros((L, L), F32)
        col_tile = jnp.zeros((L, L), F32)
        for h in range(2):
            carry, weight, last_decay = (cols_s[pl.ds(base, L), j:j + 1] for j in (h, 2 + h, 4 + h))
            beta_row = brow[b, h:h + 1, :]
            kc = slice(h * 128, h * 128 + 128)
            vc = slice(h * 256, h * 256 + 256)
            q, k = q_ref[pl.ds(base, L), kc], k_ref[pl.ds(base, L), kc]
            sq, sk = split(q), split(k)
            decay_beta = db[pl.ds(base, L), kc]
            s, u = s_ref[pl.ds(base, L), vc], u_ref[pl.ds(base, L), vc]
            do, y, ds = do_s[pl.ds(base, L), vc], y_s[pl.ds(base, L), vc], ds_s[pl.ds(base, L), vc]
            ss, su, sdo, sy, sds = split(s), split(u), split(do), split(y), split(ds)
            do_st = mm3(sdo, ss, NT)
            y_st = mm3(sy, ss, NT)
            u_dst = mm3(su, sds, NT)
            dp = mm3(sdo, su, NT)
            da = -mm3(sy, su, NT)
            dcarry = jnp.sum(q * do_st - k * y_st, axis=-1, keepdims=True)
            dcarry_last = jnp.sum(jnp.sum(ds * s, axis=0, keepdims=True), axis=1, keepdims=True)
            dw = jnp.sum(u_dst * k, axis=-1, keepdims=True)
            dqk = dp * decay_beta
            dkk = jnp.where(rowi > lane, da * decay_beta, 0.0)
            prod = dp * pp[pl.ds(base, L), kc] + da * kkp[pl.ds(base, L), kc]
            dbeta_row = jnp.sum(prod, axis=0, keepdims=True)
            dec_grad = prod * beta_row
            dc_col = jnp.sum(dec_grad, axis=1, keepdims=True) + dcarry * carry
            dc_row = -jnp.sum(dec_grad, axis=0, keepdims=True)
            dlast = dw * weight
            row1 = rowi[:, 0:1]
            dc_col = dc_col - dlast
            dc_col = dc_col + jnp.where(row1 == L - 1, jnp.sum(dlast, axis=0, keepdims=True) + dcarry_last * carry, 0.0)
            dbeta_col = dw * last_decay
            row_tile = row_tile + jnp.where(rowi == h, dbeta_row, 0.0) + jnp.where(rowi == 2 + h, dc_row, 0.0)
            col_tile = col_tile + jnp.where(lane == h, dbeta_col, 0.0) + jnp.where(lane == 2 + h, dc_col, 0.0)
            sdqk, sdkk = split(dqk), split(dkk + dkk.T)
            dq_s[pl.ds(base, L), kc] = carry * do_st + mm3(sdqk, sk)
            dk_s[pl.ds(base, L), kc] = (mm3(sdqk, sq, TN) + mm3(sdkk, sk) - carry * y_st
                                        + weight * u_dst)
        grad = col_tile + row_tile.T
        dld = tri_sum(grad, TN)
        ba = rows(ba_ref, b)
        tile = decay_tile(ba, rate, bias)
        sig_alpha = sigmoid(ba + bias)
        dalpha = dld * rate * sig_alpha
        dpre = jnp.where(lane < 2, grad * tile * (1.0 - tile), jnp.where(lane < 4, dalpha, 0.0))
        dba_ref[pl.ds(base, L), :] = dpre.astype(BF16)
        dtap_ref[32:33, :] = dtap_ref[32:33, :] + jnp.sum(dpre, axis=0, keepdims=True)
        dtap_ref[33:34, :] = dtap_ref[33:34, :] + jnp.sum(dld * tile, axis=0, keepdims=True)
        return 0

    lax.fori_loop(0, blocks, phase_3, 0)

    need(18, count)

    R = 64
    groups = []
    for h in range(2):
        c = slice(h * 128, h * 128 + 128)
        groups.append((qpad, cq_ref, dq_s, dqp_ref, fq, c, h * 128, q_ref, 128.0))
        groups.append((kpad, ck_ref, dk_s, dkp_ref, fk, c, 256 + h * 128, k_ref, 1.0))
    for j in range(4):
        groups.append((vpad, cv_ref, y_s, dvp_ref, fv, slice(j * 128, j * 128 + 128), 512 + j * 128, None, None))
    for src in (dq_s, dk_s, y_s):
        src[T:, :] = jnp.zeros((PAD, src.shape[1]), F32)

    def conv_back(i, _):
        base = pl.multiple_of((T // R - 1 - i) * R, R)
        here = pl.ds(base, R)
        behind, ahead = doc_masks(segpad, base, R, False), doc_masks(segpad, base, R, True)
        for pre, taps, src, out_ref, factor, c, tc, unit, size in groups:
            d = src[here, c]
            if unit is not None:
                v = unit[here, c]
                d = d - v * (size * jnp.sum(d * v, axis=-1, keepdims=True))
            dy = factor[here, c] * d
            src[here, c] = dy
            z = pre[pl.ds(base, R + PAD), c]
            both = src[pl.ds(base, R + PAD), c]
            tc = slice(tc, tc + 128)
            total = dy * taps[0:1, c]
            tap_s[0, :, tc] = tap_s[0, :, tc] + jnp.sum((dy * z[PAD:]).reshape(R // 8, 8, 128), axis=0)
            for t in range(1, 4):
                total = total + both[t:t + R] * (ahead[t - 1] * taps[t:t + 1, c])
                tap_s[t, :, tc] = tap_s[t, :, tc] + jnp.sum((dy * (z[PAD - t:PAD - t + R] * behind[t - 1])).reshape(R // 8, 8, 128), axis=0)
            out_ref[here, c] = total.astype(BF16)
        return 0

    lax.fori_loop(0, T // R, conv_back, 0)
    for t in range(4):
        for j in range(8):
            dtap_ref[t * 8 + j:t * 8 + j + 1, :] = jnp.sum(tap_s[t, :, j * 128:(j + 1) * 128], axis=0, keepdims=True)
    sc.finish()

    def finish(i, _):
        r = pl.ds(pl.multiple_of(i * 16, 16), 16)
        oshard_ref[r, :] = (resid_ref[r, :] + sc.value(pl.multiple_of(i * 16, 16))).astype(BF16).astype(F32)
        return 0

    lax.fori_loop(0, own // 16, finish, 0)
    dp.finish(grads_ref)
    sc.s.drain()


def mixer_bwd(resid, cq, ck, cv, dlog, dbias, gain, **held):
    T, D = held["ga"].shape
    blocks = T // L
    own = resid.shape[0]
    n = held["low"].shape[1]
    sd = jax.ShapeDtypeStruct
    vm = lambda *r: pltpu.VMEM(r, F32)
    return pl.pallas_call(
        functools.partial(bwd_kernel, blocks),
        out_shape=(sd((T, 256), BF16), sd((T, 256), BF16), sd((T, 512), BF16), sd((T, 512), BF16), sd((T, 128), BF16),
                   sd((TAPS, 128), F32), sd((8, 256), F32), sd((own, D), F32), sd((n, 128), F32)),
        in_specs=[ANY] * len(BACK) + [VM] * 7, out_specs=[VM] * 9,
        scratch_shapes=[pltpu.VMEM(held[name].shape, held[name].dtype) for name in BACK]
        + [pltpu.SemaphoreType.DMA((len(BACK),)), vm(T, 512), vm(T, 512), vm(T + PAD, 512), vm(T, 512), vm(T + PAD, 256), vm(T + PAD, 256),
           pltpu.VMEM((n, T), BF16), vm(4, 8, 1024)] + scatter_scratch(own) + dp_scratch(n, 4),
        compiler_params=params(4, 62),
        name="mixer_backward",
    )(*[held[name] for name in BACK], resid, cq, ck, cv, dlog, dbias, gain)


def in_places(source, dest, sems):
    return [pltpu.make_async_copy(source.at[pl.ds(natural_of(t, g), 32)], dest.at[pl.ds(place_of(t, g), 32)], sems.at[t * PARTS + g])
            for t in range(NT_) for g in range(PARTS)]


def mid_kernel(wg_ref, wu_ref, wd_any, hid_ref, og_any, resid_any, gain_ref,
               ga_ref, inner_ref, ffn_any, gres_ref, dgain_ref, grads_ref,
               part, whole, left, gg_ref, gu_ref, wd_ref, og_ref, resid_in, csem, gsem_og, *rest):
    scr, gsem, dscr = rest[:7], rest[7:9], rest[9:]
    fetches = [pltpu.make_async_copy(wd_any, wd_ref, csem.at[0]), pltpu.make_async_copy(resid_any, resid_in, csem.at[1])]
    reorder = in_places(og_any, og_ref, gsem_og)
    for f in fetches + reorder:
        f.start()
    ring = Ring()
    own = gres_ref.shape[0]
    n = gg_ref.shape[1]
    mine = ring.rows(0, False, own)

    def compute(a, b, put):
        hid = jnp.concatenate([hid_ref[:, a], hid_ref[:, b]], axis=1)
        put(slice(0, n), mm1(left[0:n, :], hid, NN))
        put(slice(n, 2 * n), mm1(left[n:2 * n, :], hid, NN))

    dp = DpScatter(ring, dscr, compute)
    greet([ring.right, ring.left, ring.flip] + dp.devices())
    sc = Scatter(ring, part, scr, own)
    for k in sc.ORDER:
        quarter = ring.quarter(k, own)
        hid = hid_ref[quarter, :]
        gate = mm1(hid, wg_ref[...], NT)
        up = mm1(hid, wu_ref[...], NT)
        sig = sigmoid(gate)
        act = gate * sig
        inner_ref[quarter, :] = (act * up).astype(BF16)
        if k == 2:
            for f in fetches[:1] + reorder:
                f.wait()
        back = mm1(og_ref[quarter, :], wd_ref[...], NT)
        gg_ref[quarter, :] = (back * up * sig * (1.0 + gate * (1.0 - sig))).astype(BF16)
        gu_ref[quarter, :] = (back * act).astype(BF16)

        def partial(i, _):
            cols = pl.ds(pl.multiple_of(i * 512, 512), 512)
            part[quarter, cols] = mm1(gg_ref[quarter, :], wg_ref[:, cols], NN) + mm1(gu_ref[quarter, :], wu_ref[:, cols], NN)
            return 0

        lax.fori_loop(0, part.shape[1] // 512, partial, 0)
        sc.start(k)
    left[0:n, :] = gg_ref[...].T
    left[n:2 * n, :] = gu_ref[...].T
    together(sc, dp)
    fetches[1].wait()
    sc.finish()
    dgain_ref[...] = jnp.zeros_like(dgain_ref)

    def finish(i, _):
        r = pl.multiple_of(i * 16, 16)
        resid = resid_in[pl.ds(r, 16), :]
        back = sc.value(r)
        scale = lax.rsqrt(jnp.mean(resid * resid, axis=-1, keepdims=True) + 1e-05)
        nn = resid * scale
        bn = back * nn
        dgain_ref[...] = dgain_ref[...] + bn[0:8] + bn[8:16]
        b = back * gain_ref[0:1, :]
        g = og_ref[pl.ds(pl.multiple_of(mine.start + r, 16), 16), :].astype(F32) + scale * (b - nn * jnp.mean(b * nn, axis=-1, keepdims=True))
        gres_ref[pl.ds(r, 16), :] = g
        whole[pl.ds(pl.multiple_of(mine.start + r, 16), 16), :] = g.astype(BF16).astype(F32)
        return 0

    lax.fori_loop(0, own // 16, finish, 0)
    ga = Gather(ring, whole, gsem, own)
    ga.start()
    sc.s.drain()
    steps = ga.middle()
    run(steps, 1)
    dp.second()
    run(steps, 1)

    def down(i, _):
        cols = pl.ds(pl.multiple_of(i * 256, 256), 256)
        part[:, cols] = mm1(inner_ref[...], wd_ref[:, cols], NN)
        return 0

    lax.fori_loop(0, part.shape[1] // 256, down, 0)
    leave = pltpu.make_async_copy(part, ffn_any, csem.at[3])
    leave.start()
    run(steps)
    dp.third()
    ga.finish()

    def cast(i, _):
        t, g = i // PARTS, lax.rem(i, PARTS)
        ga_ref[pl.ds(pl.multiple_of(natural_of(t, g), 32), 32), :] = whole[pl.ds(pl.multiple_of(place_of(t, g), 32), 32), :].astype(BF16)
        return 0

    lax.fori_loop(0, NT_ * PARTS, cast, 0)
    dp.finish(grads_ref)
    leave.wait()
    ga.s.drain()


def mid_exchange(wg, wu, wd, hid, og, resid, gain):
    T, D = og.shape
    own = T // NT_
    m = wg.shape[0]
    sd = jax.ShapeDtypeStruct
    return pl.pallas_call(
        mid_kernel,
        out_shape=(sd((T, D), BF16), sd((T, m), BF16), sd((T, D), F32), sd((own, D), F32), sd((8, D), F32), sd((2 * m, 128), F32)),
        in_specs=[VM, VM, ANY, VM, ANY, ANY, VM], out_specs=[VM, VM, ANY, VM, VM, VM],
        scratch_shapes=[pltpu.VMEM((T, D), F32), pltpu.VMEM((T, D), F32), pltpu.VMEM((2 * m, T), BF16),
                        pltpu.VMEM((T, m), BF16), pltpu.VMEM((T, m), BF16), pltpu.VMEM((m, D), BF16), pltpu.VMEM((T, D), BF16),
                        pltpu.VMEM((own, D), F32), pltpu.SemaphoreType.DMA((4,)), pltpu.SemaphoreType.DMA((NT_ * PARTS,))]
        + scatter_scratch(own) + gather_sems() + dp_scratch(2 * m, 4),
        compiler_params=params(2, 62),
        name="mid_exchange",
    )(wg, wu, wd, hid, og, resid, gain)


def in_kernel(*refs):
    sources, (gres_ref, x_ref, gain_ref, fpart_ref, hgain_ref, taps_ref, oshard_ref), rest = refs[:13], refs[13:20], refs[20:]
    whole, out_whole, grads_ref, gains_out, taps_out = rest[:5]
    held, rest = rest[5:18], rest[18:]
    gq, gk, gv, gt, gba, wq, wk, wv, wt, wba, inner_ref, hid_ref, og_ref = held
    part, shard, left, xown, g_own, g_recv, s_own, s_recv, fsem, csem, ssem, srsem, gsem_og = rest[:13]
    rest = rest[13:]
    scr, gsem, osem, dscr = rest[:7], rest[7:9], rest[9:11], rest[11:]
    loads = [pltpu.make_async_copy(src, dst, fsem.at[i]) for i, (src, dst) in enumerate(zip(sources[:12], held))]
    loads += in_places(sources[12], og_ref, gsem_og)
    ring = Ring()
    own = gres_ref.shape[0]
    mine = ring.rows(0, False, own)
    fetch = [pltpu.make_async_copy(x_ref.at[pl.ds(pl.multiple_of(natural_of(ring.t, g), 32), 32)], xown.at[pl.ds(g * 32, 32)], csem.at[3 + g])
             for g in range(PARTS)]
    for c in fetch:
        c.start()
    place_out = pltpu.make_async_copy(oshard_ref, out_whole.at[mine], csem.at[1])
    place_out.start()
    for c in loads:
        c.start()
    t_peers = [(ring.d, lax.rem(ring.t + j, NT_)) for j in range(1, NT_)]
    d_peers = [(lax.rem(ring.d + j, 16), ring.t) for j in range(1, 16)]
    greet(t_peers + d_peers)
    place_out.wait()
    go = Gather(ring, out_whole, osem, own)
    go.start()
    for c in loads[:10]:
        c.wait()
    sc = Scatter(ring, part, scr, own)
    for k in sc.ORDER:
        quarter = ring.quarter(k, own)

        def chosen(ref):
            return jnp.concatenate([ref[pl.ds(pl.multiple_of(natural_of(ring.at(k) * 2 + y, g), 32), 32), :] for y in range(2) for g in range(PARTS)],
                                   axis=0)

        def partial(i, _):
            rows_w = pl.ds(pl.multiple_of(i * 512, 512), 512)
            total = mm1(chosen(gq), wq[rows_w, :], NT) + mm1(chosen(gk), wk[rows_w, :], NT)
            total = total + mm1(chosen(gv), wv[rows_w, :], NT) + mm1(chosen(gt), wt[rows_w, :], NT)
            part[quarter, rows_w] = total + mm1(chosen(gba), wba[:, rows_w], NN)
            return 0

        lax.fori_loop(0, part.shape[1] // 512, partial, 0)
        sc.start(k)

    def compute(a, b, put):
        hid = jnp.concatenate([hid_ref[:, a], hid_ref[:, b]], axis=1)
        put(slice(0, 768), mm1(left[0:768, :], hid, NN))
        put(slice(768, 1552), mm1(left[768:1552, :], hid, NN))
        put(slice(1552, 2256), mm1(left[1552:, :], jnp.concatenate([og_ref[:, a], og_ref[:, b]], axis=1), NN))

    dp = DpScatter(ring, dscr, compute)
    left[0:256, :] = gq[...].T
    left[256:512, :] = gk[...].T
    left[512:1024, :] = gv[...].T
    left[1024:1536, :] = gt[...].T
    left[1536:1552, :] = gba[...].T[0:16]
    for c in loads[10:]:
        c.wait()
    left[1552:, :] = inner_ref[...].T
    outs = go.middle()
    run(outs, 1)
    together(sc, dp)
    run(outs, 2)
    for c in fetch:
        c.wait()
    sc.finish()
    g_own[...] = jnp.zeros_like(g_own)
    ffn_gain = jnp.sum(fpart_ref[...], axis=0, keepdims=True)
    for j in range(16):
        g_own[16 + j:17 + j, :] = ffn_gain[:, j * 128:(j + 1) * 128]
    for j in range(2):
        g_own[32 + j:33 + j, :] = hgain_ref[0:1, j * 128:(j + 1) * 128]

    def finish(i, total):
        r = pl.multiple_of(i * 16, 16)
        x = xown[pl.ds(r, 16), :].astype(F32)
        back = sc.value(r)
        scale = lax.rsqrt(jnp.mean(x * x, axis=-1, keepdims=True) + 1e-05)
        nn = x * scale
        total = total + jnp.sum(back * nn, axis=0, keepdims=True)
        b = back * gain_ref[0:1, :]
        g = gres_ref[pl.ds(r, 16), :] + scale * (b - nn * jnp.mean(b * nn, axis=-1, keepdims=True))
        shard[pl.ds(r, 16), :] = g.astype(BF16).astype(F32)
        return total

    total = lax.fori_loop(0, own // 16, finish, jnp.zeros((1, x_ref.shape[1]), F32))
    for j in range(16):
        g_own[j:j + 1, :] = total[:, j * 128:(j + 1) * 128]
    place = pltpu.make_async_copy(shard, whole.at[mine], csem.at[2])
    place.start()
    place.wait()
    small = Sends(ssem, srsem)
    for j, dev in enumerate(t_peers):
        small.go(j, g_own, g_recv.at[j], dev)
    ga = Gather(ring, whole, gsem, own)
    ga.start()
    run(outs)
    dp.second()
    steps = ga.middle()
    run(steps, 1)
    for j, dev in enumerate(t_peers):
        small.got(j, g_recv.at[j], dev)
    gains = g_own[...]
    for j in range(NT_ - 1):
        gains = gains + g_recv[j]
    s_own[0:SMALL, :] = gains
    s_own[SMALL:, :] = taps_ref[...]
    for j, dev in enumerate(d_peers):
        small.go(7 + j, s_own, s_recv.at[j], dev)
    run(steps)
    dp.third()
    for j, dev in enumerate(d_peers):
        small.got(7 + j, s_recv.at[j], dev)
    both = s_own[...]
    for j in range(15):
        both = both + s_recv[j]
    gains_out[...] = both[:SMALL]
    taps_out[...] = both[SMALL:]
    go.finish()
    ga.finish()
    dp.finish(grads_ref)
    small.drain()
    go.s.drain()
    sc.s.drain()
    ga.s.drain()


def in_exchange(grads, weights, inner, hid, og, gres, inputs, gain, ffn_part, hgain, taps, oshard):
    T, D = inputs.shape
    own = T // NT_
    n = 1552 + inner.shape[1]
    sd = jax.ShapeDtypeStruct
    vm = lambda *s: pltpu.VMEM(s, F32)
    held = (*grads, *weights, inner, hid, og)
    return pl.pallas_call(
        in_kernel,
        out_shape=(sd((T, D), F32), sd((T, D), F32), sd((n, 128), F32), sd((SMALL, 128), F32), sd((TAPS, 128), F32)),
        in_specs=[ANY] * 13 + [VM, ANY] + [VM] * 5, out_specs=[ANY, ANY, VM, VM, VM],
        scratch_shapes=[pltpu.VMEM(h.shape, h.dtype) for h in held]
        + [vm(T, D), vm(own, D), pltpu.VMEM((n, T), BF16), pltpu.VMEM((own, D), BF16),
           vm(SMALL, 128), vm(7, SMALL, 128), vm(SMALL + TAPS, 128), vm(15, SMALL + TAPS, 128),
           pltpu.SemaphoreType.DMA((12,)), pltpu.SemaphoreType.DMA((3 + PARTS,)), pltpu.SemaphoreType.DMA((22,)), pltpu.SemaphoreType.DMA((22,)),
           pltpu.SemaphoreType.DMA((NT_ * PARTS,))]
        + scatter_scratch(own) + gather_sems() + gather_sems() + dp_scratch(n, 4),
        compiler_params=params(3, 62),
        name="in_exchange",
    )(*held, gres, inputs, gain, ffn_part, hgain, taps, oshard)


def last_kernel(ig_ref, out_ref, gin_ref, gmid_ref, gout_ref, gains_ref, taps_ref,
                ig_low, out_low, gq, gk, gv, gt, gbeta, galpha, cq, ck, cv, dlog, dbias, hgain, again, fgain, gug, gup, gdown, gout):
    for t in range(NT_):
        ig_low[t * 32:(t + 1) * 32, :] = ig_ref[t, 0].astype(BF16)
        out_low[t * 32:(t + 1) * 32, :] = out_ref[t, 0].astype(BF16)

    @pl.when(pl.program_id(0) == 0)
    def _():
        gq[...] = gin_ref[0:256, :].T
        gk[...] = gin_ref[256:512, :].T
        gv[...] = gin_ref[512:1024, :].T
        gt[...] = gin_ref[1024:1536, :].T
        gbeta[...] = gin_ref[1536:1538, :]
        galpha[...] = gin_ref[1538:1540, :]
        gdown[...] = gin_ref[1552:, :]
        n = gug.shape[0]
        gug[...] = gmid_ref[0:n, :]
        gup[...] = gmid_ref[n:, :]
        gout[...] = gout_ref[...]
        for t in range(4):
            for j in range(8):
                row = taps_ref[t * 8 + j:t * 8 + j + 1, :]
                ref, at = ((cq, j), (ck, j - 2), (cv, j - 4))[0 if j < 2 else 1 if j < 4 else 2]
                ref[t:t + 1, at * 128:(at + 1) * 128] = row
        dbias[...] = taps_ref[32:33, 2:4]
        dlog[...] = taps_ref[33:34, 2:4]
        again[...] = gains_ref[0:16, :]
        fgain[...] = gains_ref[16:32, :]
        hgain[...] = gains_ref[32:34, :]


def last(ig, out, gin, gmid, gout, gains, taps):
    T, D = ig.shape
    n = gmid.shape[0] // 2
    sd = lambda *s: jax.ShapeDtypeStruct(s, F32)
    step = lambda: pl.BlockSpec((T // PARTS, D), lambda i: (i, 0))
    shares = lambda: pl.BlockSpec((NT_, 1, 32, D), lambda i: (0, i, 0, 0))
    fixed = lambda s: pl.BlockSpec(s, lambda i: (0, 0))
    small = [sd(128, 256), sd(128, 256), sd(128, 512), sd(128, 512), sd(2, 128), sd(2, 128), sd(4, 256), sd(4, 256), sd(4, 512),
             sd(1, 2), sd(1, 2), sd(2, 128), sd(16, 128), sd(16, 128), sd(n, 128), sd(n, 128), sd(gin.shape[0] - 1552, 128), sd(gout.shape[0], 128)]
    return pl.pallas_call(
        last_kernel,
        grid=(PARTS,),
        out_shape=[jax.ShapeDtypeStruct((T, D), BF16)] * 2 + small,
        in_specs=[shares(), shares()] + [fixed(a.shape) for a in (gin, gmid, gout, gains, taps)],
        out_specs=[step(), step()] + [fixed(a.shape) for a in small],
        compiler_params=pltpu.CompilerParams(vmem_limit_bytes=62 * 2 ** 20),
        name="last",
    )(*(a.reshape(NT_, PARTS, 32, D) for a in (ig, out)), gin, gmid, gout, gains, taps)


def row(v):
    return v.reshape(1, v.shape[0])


def per_device(inputs, segments, attn_gain, w_query, w_key, w_value, w_gate, w_beta, w_alpha, conv_query, conv_key, conv_value,
               decay_log, decay_bias, head_gain, w_out, ffn_gain, w_up_gate, w_up, w_down, out_grad):
    D = inputs.shape[1]
    w_ba = jnp.concatenate([w_beta.T, w_alpha.T, jnp.zeros((124, D), BF16)], axis=0)
    dlog, dbias, hgain = row(decay_log), row(decay_bias), row(head_gain)
    hidden_mid, resid, hidden_in, low, *saved = front(
        inputs, row(attn_gain), w_query, w_key, w_value, w_gate, w_ba, w_out, segments, conv_query, conv_key, conv_value,
        dlog, dbias, hgain, row(ffn_gain))
    names = ("qpad", "kpad", "vpad", "segpad", "gp", "ba", "q", "k", "x", "u", "s", "o", "fq", "fk", "fv", "pp", "kkp", "db", "z", "cols", "brow")
    grad_attn, inner, ffn, grad_resid, ffn_gain_part, grads_mid = mid_exchange(
        w_up_gate.T, w_up.T, w_down, hidden_mid, out_grad, resid, row(ffn_gain))
    *grads, taps, hgain_part, oshard, grads_out = mixer_bwd(
        resid, conv_query, conv_key, conv_value, dlog, dbias, hgain, ga=grad_attn, wout=w_out, low=low, ffn=ffn, **dict(zip(names, saved)))
    ig, out, grads_in, gains, taps = in_exchange(
        grads, (w_query, w_key, w_value, w_gate, w_ba), inner, hidden_in, out_grad, grad_resid, inputs,
        row(attn_gain), ffn_gain_part, hgain_part, taps, oshard)
    (input_grad, outputs, gq, gk, gv, gt, gbeta, galpha, cq, ck, cv, g_dlog, g_dbias, g_hgain, g_again, g_fgain,
     gug, gup, gdown, gout) = last(ig, out, grads_in, grads_mid, grads_out, gains, taps)
    return (outputs, input_grad, g_again.reshape(D), gq, gk, gv, gt, gbeta.T, galpha.T, cq, ck, cv,
            g_dlog.reshape(2), g_dbias.reshape(2), g_hgain.reshape(head_gain.shape), gout, g_fgain.reshape(D), gug.T, gup.T, gdown)


def solution(mesh):
    col, rows_t, rep = P(None, "tensor"), P("tensor", None), P()
    tok, both, head = P("dp", None), P("dp", "tensor"), P("tensor")
    return jax.shard_map(
        per_device,
        mesh=mesh,
        in_specs=(tok, tok, rep, col, col, col, col, col, col, col, col, col, head, head, rep, rows_t, rep, col, col, rows_t, tok),
        out_specs=(tok, tok, rep, both, both, both, both, both, both, col, col, col, head, head, rep, P("tensor", "dp"), rep, both, both, P("tensor", "dp")),
        check_vma=False,
    )
```
